512 devices in a mesh: narrow: 16 (over y, x), wide: 32 (over z, core).
Axes of the slice: x: 4, y: 4, z: 16, core: 2. Of those that a mesh axis runs over, the one named last changes fastest.
Arguments:
- adjoint_rhs: float32 [32, 256, 760], P('wide', 'narrow'), may hold values from -1.8 to 1.8
- pivot_inverse: bfloat16 [32, 256, 9025], P('wide', 'narrow'), may hold values from -0.05 to 1.05
- upper_blocks: bfloat16 [32, 256, 9025], P('wide', 'narrow'), may hold values from -0.05 to 2.05
- lower_blocks: bfloat16 [32, 256, 9025], P('wide', 'narrow'), may hold values from -0.05 to 2.05
- face_neighbors: int32 [32, 2], P('wide'), may hold values from 0 to 31, as said below
- face_coupling: float32 [32, 256, 190], P('wide', 'narrow'), may hold values from 0.15 to 0.6
Outputs:
- first_apply: float32 [32, 256, 760], P('wide', 'narrow')
- second_apply: float32 [32, 256, 760], P('wide', 'narrow')
The draws below stay inside these ranges and needn't reach their ends.
Inputs may be any that keep to these rules, and one draw needn't show every extreme that they name: `face_neighbors`: with the lines in blocks of 1 (block b holds lines b * 1 to (b + 1) - 1), both neighbors of a line of block b lie in blocks b - 1, b or b + 1, taken cyclically over the 32 lines.
All inputs are finite; a program needn't handle non-finite values.
Results may differ from the reference program's by a relative error of at most 0.0003.
Values sent between devices are 32-bit elements; how exact they have to be, the bound alone decides.
A program may use at most 64 MiB of HBM per device.

```python
import jax
import jax.numpy as jnp
from jax import lax

NV = 95
NR = 8
LINES_DEV = 1
LINE_TOTAL = 32
CELLS_PER_LINE = 256


def pivot_scale(key):
    return jnp.exp(jax.random.uniform(key, (LINE_TOTAL, CELLS_PER_LINE, NV), jnp.float32, jnp.log(0.5), 0.0))


def carried_rates(key, shortest, longest):
    first_key, second_key, key_third = jax.random.split(key, 3)
    line_lengths = jnp.exp(jax.random.uniform(first_key, (LINE_TOTAL, 1, NV), jnp.float32, jnp.log(shortest), jnp.log(longest)))
    match_count = jax.random.uniform(second_key, (LINE_TOTAL, CELLS_PER_LINE, 1), jnp.float32)
    pulse_groups = jnp.where(match_count < 3.0 / CELLS_PER_LINE, jax.random.uniform(key_third, (LINE_TOTAL, CELLS_PER_LINE, 1), jnp.float32, 0.5, 0.8), 1.0)
    return jnp.exp(-1.0 / line_lengths) * pulse_groups


def draw_pivot_inverse(key, part):
    scale_diag = pivot_scale(key)
    key = jax.random.fold_in(key, 3)
    perturb = jnp.clip(0.01 * jax.random.normal(key, (LINE_TOTAL, CELLS_PER_LINE, NV, NV), jnp.float32), -0.04, 0.04)
    matrix = perturb + scale_diag[..., None] * jnp.eye(NV, dtype=jnp.float32)
    return matrix.reshape(LINE_TOTAL, CELLS_PER_LINE, NV * NV).astype(jnp.bfloat16)


def draw_upper_blocks(key, part):
    scale_diag = pivot_scale(key)
    key = jax.random.fold_in(key, 5)
    rate_key, perturb_key = jax.random.split(key)
    decays = carried_rates(rate_key, 0.4 * CELLS_PER_LINE, 4.0 * CELLS_PER_LINE)
    perturb = jnp.clip(0.01 * jax.random.normal(perturb_key, (LINE_TOTAL, CELLS_PER_LINE, NV, NV), jnp.float32), -0.04, 0.04)
    diagonal = decays / jnp.roll(scale_diag, -1, axis=1)
    matrix = perturb + diagonal[..., None] * jnp.eye(NV, dtype=jnp.float32)
    return matrix.reshape(LINE_TOTAL, CELLS_PER_LINE, NV * NV).astype(jnp.bfloat16)


def draw_lower_blocks(key, part):
    scale_diag = pivot_scale(key)
    key = jax.random.fold_in(key, 7)
    rate_key, perturb_key = jax.random.split(key)
    decays = carried_rates(rate_key, 0.4 * CELLS_PER_LINE, 4.0 * CELLS_PER_LINE)
    perturb = jnp.clip(0.01 * jax.random.normal(perturb_key, (LINE_TOTAL, CELLS_PER_LINE, NV, NV), jnp.float32), -0.04, 0.04)
    diagonal = decays / jnp.roll(scale_diag, 1, axis=1)
    matrix = perturb + diagonal[..., None] * jnp.eye(NV, dtype=jnp.float32)
    return matrix.reshape(LINE_TOTAL, CELLS_PER_LINE, NV * NV).astype(jnp.bfloat16)


def draw_face_neighbors(key, part):
    key = jax.random.fold_in(key, 9)
    first_key, second_key = jax.random.split(key)
    line_index = jnp.arange(LINE_TOTAL, dtype=jnp.int32)
    groups = LINE_TOTAL // LINES_DEV
    owner_block = line_index // LINES_DEV
    lower_pick = jax.random.randint(first_key, (LINE_TOTAL,), 0, 3 * LINES_DEV, dtype=jnp.int32)
    upper_pick = jax.random.randint(second_key, (LINE_TOTAL,), 0, 3 * LINES_DEV, dtype=jnp.int32)
    lower_pick = lower_pick.at[0].set(LINES_DEV - 1)
    lower_pick = lower_pick.at[LINES_DEV].set(0)
    lower_side = (owner_block - 1 + lower_pick // LINES_DEV) % groups * LINES_DEV + lower_pick % LINES_DEV
    upper_side = (owner_block - 1 + upper_pick // LINES_DEV) % groups * LINES_DEV + upper_pick % LINES_DEV
    return jnp.stack([lower_side, upper_side], axis=1).astype(jnp.int32)


def steps_of(key, dims, cuts, low, largest):
    factor_of, own = 1.0, jax.random.fold_in(key, 6)
    for position, shards_of in cuts:
        steps = jnp.exp(jax.random.uniform(jax.random.fold_in(own, position), (shards_of,), jnp.float32, low / len(cuts), largest / len(cuts)))
        factor_of = factor_of * jnp.repeat(steps, dims[position] // shards_of).reshape([-1 if axis == position else 1 for axis in range(len(dims))])
    return factor_of


def scatter_about(own_key, extent, scale, limit, cuts=(), held_as=jnp.bfloat16):
    array = jax.random.normal(own_key, extent, jnp.float32) * scale
    if len(cuts) > 0:
        array = steps_of(own_key, extent, cuts, -0.22, 0.18) * array
    return jnp.clip(array, min=-limit, max=limit).astype(held_as)


def setup_inputs(seed: int = 0) -> dict:
    arg_keys = jax.random.split(jax.random.key(seed), 7)
    return {
        "adjoint_rhs": scatter_about(arg_keys[0], (LINE_TOTAL, CELLS_PER_LINE, NV * NR), 0.3, 1.8, ((0, 32), (1, 16)), jnp.float32),
        "pivot_inverse": draw_pivot_inverse(jax.random.fold_in(arg_keys[6], 71), 0),
        "upper_blocks": draw_upper_blocks(jax.random.fold_in(arg_keys[6], 71), 0),
        "lower_blocks": draw_lower_blocks(jax.random.fold_in(arg_keys[6], 71), 0),
        "face_neighbors": draw_face_neighbors(jax.random.fold_in(arg_keys[6], 71), 0),
        "face_coupling": jnp.clip(0.15 + 0.45000002 * jax.random.uniform(arg_keys[5], (LINE_TOTAL, CELLS_PER_LINE, 2 * NV), jnp.float32) ** steps_of(arg_keys[5], (LINE_TOTAL, CELLS_PER_LINE, 2 * NV), ((0, 32), (1, 16)), -0.2, 0.2), 0.15, 0.6),
    }


exact_precision = lax.Precision.HIGHEST


def adjoint_multiply(matrix_block, vector):
    return jnp.einsum("...ba,...bk->...ak", matrix_block.astype(jnp.float32), vector, precision=exact_precision)


def cell_slice(stacked, i, columns):
    return lax.dynamic_index_in_dim(stacked, i, 1, keepdims=False).astype(jnp.float32).reshape(LINE_TOTAL, NV, columns)


def apply_preconditioner(forcing_vector, pivot_inverse, upper_blocks, lower_blocks):
    empty = jnp.zeros((LINE_TOTAL, NV, NR), jnp.float32)

    def forward_step(i, carried_state):
        running, outputs = carried_state
        pivot_block = cell_slice(pivot_inverse, i, NV)
        source = cell_slice(forcing_vector, i, NR)
        numeric_elements = adjoint_multiply(pivot_block, source) - adjoint_multiply(pivot_block, running)
        outputs = lax.dynamic_update_index_in_dim(outputs, numeric_elements.reshape(LINE_TOTAL, NV * NR), i, 1)
        return adjoint_multiply(cell_slice(upper_blocks, i, NV), numeric_elements), outputs

    unused_slot, forward = lax.fori_loop(0, CELLS_PER_LINE, forward_step, (empty, jnp.zeros_like(forcing_vector)))

    def backward_step(j, carried_state):
        i = CELLS_PER_LINE - 1 - j
        running, outputs = carried_state
        pivot_block = cell_slice(pivot_inverse, i, NV)
        numeric_elements = cell_slice(forward, i, NR) - adjoint_multiply(pivot_block, running)
        outputs = lax.dynamic_update_index_in_dim(outputs, numeric_elements.reshape(LINE_TOTAL, NV * NR), i, 1)
        return adjoint_multiply(cell_slice(lower_blocks, i, NV), numeric_elements), outputs

    unused_slot, result = lax.fori_loop(0, CELLS_PER_LINE, backward_step, (empty, jnp.zeros_like(forcing_vector)))
    return result


def reference(adjoint_rhs, pivot_inverse, upper_blocks, lower_blocks, face_neighbors, face_coupling):
    first_apply = apply_preconditioner(adjoint_rhs, pivot_inverse, upper_blocks, lower_blocks)
    cell_values = first_apply.reshape(LINE_TOTAL, CELLS_PER_LINE, NV, NR)
    coefficients = face_coupling.reshape(LINE_TOTAL, CELLS_PER_LINE, 2, NV)
    lower_side = jnp.take(cell_values, face_neighbors[:, 0], axis=0)
    upper_side = jnp.take(cell_values, face_neighbors[:, 1], axis=0)
    coupled_source = adjoint_rhs.reshape(LINE_TOTAL, CELLS_PER_LINE, NV, NR) - coefficients[:, :, 0, :, None] * lower_side - coefficients[:, :, 1, :, None] * upper_side
    second_apply = apply_preconditioner(coupled_source.reshape(LINE_TOTAL, CELLS_PER_LINE, NV * NR), pivot_inverse, upper_blocks, lower_blocks)
    return first_apply, second_apply
```

```python
import functools

import jax
import jax.numpy as jnp
from jax import lax
from jax.experimental import pallas as pl
from jax.experimental.pallas import tpu as pltpu
from jax.sharding import PartitionSpec as P

NV = 95
NR = 8
ROWS = 96
PACKED = 72
LANES = 128
F32 = jnp.float32
BF16 = jnp.bfloat16
MESH = pl.DeviceIdType.MESH


def dot(left, right):
    return jnp.dot(left, right, preferred_element_type=F32)


def parts(value):
    high = value.astype(BF16)
    return high, (value - high.astype(F32)).astype(BF16)


def stacked_vector(value):
    high = value.astype(BF16).astype(F32)
    return jnp.concatenate([high, value - high], axis=0).astype(BF16)


def folded(product):
    rows = product.shape[0] // 2
    return product[:rows, :LANES] + (product[:rows, LANES:] + product[rows:, :LANES])


def put(ref, index, value):
    high, low = parts(value)
    ref[index, pl.ds(0, ROWS), pl.ds(0, LANES)] = high
    ref[index, pl.ds(0, ROWS), pl.ds(LANES, LANES)] = low


def left_of(place):
    ref, index = place
    return ref[index, pl.ds(0, ROWS), :]


def right_of(place):
    ref, index = place
    value = ref[index]
    return jnp.concatenate([value, value], axis=0)


def multiply(left, right):
    product = dot(left, right)
    return product[:, :LANES] + product[:, LANES:]


def packed(value):
    top, rest = value[:PACKED], value[PACKED:]
    lane = lax.broadcasted_iota(jnp.int32, rest.shape, 1)
    pieces = []
    for part in range(3):
        moved = pltpu.roll(rest, (ROWS - 32 * part) % LANES, 1)
        pieces.append(jnp.where(lane >= ROWS, moved, top[24 * part : 24 * part + 24]))
    return jnp.concatenate(pieces, axis=0)


def unpacked(value):
    lane = lax.broadcasted_iota(jnp.int32, (24, LANES), 1)
    rest = jnp.zeros((24, LANES), F32)
    pieces = []
    for part in range(3):
        own = value[24 * part : 24 * part + 24]
        moved = pltpu.roll(own, (LANES - ROWS + 32 * part) % LANES, 1)
        rest = jnp.where((lane >= 32 * part) & (lane < 32 * part + 32), moved, rest)
        pieces.append(jnp.where(lane < ROWS, own, 0.0))
    return jnp.concatenate(pieces + [rest], axis=0)


def granule_transpose(value):
    row = lax.broadcasted_iota(jnp.int32, value.shape, 0)
    group = lax.broadcasted_iota(jnp.int32, value.shape, 1) // NR
    height = value.shape[0]
    for bit in (1, 2, 4, 8):
        row_set = (row & bit) != 0
        group_set = (group & bit) != 0
        down = pltpu.roll(pltpu.roll(value, bit, 0), LANES - NR * bit, 1)
        up = pltpu.roll(pltpu.roll(value, height - bit, 0), NR * bit, 1)
        value = jnp.where(row_set == group_set, value, jnp.where(row_set, down, up))
    return value


def load_cells(flat_ref, pad_ref):
    cells = flat_ref.shape[0]
    width = NV * NR
    pad_ref[...] = jnp.zeros_like(pad_ref)
    for block in range(ROWS // 16):
        first = block * LANES
        wide = min(LANES, width - first)
        pad_ref[pl.ds(block * 16, cells), pl.ds(0, wide)] = flat_ref[:, pl.ds(first, wide)]
    turned = granule_transpose(pad_ref[pl.ds(0, ROWS), :])
    pad_ref[pl.ds(0, ROWS), :] = turned
    return jnp.transpose(pad_ref[...])


def store_cells(blocks, flat_ref):
    width = NV * NR
    cells = flat_ref.shape[0]
    turned = granule_transpose(jnp.transpose(blocks)[:ROWS])
    for block in range(ROWS // 16):
        first = block * LANES
        wide = min(LANES, width - first)
        flat_ref[:, pl.ds(first, wide)] = turned[block * 16 : block * 16 + cells, :wide]


def low_bit(m):
    return m & -m


def node(level_size, cells, first):
    return 2 * cells - 2 * cells // level_size + first // level_size


def kernel(
    n,
    lines,
    pivot_hbm,
    upper_hbm,
    lower_hbm,
    rhs_hbm,
    face_ref,
    coef_hbm,
    first_ref,
    second_ref,
    flat,
    rhs_ref,
    coef_ref,
    slab,
    pad,
    pivot,
    tn,
    tb,
    qw,
    ew,
    kw,
    jw,
    jp,
    hw,
    maps,
    came,
    phi,
    src,
    zs,
    us,
    xs,
    halo,
    fsend,
    gsend,
    fcame,
    gcame,
    load_sem,
    map_out,
    map_in,
    f_out,
    f_in,
    g_out,
    g_in,
    halo_out,
    halo_in,
):
    cells = rhs_ref.shape[0]
    me = lax.axis_index("narrow")
    line = lax.axis_index("wide")
    low_line = lax.rem(line + lines - 1, lines)
    high_line = lax.rem(line + 1, lines)

    loads = [
        pltpu.make_async_copy(hbm, flat.at[number], load_sem.at[number])
        for number, hbm in enumerate((pivot_hbm, upper_hbm, lower_hbm))
    ]
    loads.append(pltpu.make_async_copy(rhs_hbm, rhs_ref, load_sem.at[3]))
    loads.append(pltpu.make_async_copy(coef_hbm, coef_ref, load_sem.at[4]))
    for load in loads:
        load.start()

    fcame[...] = jnp.zeros_like(fcame)
    gcame[...] = jnp.zeros_like(gcame)

    barrier = pltpu.get_barrier_semaphore()

    def greet(step, _):
        pl.semaphore_signal(
            barrier, inc=1, device_id={"narrow": lax.rem(me + step, n)}, device_id_type=MESH
        )
        return 0

    lax.fori_loop(1, n, greet, 0)
    for other in (low_line, high_line):
        pl.semaphore_signal(barrier, inc=1, device_id={"wide": other}, device_id_type=MESH)

    slab[...] = jnp.zeros_like(slab)
    tail = jnp.zeros((LANES - ROWS, 2 * LANES), BF16)

    def clear_nodes(i, _):
        for ref in (tn, tb):
            ref[i, pl.ds(ROWS, LANES - ROWS), :] = tail
        return 0

    lax.fori_loop(0, 2 * cells - 1, clear_nodes, 0)

    def clear(i, _):
        for ref in (qw, ew, kw, jw, jp):
            ref[i, pl.ds(ROWS, LANES - ROWS), :] = tail
        return 0

    lax.fori_loop(0, cells, clear, 0)
    hw[0, pl.ds(ROWS, LANES - ROWS), :] = tail

    def clear_phi(i, _):
        phi[i] = jnp.zeros((LANES, 2 * LANES), BF16)
        return 0

    lax.fori_loop(0, n, clear_phi, 0)

    for number in range(3):
        loads[number].wait()
        for row in range(NV):
            slab[number, pl.ds(row * cells, cells), pl.ds(0, NV)] = flat[
                number, :, pl.ds(row * NV, NV)
            ].astype(F32)

    no_rows = jnp.zeros((LANES - ROWS, LANES), BF16)
    together = 4

    def multiply_blocks(group, _):
        for member in range(together):
            i = group * together + member
            p, u, l = (
                slab[number, pl.ds(i, ROWS, stride=cells), :] for number in range(3)
            )
            p16 = p.astype(BF16)
            pivot[i] = jnp.concatenate([p16, no_rows], axis=0)
            right = jnp.concatenate([(-u).astype(BF16), (-l).astype(BF16)], axis=1)
            right = jnp.concatenate([right, tail], axis=0)
            both = dot(p16, right)
            put(tn, i, both[:, :LANES])
            put(tb, i, both[:, LANES:])
        return 0

    lax.fori_loop(0, cells // together, multiply_blocks, 0)

    def join(place):
        forward = multiply(left_of((tn, 2 * place)), right_of((tn, 2 * place + 1)))
        backward = multiply(left_of((tb, 2 * place + 1)), right_of((tb, 2 * place)))
        return forward, backward

    def join_group(group, _):
        for member in range(together):
            place = group * together + member
            forward, backward = join(place)
            put(tn, cells + place, forward)
            put(tb, cells + place, backward)
        return 0

    last = cells - 2
    grouped = (cells - 4) // together
    lax.fori_loop(0, grouped, join_group, 0)
    for place in range(grouped * together, last):
        forward, backward = join(place)
        put(tn, cells + place, forward)
        put(tb, cells + place, backward)
    forward, backward = join(last)
    maps[0] = packed(forward)
    maps[1] = packed(backward)

    pl.semaphore_wait(barrier, n - 1 + 2)

    def map_copy(which, slot, target):
        return pltpu.make_async_remote_copy(
            src_ref=maps.at[which],
            dst_ref=came.at[slot],
            send_sem=map_out.at[slot],
            recv_sem=map_in.at[slot],
            device_id={"narrow": target},
            device_id_type=MESH,
        )

    def send_maps(step, _):
        @pl.when((me >= 1) & (me + step < n))
        def _():
            map_copy(0, step, me + step).start()

        @pl.when((me <= n - 2) & (me - step >= 0))
        def _():
            map_copy(1, n - step, me - step).start()

        return 0

    lax.fori_loop(1, n, send_maps, 0)
    put(tn, cells + last, forward)
    put(tb, cells + last, backward)

    def offset_copy(source, target_ref, turn, slot, out, arrived, target):
        return pltpu.make_async_remote_copy(
            src_ref=source.at[turn],
            dst_ref=target_ref.at[turn, slot],
            send_sem=out.at[turn, slot],
            recv_sem=arrived.at[turn, slot],
            device_id={"narrow": target},
            device_id_type=MESH,
        )

    def f_copy(turn, slot, target):
        return offset_copy(fsend, fcame, turn, slot, f_out, f_in, target)

    def g_copy(turn, slot, target):
        return offset_copy(gsend, gcame, turn, slot, g_out, g_in, target)

    def send_f(turn):
        def send(step, _):
            @pl.when(me + step < n)
            def _():
                f_copy(turn, step, me + step).start()

            return 0

        lax.fori_loop(1, n, send, 0)

    def send_g(turn):
        def send(step, _):
            @pl.when(me - step >= 0)
            def _():
                g_copy(turn, n - step, me - step).start()

            return 0

        lax.fori_loop(1, n, send, 0)

    def wait_f(turn):
        def wait(step, _):
            @pl.when(step <= me)
            def _():
                f_copy(turn, step, me).wait_recv()

            return 0

        lax.fori_loop(1, n, wait, 0)

    def wait_g(turn):
        def wait(step, _):
            @pl.when(me + step < n)
            def _():
                g_copy(turn, n - step, me).wait_recv()

            return 0

        lax.fori_loop(1, n, wait, 0)

    def deep(vectors, weights):
        left = jnp.concatenate([stacked_vector(v) for v in vectors], axis=1)
        right = jnp.concatenate([ref[index] for ref, index in weights], axis=0)
        return folded(dot(left, right))

    def by(vector, place):
        ref, index = place
        return folded(dot(stacked_vector(vector), ref[index]))

    def first_n(m):
        return (tn, node(m, cells, 0)) if m and low_bit(m) == m else (kw, m)

    def last_n(m):
        return (tn, node(m, cells, cells - m)) if low_bit(m) == m else (qw, m)

    def last_b(m):
        return (tb, node(m, cells, cells - m)) if m and low_bit(m) == m else (jw, m)

    def first_b(m):
        return (tb, node(m, cells, 0)) if low_bit(m) == m else (ew, m)

    row = lax.broadcasted_iota(jnp.int32, (ROWS, LANES), 0)
    column = lax.broadcasted_iota(jnp.int32, (ROWS, LANES), 1)
    unit = jnp.where((row == column) & (row < NV), 1.0, 0.0).astype(F32)
    put(kw, 0, unit)
    put(jw, 0, unit)

    loads[3].wait()
    blocks = load_cells(rhs_ref, pad)
    for i in range(cells):
        src[i] = blocks[i * NR : (i + 1) * NR]

    mixed = [m for m in range(1, cells) if low_bit(m) != m]
    for m in mixed:
        size = low_bit(m)
        at_end = node(size, cells, m - size)
        at_start = node(size, cells, cells - m)
        put(qw, m, multiply(left_of((tn, at_start)), right_of(last_n(m - size))))
        put(ew, m, multiply(left_of((tb, at_end)), right_of(first_b(m - size))))

    suffixes = [last_n(cells - i) for i in range(cells)]
    prefixes = [first_b(i + 1) for i in range(cells)]

    fsend[0] = deep([src[i] for i in range(cells)], suffixes)
    send_f(0)

    for m in mixed:
        size = low_bit(m)
        at_end = node(size, cells, m - size)
        at_start = node(size, cells, cells - m)
        put(kw, m, multiply(left_of(first_n(m - size)), right_of((tn, at_end))))
        put(jw, m, multiply(left_of(last_b(m - size)), right_of((tb, at_start))))

    response = multiply(
        jnp.concatenate([left_of(first_n(i)) for i in range(cells)], axis=1),
        jnp.concatenate([right_of(first_b(i + 1)) for i in range(cells)], axis=0),
    )
    put(hw, 0, response)
    for i in range(cells):
        exact = pivot[i]
        put(jp, i, dot(left_of(last_b(cells - 1 - i)), jnp.concatenate([exact, exact], axis=0)))

    def sweep():
        def forward(i, z):
            z = src[i] + by(z, (tn, i - 1))
            zs[i] = z
            return z

        zs[0] = src[0]
        lax.fori_loop(1, cells, forward, src[0])

    sweep()

    @pl.when(me >= 1)
    def _():
        put(phi, 1, unit)

    @pl.when(me <= n - 2)
    def _():
        put(phi, n - 1, unit)

    def extend(slot, towards):
        high, low = parts(unpacked(came[slot]))
        put(phi, towards, multiply(jnp.concatenate([high, low], axis=1), right_of((phi, slot))))

    def chain(step, _):
        @pl.when(step <= me - 1)
        def _():
            map_copy(0, step, me).wait_recv()
            extend(step, step + 1)

        @pl.when(step <= n - 2 - me)
        def _():
            map_copy(1, n - step, me).wait_recv()
            extend(n - step, n - step - 1)

        return 0

    lax.fori_loop(1, n - 1, chain, 0)

    between = [(phi, k) for k in range(n)]

    def finish(turn):
        alone = deep([zs[i] for i in range(cells)], prefixes)
        wait_f(turn)
        entering = deep([fcame[turn, k] for k in range(n)], between)
        left = stacked_vector(entering)
        gsend[turn] = alone + folded(dot(left, hw[0]))
        send_g(turn)
        for i in range(cells):
            ref, index = first_n(i)
            zs[i] = zs[i] + folded(dot(left, ref[index]))
        us[cells - 1] = zs[cells - 1]

        def backward(i, u):
            back = cells - 1 - i
            u = zs[back] + by(u, (tb, back + 1))
            us[back] = u
            return u

        lax.fori_loop(1, cells, backward, zs[cells - 1])
        for i in range(cells):
            product = dot(stacked_vector(us[i]), pivot[i])
            xs[turn, i] = product[:NR] + product[NR:]
        wait_g(turn)
        entering = deep([gcame[turn, k] for k in range(n)], between)
        left = stacked_vector(entering)
        for i in range(cells):
            xs[turn, i] = xs[turn, i] + folded(dot(left, jp[i]))

    finish(0)

    def halo_copy(side, other):
        return pltpu.make_async_remote_copy(
            src_ref=xs.at[0],
            dst_ref=halo.at[side],
            send_sem=halo_out.at[side],
            recv_sem=halo_in.at[side],
            device_id={"wide": other},
            device_id_type=MESH,
        )

    halo_copy(0, high_line).start()
    halo_copy(1, low_line).start()

    store_cells(xs[0].reshape(cells * NR, LANES), first_ref)

    loads[4].wait()
    weights = []
    for place in range(3):
        total = jnp.zeros((cells, NV), F32)
        for side in range(2):
            relative = lax.rem(face_ref[0, side] - line + 1 + lines, lines)
            total = total + jnp.where(
                relative == place, coef_ref[:, pl.ds(side * NV, NV)], 0.0
            )
        weights.append(jnp.concatenate([total, jnp.zeros((cells, LANES - NV), F32)], axis=1))

    halo_copy(0, high_line).wait_recv()
    halo_copy(1, low_line).wait_recv()

    for i in range(cells):
        coupled = (
            weights[0][i : i + 1] * halo[0, i]
            + weights[1][i : i + 1] * xs[0, i]
            + weights[2][i : i + 1] * halo[1, i]
        )
        src[i] = src[i] - coupled

    fsend[1] = deep([src[i] for i in range(cells)], suffixes)
    send_f(1)
    sweep()
    finish(1)
    store_cells(xs[1].reshape(cells * NR, LANES), second_ref)

    halo_copy(0, high_line).wait_send()
    halo_copy(1, low_line).wait_send()

    def drain(step, _):
        @pl.when(me + step < n)
        def _():
            f_copy(0, step, me + step).wait_send()
            f_copy(1, step, me + step).wait_send()

        @pl.when(me - step >= 0)
        def _():
            g_copy(0, n - step, me - step).wait_send()
            g_copy(1, n - step, me - step).wait_send()

        @pl.when((me >= 1) & (me + step < n))
        def _():
            map_copy(0, step, me + step).wait_send()

        @pl.when((me <= n - 2) & (me - step >= 0))
        def _():
            map_copy(1, n - step, me - step).wait_send()

        return 0

    lax.fori_loop(1, n, drain, 0)


def body(n, lines, rhs, pivot, upper, lower, neighbors, coupling):
    cells = rhs.shape[1]
    matrix = (LANES, 2 * LANES)
    tree = pltpu.VMEM((2 * cells - 1, *matrix), BF16)
    weight = pltpu.VMEM((cells, *matrix), BF16)
    vectors = pltpu.VMEM((cells, NR, LANES), F32)
    vmem = pl.BlockSpec(memory_space=pltpu.VMEM)
    hbm = pl.BlockSpec(memory_space=pltpu.HBM)
    dma = pltpu.SemaphoreType.DMA
    first, second = pl.pallas_call(
        functools.partial(kernel, n, lines),
        out_shape=[jax.ShapeDtypeStruct((cells, NV * NR), F32)] * 2,
        in_specs=[hbm] * 4 + [pl.BlockSpec(memory_space=pltpu.SMEM), hbm],
        out_specs=[vmem] * 2,
        scratch_shapes=[
            pltpu.VMEM((3, cells, NV * NV), BF16),
            pltpu.VMEM((cells, NV * NR), F32),
            pltpu.VMEM((cells, 2 * NV), F32),
            pltpu.VMEM((3, ROWS * cells, LANES), F32),
            pltpu.VMEM((LANES, LANES), F32),
            pltpu.VMEM((cells, LANES, LANES), BF16),
            tree,
            tree,
            weight,
            weight,
            weight,
            weight,
            weight,
            pltpu.VMEM((1, *matrix), BF16),
            pltpu.VMEM((2, PACKED, LANES), F32),
            pltpu.VMEM((n, PACKED, LANES), F32),
            pltpu.VMEM((n, *matrix), BF16),
            vectors,
            vectors,
            vectors,
            pltpu.VMEM((2, cells, NR, LANES), F32),
            pltpu.VMEM((2, cells, NR, LANES), F32),
            pltpu.VMEM((2, NR, LANES), F32),
            pltpu.VMEM((2, NR, LANES), F32),
            pltpu.VMEM((2, n, NR, LANES), F32),
            pltpu.VMEM((2, n, NR, LANES), F32),
            dma((5,)),
            dma((n,)),
            dma((n,)),
            dma((2, n)),
            dma((2, n)),
            dma((2, n)),
            dma((2, n)),
            dma((2,)),
            dma((2,)),
        ],
        compiler_params=pltpu.CompilerParams(
            collective_id=0, has_side_effects=True, vmem_limit_bytes=56 * 1024 * 1024
        ),
    )(pivot[0], upper[0], lower[0], rhs[0], neighbors, coupling[0])
    return first[None], second[None]


def solution(mesh):
    blocks = P("wide", "narrow", None)
    return jax.shard_map(
        functools.partial(body, mesh.shape["narrow"], mesh.shape["wide"]),
        mesh=mesh,
        in_specs=(blocks, blocks, blocks, blocks, P("wide", None), blocks),
        out_specs=(blocks, blocks),
        check_vma=False,
    )
```

```python
import functools

import jax
import jax.numpy as jnp
from jax import lax
from jax.experimental import pallas as pl
from jax.experimental.pallas import tpu as pltpu
from jax.sharding import PartitionSpec as P

NV = 95
NR = 8
ROWS = 96
PACKED = 72
LANES = 128
F32 = jnp.float32
BF16 = jnp.bfloat16
MESH = pl.DeviceIdType.MESH


def dot(left, right):
    return jnp.dot(left, right, preferred_element_type=F32)


def parts(value):
    high = value.astype(BF16)
    return high, (value - high.astype(F32)).astype(BF16)


def stacked_vector(value):
    high = value.astype(BF16).astype(F32)
    return jnp.concatenate([high, value - high], axis=0).astype(BF16)


def folded(product):
    rows = product.shape[0] // 2
    return product[:rows, :LANES] + (product[:rows, LANES:] + product[rows:, :LANES])


def put(ref, index, value):
    high, low = parts(value)
    ref[index, pl.ds(0, ROWS), pl.ds(0, LANES)] = high
    ref[index, pl.ds(0, ROWS), pl.ds(LANES, LANES)] = low


def left_of(place):
    ref, index = place
    return ref[index, pl.ds(0, ROWS), :]


def right_of(place):
    ref, index = place
    value = ref[index]
    return jnp.concatenate([value, value], axis=0)


def multiply(left, right):
    product = dot(left, right)
    return product[:, :LANES] + product[:, LANES:]


def packed(value):
    top, rest = value[:PACKED], value[PACKED:]
    lane = lax.broadcasted_iota(jnp.int32, rest.shape, 1)
    pieces = []
    for part in range(3):
        moved = pltpu.roll(rest, (ROWS - 32 * part) % LANES, 1)
        pieces.append(jnp.where(lane >= ROWS, moved, top[24 * part : 24 * part + 24]))
    return jnp.concatenate(pieces, axis=0)


def unpacked(value):
    lane = lax.broadcasted_iota(jnp.int32, (24, LANES), 1)
    rest = jnp.zeros((24, LANES), F32)
    pieces = []
    for part in range(3):
        own = value[24 * part : 24 * part + 24]
        moved = pltpu.roll(own, (LANES - ROWS + 32 * part) % LANES, 1)
        rest = jnp.where((lane >= 32 * part) & (lane < 32 * part + 32), moved, rest)
        pieces.append(jnp.where(lane < ROWS, own, 0.0))
    return jnp.concatenate(pieces + [rest], axis=0)


def granule_transpose(value):
    row = lax.broadcasted_iota(jnp.int32, value.shape, 0)
    group = lax.broadcasted_iota(jnp.int32, value.shape, 1) // NR
    height = value.shape[0]
    for bit in (1, 2, 4, 8):
        row_set = (row & bit) != 0
        group_set = (group & bit) != 0
        down = pltpu.roll(pltpu.roll(value, bit, 0), LANES - NR * bit, 1)
        up = pltpu.roll(pltpu.roll(value, height - bit, 0), NR * bit, 1)
        value = jnp.where(row_set == group_set, value, jnp.where(row_set, down, up))
    return value


def load_cells(flat_ref, pad_ref):
    cells = flat_ref.shape[0]
    width = NV * NR
    pad_ref[...] = jnp.zeros_like(pad_ref)
    for block in range(ROWS // 16):
        first = block * LANES
        wide = min(LANES, width - first)
        pad_ref[pl.ds(block * 16, cells), pl.ds(0, wide)] = flat_ref[:, pl.ds(first, wide)]
    turned = granule_transpose(pad_ref[pl.ds(0, ROWS), :])
    pad_ref[pl.ds(0, ROWS), :] = turned
    return jnp.transpose(pad_ref[...])


def store_cells(blocks, flat_ref):
    width = NV * NR
    cells = flat_ref.shape[0]
    turned = granule_transpose(jnp.transpose(blocks)[:ROWS])
    for block in range(ROWS // 16):
        first = block * LANES
        wide = min(LANES, width - first)
        flat_ref[:, pl.ds(first, wide)] = turned[block * 16 : block * 16 + cells, :wide]


def low_bit(m):
    return m & -m


def node(level_size, cells, first):
    return 2 * cells - 2 * cells // level_size + first // level_size


def kernel(
    n,
    lines,
    pivot_hbm,
    upper_hbm,
    lower_hbm,
    rhs_hbm,
    face_ref,
    coef_hbm,
    first_ref,
    second_ref,
    flat,
    rhs_ref,
    coef_ref,
    slab,
    pad,
    pivot,
    tn,
    tb,
    ew,
    kw,
    jw,
    jp,
    hw,
    hsum,
    rho,
    maps,
    came,
    answers,
    answered,
    phi,
    src,
    zs,
    xs,
    halo,
    fsend,
    gsend,
    fcame,
    gcame,
    load_sem,
    map_out,
    map_in,
    answer_out,
    answer_in,
    f_out,
    f_in,
    g_out,
    g_in,
    halo_out,
    halo_in,
):
    cells = rhs_ref.shape[0]
    me = lax.axis_index("narrow")
    line = lax.axis_index("wide")
    low_line = lax.rem(line + lines - 1, lines)
    high_line = lax.rem(line + 1, lines)

    loads = [
        pltpu.make_async_copy(hbm, flat.at[number], load_sem.at[number])
        for number, hbm in enumerate((pivot_hbm, upper_hbm, lower_hbm))
    ]
    loads.append(pltpu.make_async_copy(rhs_hbm, rhs_ref, load_sem.at[3]))
    loads.append(pltpu.make_async_copy(coef_hbm, coef_ref, load_sem.at[4]))
    for load in loads:
        load.start()

    fcame[...] = jnp.zeros_like(fcame)
    gcame[...] = jnp.zeros_like(gcame)
    answered[...] = jnp.zeros_like(answered)

    barrier = pltpu.get_barrier_semaphore()

    def greet(step, _):
        pl.semaphore_signal(
            barrier, inc=1, device_id={"narrow": lax.rem(me + step, n)}, device_id_type=MESH
        )
        return 0

    lax.fori_loop(1, n, greet, 0)
    for other in (low_line, high_line):
        pl.semaphore_signal(barrier, inc=1, device_id={"wide": other}, device_id_type=MESH)

    slab[...] = jnp.zeros_like(slab)
    tail = jnp.zeros((LANES - ROWS, 2 * LANES), BF16)

    def clear_nodes(i, _):
        for ref in (tn, tb):
            ref[i, pl.ds(ROWS, LANES - ROWS), :] = tail
        return 0

    lax.fori_loop(0, 2 * cells - 1, clear_nodes, 0)

    def clear(i, _):
        for ref in (ew, kw, jw, jp):
            ref[i, pl.ds(ROWS, LANES - ROWS), :] = tail
        return 0

    lax.fori_loop(0, cells, clear, 0)
    hw[0, pl.ds(ROWS, LANES - ROWS), :] = tail
    for i in range(3):
        rho[i, pl.ds(ROWS, LANES - ROWS), :] = tail

    def clear_phi(i, _):
        phi[i] = jnp.zeros((LANES, 2 * LANES), BF16)
        return 0

    lax.fori_loop(0, n, clear_phi, 0)

    for number in range(3):
        loads[number].wait()
        for row in range(NV):
            slab[number, pl.ds(row * cells, cells), pl.ds(0, NV)] = flat[
                number, :, pl.ds(row * NV, NV)
            ].astype(F32)

    no_rows = jnp.zeros((LANES - ROWS, LANES), BF16)
    together = 4

    def multiply_blocks(group, _):
        for member in range(together):
            i = group * together + member
            p, u, l = (
                slab[number, pl.ds(i, ROWS, stride=cells), :] for number in range(3)
            )
            p16 = p.astype(BF16)
            pivot[i] = jnp.concatenate([p16, no_rows], axis=0)
            right = jnp.concatenate([(-u).astype(BF16), (-l).astype(BF16)], axis=1)
            right = jnp.concatenate([right, tail], axis=0)
            both = dot(p16, right)
            put(tn, i, both[:, :LANES])
            put(tb, i, both[:, LANES:])
        return 0

    lax.fori_loop(0, cells // together, multiply_blocks, 0)

    def join(place):
        forward = multiply(left_of((tn, 2 * place)), right_of((tn, 2 * place + 1)))
        backward = multiply(left_of((tb, 2 * place + 1)), right_of((tb, 2 * place)))
        return forward, backward

    def join_group(group, _):
        for member in range(together):
            place = group * together + member
            forward, backward = join(place)
            put(tn, cells + place, forward)
            put(tb, cells + place, backward)
        return 0

    last = cells - 2
    grouped = (cells - 4) // together
    lax.fori_loop(0, grouped, join_group, 0)
    for place in range(grouped * together, last):
        forward, backward = join(place)
        put(tn, cells + place, forward)
        put(tb, cells + place, backward)
    forward, backward = join(last)
    maps[0] = packed(forward)
    maps[1] = packed(backward)

    pl.semaphore_wait(barrier, n - 1 + 2)

    def map_copy(which, slot, target):
        return pltpu.make_async_remote_copy(
            src_ref=maps.at[which],
            dst_ref=came.at[slot],
            send_sem=map_out.at[slot],
            recv_sem=map_in.at[slot],
            device_id={"narrow": target},
            device_id_type=MESH,
        )

    def send_maps(step, _):
        @pl.when((me >= 1) & (me + step < n))
        def _():
            map_copy(0, step, me + step).start()

        @pl.when((me <= n - 2) & (me - step >= 0))
        def _():
            map_copy(1, n - step, me - step).start()

        return 0

    lax.fori_loop(1, n, send_maps, 0)
    whole = cells + last
    put(tn, whole, forward)
    put(tb, whole, backward)

    def offset_copy(source, target_ref, turn, slot, out, arrived, target):
        return pltpu.make_async_remote_copy(
            src_ref=source.at[turn],
            dst_ref=target_ref.at[turn, slot],
            send_sem=out.at[turn, slot],
            recv_sem=arrived.at[turn, slot],
            device_id={"narrow": target},
            device_id_type=MESH,
        )

    def f_copy(turn, slot, target):
        return offset_copy(fsend, fcame, turn, slot, f_out, f_in, target)

    def g_copy(turn, slot, target):
        return offset_copy(gsend, gcame, turn, slot, g_out, g_in, target)

    def send_f(turn):
        def send(step, _):
            @pl.when(me + step < n)
            def _():
                f_copy(turn, step, me + step).start()

            return 0

        lax.fori_loop(1, n, send, 0)

    def send_g(turn):
        def send(step, _):
            @pl.when(me - step >= 0)
            def _():
                g_copy(turn, n - step, me - step).start()

            return 0

        lax.fori_loop(1, n, send, 0)

    def wait_f(turn):
        def wait(step, _):
            @pl.when(step <= me)
            def _():
                f_copy(turn, step, me).wait_recv()

            return 0

        lax.fori_loop(1, n, wait, 0)

    def wait_g(turn):
        def wait(step, _):
            @pl.when(me + step < n)
            def _():
                g_copy(turn, n - step, me).wait_recv()

            return 0

        lax.fori_loop(1, n, wait, 0)

    def deep(vectors, weights):
        left = jnp.concatenate([stacked_vector(v) for v in vectors], axis=1)
        right = jnp.concatenate([ref[index] for ref, index in weights], axis=0)
        return folded(dot(left, right))

    def by(vector, place):
        ref, index = place
        return folded(dot(stacked_vector(vector), ref[index]))

    def forward_node(size, first):
        return tn, node(size, cells, first)

    def backward_node(size, first):
        return tb, node(size, cells, cells - first - size)

    def climb(source, at, whole):
        sums, source = {}, list(source)
        for p in range(0, cells, 2):
            source[p + 1] = source[p + 1] + by(source[p], at(1, p))
        for p in range(0, cells, 2):
            sums[2, p] = by(source[p + 1], at(1, p + 1))
        size = 2
        while size < cells // 2 or (whole and size < cells):
            for p in range(0, cells, 2 * size):
                sums[2 * size, p] = sums[size, p + size] + by(sums[size, p], at(size, p + size))
            size *= 2
        return source, sums

    def descend(source, sums, at):
        entering = {0: None}
        size = cells // 2
        while size >= 2:
            for p in range(0, cells, 2 * size):
                after = sums[size, p]
                if entering[p] is not None:
                    after = after + by(entering[p], at(size, p))
                entering[p + size] = after
            size //= 2
        values = list(source)
        for p in range(0, cells, 2):
            if entering[p] is not None:
                values[p] = values[p] + entering[p]
                values[p + 1] = values[p + 1] + by(entering[p], at(1, p))
        return values

    row = lax.broadcasted_iota(jnp.int32, (ROWS, LANES), 0)
    column = lax.broadcasted_iota(jnp.int32, (ROWS, LANES), 1)
    unit = jnp.where((row == column) & (row < NV), 1.0, 0.0).astype(F32)
    put(kw, 0, unit)
    put(jw, cells - 1, unit)
    ew[0] = tb[0]
    hsum[...] = jnp.zeros_like(hsum)
    came[0] = jnp.zeros_like(came[0])

    @pl.when(me >= 1)
    def _():
        put(phi, 1, unit)

    @pl.when(me <= n - 2)
    def _():
        put(phi, n - 1, unit)

    def start(turn):
        source, sums = climb([src[i] for i in range(cells)], forward_node, True)
        leaving = sums[cells, 0]
        fsend[turn] = leaving
        send_f(turn)
        for i, value in enumerate(descend(source, sums, forward_node)):
            zs[i] = value
        return leaving

    loads[3].wait()
    blocks = load_cells(rhs_ref, pad)
    for i in range(cells):
        src[i] = blocks[i * NR : (i + 1) * NR]
    start(0)

    from_before = jnp.maximum(me - 1, 0)
    from_after = jnp.maximum(n - 2 - me, 0)

    def with_pivot(i):
        exact = pivot[i]
        put(jp, i, dot(left_of((jw, i)), jnp.concatenate([exact, exact], axis=0)))

    def tables(step, _):
        before = step <= from_before
        after = step - from_before
        arrived = before | (after <= from_after)
        slot = jnp.where(before, step, jnp.where(arrived, n - after, 0))
        towards = jnp.where(before, step + 1, jnp.where(arrived, n - after - 1, n))

        @pl.when(arrived)
        def _():
            map_copy(0, slot, me).wait_recv()

        high, low = parts(unpacked(came[slot]))
        chained = multiply(jnp.concatenate([high, low], axis=1), right_of((phi, slot)))
        back = cells - 1 - step
        k = multiply(left_of((kw, step - 1)), right_of((tn, step - 1)))
        e = multiply(left_of((tb, step)), right_of((ew, step - 1)))
        j = multiply(left_of((jw, back + 1)), right_of((tb, back + 1)))
        h = multiply(left_of((kw, step - 1)), right_of((ew, step - 1)))
        with_pivot(back + 1)
        put(phi, towards, chained)
        put(kw, step, k)
        put(ew, step, e)
        put(jw, back, j)
        hsum[...] += h
        return 0

    lax.fori_loop(1, cells, tables, 0)
    with_pivot(0)
    put(hw, 0, hsum[...] + multiply(left_of((kw, cells - 1)), right_of((ew, cells - 1))))

    between = [(phi, k) for k in range(n)]

    def answer_copy(slot, target):
        return pltpu.make_async_remote_copy(
            src_ref=answers.at[slot],
            dst_ref=answered.at[slot],
            send_sem=answer_out.at[slot],
            recv_sem=answer_in.at[slot],
            device_id={"narrow": target},
            device_id_type=MESH,
        )

    def send_answers():
        high_low = jnp.concatenate([left_of((phi, k)) for k in range(1, n)], axis=0)
        products = multiply(high_low, right_of((hw, 0)))
        for k in range(1, n):
            answers[n - k] = packed(products[(k - 1) * ROWS : k * ROWS])

        def send(step, _):
            answer_copy(n - step, me - step).start()
            return 0

        lax.fori_loop(1, me + 1, send, 0)

    def take_answers():
        def wait(step, _):
            answer_copy(n - step, me).wait_recv()
            return 0

        lax.fori_loop(1, n - me, wait, 0)
        left = []
        for k in range(1, n):
            high, low = parts(unpacked(answered[k]))
            left += [high, low]
        put(
            rho,
            0,
            multiply(
                jnp.concatenate(left, axis=1),
                jnp.concatenate([right_of((phi, k)) for k in range(1, n)], axis=0),
            ),
        )
        put(rho, 1, multiply(left_of((rho, 0)), right_of((tb, whole))))
        put(rho, 2, multiply(left_of((tn, whole)), right_of((rho, 0))))

    def inside(turn, left):
        z = [zs[i] + folded(dot(left, kw[i])) for i in range(cells)]
        source, sums = climb(z[::-1], backward_node, False)
        for p, u in enumerate(descend(source, sums, backward_node)):
            i = cells - 1 - p
            product = dot(stacked_vector(u), pivot[i])
            xs[turn, i] = product[:NR] + product[NR:]

    def complete(turn, entering):
        left = stacked_vector(entering)
        for i in range(cells):
            xs[turn, i] = xs[turn, i] + folded(dot(left, jp[i]))

    def backward_alone():
        return deep([zs[i] for i in range(cells)], [(ew, i) for i in range(cells)])

    alone = backward_alone()
    wait_f(0)
    left = stacked_vector(deep([fcame[0, k] for k in range(n)], between))
    gsend[0] = alone + folded(dot(left, hw[0]))
    send_g(0)
    send_answers()
    inside(0, left)
    wait_g(0)
    complete(0, deep([gcame[0, k] for k in range(n)], between))

    def halo_copy(side, other):
        return pltpu.make_async_remote_copy(
            src_ref=xs.at[0],
            dst_ref=halo.at[side],
            send_sem=halo_out.at[side],
            recv_sem=halo_in.at[side],
            device_id={"wide": other},
            device_id_type=MESH,
        )

    halo_copy(0, high_line).start()
    halo_copy(1, low_line).start()

    store_cells(xs[0].reshape(cells * NR, LANES), first_ref)

    loads[4].wait()
    weights = []
    for place in range(3):
        total = jnp.zeros((cells, NV), F32)
        for side in range(2):
            relative = lax.rem(face_ref[0, side] - line + 1 + lines, lines)
            total = total + jnp.where(
                relative == place, coef_ref[:, pl.ds(side * NV, NV)], 0.0
            )
        weights.append(jnp.concatenate([total, jnp.zeros((cells, LANES - NV), F32)], axis=1))

    take_answers()

    halo_copy(0, high_line).wait_recv()
    halo_copy(1, low_line).wait_recv()

    for i in range(cells):
        coupled = (
            weights[0][i : i + 1] * halo[0, i]
            + weights[1][i : i + 1] * xs[0, i]
            + weights[2][i : i + 1] * halo[1, i]
        )
        src[i] = src[i] - coupled

    leaving = start(1)
    gsend[1] = backward_alone() + by(leaving, (rho, 1))
    send_g(1)
    wait_f(1)
    left = stacked_vector(deep([fcame[1, k] for k in range(n)], between))
    inside(1, left)
    back = by(leaving, (rho, 0)) + folded(dot(left, rho[2]))
    wait_g(1)
    complete(1, back + deep([gcame[1, k] for k in range(n)], between))
    store_cells(xs[1].reshape(cells * NR, LANES), second_ref)

    halo_copy(0, high_line).wait_send()
    halo_copy(1, low_line).wait_send()

    def drain(step, _):
        @pl.when(me + step < n)
        def _():
            f_copy(0, step, me + step).wait_send()
            f_copy(1, step, me + step).wait_send()

        @pl.when(me - step >= 0)
        def _():
            g_copy(0, n - step, me - step).wait_send()
            g_copy(1, n - step, me - step).wait_send()
            answer_copy(n - step, me - step).wait_send()

        @pl.when((me >= 1) & (me + step < n))
        def _():
            map_copy(0, step, me + step).wait_send()

        @pl.when((me <= n - 2) & (me - step >= 0))
        def _():
            map_copy(1, n - step, me - step).wait_send()

        return 0

    lax.fori_loop(1, n, drain, 0)


def body(n, lines, rhs, pivot, upper, lower, neighbors, coupling):
    cells = rhs.shape[1]
    matrix = (LANES, 2 * LANES)
    tree = pltpu.VMEM((2 * cells - 1, *matrix), BF16)
    weight = pltpu.VMEM((cells, *matrix), BF16)
    vectors = pltpu.VMEM((cells, NR, LANES), F32)
    vmem = pl.BlockSpec(memory_space=pltpu.VMEM)
    hbm = pl.BlockSpec(memory_space=pltpu.HBM)
    dma = pltpu.SemaphoreType.DMA
    first, second = pl.pallas_call(
        functools.partial(kernel, n, lines),
        out_shape=[jax.ShapeDtypeStruct((cells, NV * NR), F32)] * 2,
        in_specs=[hbm] * 4 + [pl.BlockSpec(memory_space=pltpu.SMEM), hbm],
        out_specs=[vmem] * 2,
        scratch_shapes=[
            pltpu.VMEM((3, cells, NV * NV), BF16),
            pltpu.VMEM((cells, NV * NR), F32),
            pltpu.VMEM((cells, 2 * NV), F32),
            pltpu.VMEM((3, ROWS * cells, LANES), F32),
            pltpu.VMEM((LANES, LANES), F32),
            pltpu.VMEM((cells, LANES, LANES), BF16),
            tree,
            tree,
            weight,
            weight,
            weight,
            weight,
            pltpu.VMEM((1, *matrix), BF16),
            pltpu.VMEM((ROWS, LANES), F32),
            pltpu.VMEM((3, *matrix), BF16),
            pltpu.VMEM((2, PACKED, LANES), F32),
            pltpu.VMEM((n, PACKED, LANES), F32),
            pltpu.VMEM((n, PACKED, LANES), F32),
            pltpu.VMEM((n, PACKED, LANES), F32),
            pltpu.VMEM((n + 1, *matrix), BF16),
            vectors,
            vectors,
            pltpu.VMEM((2, cells, NR, LANES), F32),
            pltpu.VMEM((2, cells, NR, LANES), F32),
            pltpu.VMEM((2, NR, LANES), F32),
            pltpu.VMEM((2, NR, LANES), F32),
            pltpu.VMEM((2, n, NR, LANES), F32),
            pltpu.VMEM((2, n, NR, LANES), F32),
            dma((5,)),
            dma((n,)),
            dma((n,)),
            dma((n,)),
            dma((n,)),
            dma((2, n)),
            dma((2, n)),
            dma((2, n)),
            dma((2, n)),
            dma((2,)),
            dma((2,)),
        ],
        compiler_params=pltpu.CompilerParams(
            collective_id=0, has_side_effects=True, vmem_limit_bytes=56 * 1024 * 1024
        ),
    )(pivot[0], upper[0], lower[0], rhs[0], neighbors, coupling[0])
    return first[None], second[None]


def solution(mesh):
    blocks = P("wide", "narrow", None)
    return jax.shard_map(
        functools.partial(body, mesh.shape["narrow"], mesh.shape["wide"]),
        mesh=mesh,
        in_specs=(blocks, blocks, blocks, blocks, P("wide", None), blocks),
        out_specs=(blocks, blocks),
        check_vma=False,
    )
```

```python
import functools

import jax
import jax.numpy as jnp
from jax import lax
from jax.experimental import pallas as pl
from jax.experimental.pallas import tpu as pltpu
from jax.sharding import PartitionSpec as P

NV = 95
NR = 8
ROWS = 96
PACKED = 72
LANES = 128
F32 = jnp.float32
BF16 = jnp.bfloat16
MESH = pl.DeviceIdType.MESH


def dot(left, right):
    return jnp.dot(left, right, preferred_element_type=F32)


def parts(value):
    high = value.astype(BF16)
    return high, (value - high.astype(F32)).astype(BF16)


def stacked_vector(value):
    high = value.astype(BF16).astype(F32)
    return jnp.concatenate([high, value - high], axis=0).astype(BF16)


def folded(product):
    rows = product.shape[0] // 2
    return product[:rows, :LANES] + (product[:rows, LANES:] + product[rows:, :LANES])


def put(ref, index, value):
    high, low = parts(value)
    ref[index, pl.ds(0, ROWS), pl.ds(0, LANES)] = high
    ref[index, pl.ds(0, ROWS), pl.ds(LANES, LANES)] = low


def left_of(place):
    ref, index = place
    return ref[index, pl.ds(0, ROWS), :]


def right_of(place):
    ref, index = place
    value = ref[index]
    return jnp.concatenate([value, value], axis=0)


def multiply(left, right):
    product = dot(left, right)
    return product[:, :LANES] + product[:, LANES:]


def packed(value):
    top, rest = value[:PACKED], value[PACKED:]
    lane = lax.broadcasted_iota(jnp.int32, rest.shape, 1)
    pieces = []
    for part in range(3):
        moved = pltpu.roll(rest, (ROWS - 32 * part) % LANES, 1)
        pieces.append(jnp.where(lane >= ROWS, moved, top[24 * part : 24 * part + 24]))
    return jnp.concatenate(pieces, axis=0)


def unpacked(value):
    lane = lax.broadcasted_iota(jnp.int32, (24, LANES), 1)
    rest = jnp.zeros((24, LANES), F32)
    pieces = []
    for part in range(3):
        own = value[24 * part : 24 * part + 24]
        moved = pltpu.roll(own, (LANES - ROWS + 32 * part) % LANES, 1)
        rest = jnp.where((lane >= 32 * part) & (lane < 32 * part + 32), moved, rest)
        pieces.append(jnp.where(lane < ROWS, own, 0.0))
    return jnp.concatenate(pieces + [rest], axis=0)


def granule_transpose(value):
    row = lax.broadcasted_iota(jnp.int32, value.shape, 0)
    group = lax.broadcasted_iota(jnp.int32, value.shape, 1) // NR
    height = value.shape[0]
    for bit in (1, 2, 4, 8):
        row_set = (row & bit) != 0
        group_set = (group & bit) != 0
        down = pltpu.roll(pltpu.roll(value, bit, 0), LANES - NR * bit, 1)
        up = pltpu.roll(pltpu.roll(value, height - bit, 0), NR * bit, 1)
        value = jnp.where(row_set == group_set, value, jnp.where(row_set, down, up))
    return value


def load_cells(flat_ref, pad_ref):
    cells = flat_ref.shape[0]
    width = NV * NR
    pad_ref[...] = jnp.zeros_like(pad_ref)
    for block in range(ROWS // 16):
        first = block * LANES
        wide = min(LANES, width - first)
        pad_ref[pl.ds(block * 16, cells), pl.ds(0, wide)] = flat_ref[:, pl.ds(first, wide)]
    turned = granule_transpose(pad_ref[pl.ds(0, ROWS), :])
    pad_ref[pl.ds(0, ROWS), :] = turned
    return jnp.transpose(pad_ref[...])


def store_cells(blocks, flat_ref):
    width = NV * NR
    cells = flat_ref.shape[0]
    turned = granule_transpose(jnp.transpose(blocks)[:ROWS])
    for block in range(ROWS // 16):
        first = block * LANES
        wide = min(LANES, width - first)
        flat_ref[:, pl.ds(first, wide)] = turned[block * 16 : block * 16 + cells, :wide]


def far_first(n):
    return sorted(range(1, n), key=lambda step: -sum(min(d, 4 - d) for d in (step % 4, step // 4 % 4)))


def low_bit(m):
    return m & -m


def node(level_size, cells, first):
    return 2 * cells - 2 * cells // level_size + first // level_size


def kernel(
    n,
    lines,
    pivot_hbm,
    upper_hbm,
    lower_hbm,
    rhs_hbm,
    face_ref,
    coef_hbm,
    first_ref,
    second_ref,
    flat,
    rhs_ref,
    coef_ref,
    slab,
    pad,
    pivot,
    tn,
    tb,
    ew,
    kw,
    jw,
    jp,
    hw,
    hsum,
    rho,
    maps,
    came,
    answers,
    answered,
    phi,
    src,
    zs,
    xs,
    halo,
    fsend,
    gsend,
    fcame,
    gcame,
    load_sem,
    map_out,
    map_in,
    answer_out,
    answer_in,
    f_out,
    f_in,
    g_out,
    g_in,
    halo_out,
    halo_in,
):
    cells = rhs_ref.shape[0]
    me = lax.axis_index("narrow")
    line = lax.axis_index("wide")
    low_line = lax.rem(line + lines - 1, lines)
    high_line = lax.rem(line + 1, lines)

    loads = [
        pltpu.make_async_copy(hbm, flat.at[number], load_sem.at[number])
        for number, hbm in enumerate((pivot_hbm, upper_hbm, lower_hbm))
    ]
    loads.append(pltpu.make_async_copy(rhs_hbm, rhs_ref, load_sem.at[3]))
    loads.append(pltpu.make_async_copy(coef_hbm, coef_ref, load_sem.at[4]))
    for load in loads:
        load.start()

    fcame[...] = jnp.zeros_like(fcame)
    gcame[...] = jnp.zeros_like(gcame)
    answered[...] = jnp.zeros_like(answered)

    barrier = pltpu.get_barrier_semaphore()

    def greet(step, _):
        pl.semaphore_signal(
            barrier, inc=1, device_id={"narrow": lax.rem(me + step, n)}, device_id_type=MESH
        )
        return 0

    lax.fori_loop(1, n, greet, 0)
    for other in (low_line, high_line):
        pl.semaphore_signal(barrier, inc=1, device_id={"wide": other}, device_id_type=MESH)

    slab[...] = jnp.zeros_like(slab)
    tail = jnp.zeros((LANES - ROWS, 2 * LANES), BF16)

    def clear_nodes(i, _):
        for ref in (tn, tb):
            ref[i, pl.ds(ROWS, LANES - ROWS), :] = tail
        return 0

    lax.fori_loop(0, 2 * cells - 1, clear_nodes, 0)

    def clear(i, _):
        for ref in (ew, kw, jw, jp):
            ref[i, pl.ds(ROWS, LANES - ROWS), :] = tail
        return 0

    lax.fori_loop(0, cells, clear, 0)
    hw[0, pl.ds(ROWS, LANES - ROWS), :] = tail
    for i in range(3):
        rho[i, pl.ds(ROWS, LANES - ROWS), :] = tail

    def clear_phi(i, _):
        phi[i] = jnp.zeros((LANES, 2 * LANES), BF16)
        return 0

    lax.fori_loop(0, n, clear_phi, 0)

    for number in range(3):
        loads[number].wait()
        for row in range(NV):
            slab[number, pl.ds(row * cells, cells), pl.ds(0, NV)] = flat[
                number, :, pl.ds(row * NV, NV)
            ].astype(F32)

    no_rows = jnp.zeros((LANES - ROWS, LANES), BF16)
    together = 4

    def multiply_blocks(group, _):
        for member in range(together):
            i = group * together + member
            p, u, l = (
                slab[number, pl.ds(i, ROWS, stride=cells), :] for number in range(3)
            )
            p16 = p.astype(BF16)
            pivot[i] = jnp.concatenate([p16, no_rows], axis=0)
            right = jnp.concatenate([(-u).astype(BF16), (-l).astype(BF16)], axis=1)
            right = jnp.concatenate([right, tail], axis=0)
            both = dot(p16, right)
            put(tn, i, both[:, :LANES])
            put(tb, i, both[:, LANES:])
        return 0

    lax.fori_loop(0, cells // together, multiply_blocks, 0)

    def join(place):
        forward = multiply(left_of((tn, 2 * place)), right_of((tn, 2 * place + 1)))
        backward = multiply(left_of((tb, 2 * place + 1)), right_of((tb, 2 * place)))
        return forward, backward

    def join_group(group, _):
        for member in range(together):
            place = group * together + member
            forward, backward = join(place)
            put(tn, cells + place, forward)
            put(tb, cells + place, backward)
        return 0

    last = cells - 2
    lax.fori_loop(0, 2, join_group, 0)
    for place in range(2 * together, last):
        forward, backward = join(place)
        put(tn, cells + place, forward)
        put(tb, cells + place, backward)
    forward, backward = join(last)
    maps[0] = packed(forward)
    maps[1] = packed(backward)

    pl.semaphore_wait(barrier, n - 1 + 2)

    def map_copy(which, slot, target):
        return pltpu.make_async_remote_copy(
            src_ref=maps.at[which],
            dst_ref=came.at[slot],
            send_sem=map_out.at[slot],
            recv_sem=map_in.at[slot],
            device_id={"narrow": target},
            device_id_type=MESH,
        )

    def send_maps(step, _):
        @pl.when((me >= 1) & (me + step < n))
        def _():
            map_copy(0, step, me + step).start()

        @pl.when((me <= n - 2) & (me - step >= 0))
        def _():
            map_copy(1, n - step, me - step).start()

        return 0

    lax.fori_loop(1, n, send_maps, 0)
    whole = cells + last
    put(tn, whole, forward)
    put(tb, whole, backward)

    def offset_copy(source, target_ref, turn, slot, out, arrived, target):
        return pltpu.make_async_remote_copy(
            src_ref=source.at[turn],
            dst_ref=target_ref.at[turn, slot],
            send_sem=out.at[turn, slot],
            recv_sem=arrived.at[turn, slot],
            device_id={"narrow": target},
            device_id_type=MESH,
        )

    def f_copy(turn, slot, target):
        return offset_copy(fsend, fcame, turn, slot, f_out, f_in, target)

    def g_copy(turn, slot, target):
        return offset_copy(gsend, gcame, turn, slot, g_out, g_in, target)

    def send_f(turn):
        for step in far_first(n):

            @pl.when(me + step < n)
            def _():
                f_copy(turn, step, me + step).start()

    def send_g(turn):
        for step in far_first(n):

            @pl.when(me - step >= 0)
            def _():
                g_copy(turn, n - step, me - step).start()

    def wait_f(turn):
        for step in range(1, n):

            @pl.when(step <= me)
            def _():
                f_copy(turn, step, me).wait_recv()

    def wait_g(turn):
        for step in range(1, n):

            @pl.when(me + step < n)
            def _():
                g_copy(turn, n - step, me).wait_recv()

    def deep(vectors, weights):
        left = jnp.concatenate([stacked_vector(v) for v in vectors], axis=1)
        right = jnp.concatenate([ref[index] for ref, index in weights], axis=0)
        return folded(dot(left, right))

    def by(vector, place):
        ref, index = place
        return folded(dot(stacked_vector(vector), ref[index]))

    def forward_node(size, first):
        return tn, node(size, cells, first)

    def backward_node(size, first):
        return tb, node(size, cells, cells - first - size)

    def climb(source, at, whole):
        sums, source = {}, list(source)
        for p in range(0, cells, 2):
            source[p + 1] = source[p + 1] + by(source[p], at(1, p))
        for p in range(0, cells, 2):
            sums[2, p] = by(source[p + 1], at(1, p + 1))
        size = 2
        while size < cells // 2 or (whole and size < cells):
            for p in range(0, cells, 2 * size):
                sums[2 * size, p] = sums[size, p + size] + by(sums[size, p], at(size, p + size))
            size *= 2
        return source, sums

    def descend(source, sums, at):
        entering = {0: None}
        size = cells // 2
        while size >= 2:
            for p in range(0, cells, 2 * size):
                after = sums[size, p]
                if entering[p] is not None:
                    after = after + by(entering[p], at(size, p))
                entering[p + size] = after
            size //= 2
        values = list(source)
        for p in range(0, cells, 2):
            if entering[p] is not None:
                values[p] = values[p] + entering[p]
                values[p + 1] = values[p + 1] + by(entering[p], at(1, p))
        return values

    row = lax.broadcasted_iota(jnp.int32, (ROWS, LANES), 0)
    column = lax.broadcasted_iota(jnp.int32, (ROWS, LANES), 1)
    unit = jnp.where((row == column) & (row < NV), 1.0, 0.0).astype(F32)
    put(kw, 0, unit)
    put(jw, cells - 1, unit)
    ew[0] = tb[0]
    hsum[...] = jnp.zeros_like(hsum)
    came[0] = jnp.zeros_like(came[0])

    @pl.when(me >= 1)
    def _():
        put(phi, 1, unit)

    @pl.when(me <= n - 2)
    def _():
        put(phi, n - 1, unit)

    def start(turn):
        source, sums = climb([src[i] for i in range(cells)], forward_node, True)
        leaving = sums[cells, 0]
        fsend[turn] = leaving
        send_f(turn)
        for i, value in enumerate(descend(source, sums, forward_node)):
            zs[i] = value
        return leaving

    loads[3].wait()
    blocks = load_cells(rhs_ref, pad)
    for i in range(cells):
        src[i] = blocks[i * NR : (i + 1) * NR]
    start(0)

    from_before = jnp.maximum(me - 1, 0)
    from_after = jnp.maximum(n - 2 - me, 0)

    def with_pivot(i):
        exact = pivot[i]
        put(jp, i, dot(left_of((jw, i)), jnp.concatenate([exact, exact], axis=0)))

    def tables(step, _):
        before = step <= from_before
        after = step - from_before
        arrived = before | (after <= from_after)
        slot = jnp.where(before, step, jnp.where(arrived, n - after, 0))
        towards = jnp.where(before, step + 1, jnp.where(arrived, n - after - 1, n))

        @pl.when(arrived)
        def _():
            map_copy(0, slot, me).wait_recv()

        high, low = parts(unpacked(came[slot]))
        chained = multiply(jnp.concatenate([high, low], axis=1), right_of((phi, slot)))
        back = cells - 1 - step
        k = multiply(left_of((kw, step - 1)), right_of((tn, step - 1)))
        e = multiply(left_of((tb, step)), right_of((ew, step - 1)))
        j = multiply(left_of((jw, back + 1)), right_of((tb, back + 1)))
        h = multiply(left_of((kw, step - 1)), right_of((ew, step - 1)))
        with_pivot(back + 1)
        put(phi, towards, chained)
        put(kw, step, k)
        put(ew, step, e)
        put(jw, back, j)
        hsum[...] += h
        return 0

    lax.fori_loop(1, cells, tables, 0)
    with_pivot(0)
    put(hw, 0, hsum[...] + multiply(left_of((kw, cells - 1)), right_of((ew, cells - 1))))

    between = [(phi, k) for k in range(n)]

    def answer_copy(slot, target):
        return pltpu.make_async_remote_copy(
            src_ref=answers.at[slot],
            dst_ref=answered.at[slot],
            send_sem=answer_out.at[slot],
            recv_sem=answer_in.at[slot],
            device_id={"narrow": target},
            device_id_type=MESH,
        )

    def send_answers():
        high_low = jnp.concatenate([left_of((phi, k)) for k in range(1, n)], axis=0)
        products = multiply(high_low, right_of((hw, 0)))
        for k in range(1, n):
            answers[n - k] = packed(products[(k - 1) * ROWS : k * ROWS])

        def send(step, _):
            answer_copy(n - step, me - step).start()
            return 0

        lax.fori_loop(1, me + 1, send, 0)

    def take_answers():
        def wait(step, _):
            answer_copy(n - step, me).wait_recv()
            return 0

        lax.fori_loop(1, n - me, wait, 0)
        left = []
        for k in range(1, n):
            high, low = parts(unpacked(answered[k]))
            left += [high, low]
        put(
            rho,
            0,
            multiply(
                jnp.concatenate(left, axis=1),
                jnp.concatenate([right_of((phi, k)) for k in range(1, n)], axis=0),
            ),
        )
        put(rho, 1, multiply(left_of((rho, 0)), right_of((tb, whole))))
        put(rho, 2, multiply(left_of((tn, whole)), right_of((rho, 0))))

    def inside(turn, left):
        z = [zs[i] + folded(dot(left, kw[i])) for i in range(cells)]
        source, sums = climb(z[::-1], backward_node, False)
        for p, u in enumerate(descend(source, sums, backward_node)):
            i = cells - 1 - p
            product = dot(stacked_vector(u), pivot[i])
            xs[turn, i] = product[:NR] + product[NR:]

    def complete(turn, entering):
        left = stacked_vector(entering)
        for i in range(cells):
            xs[turn, i] = xs[turn, i] + folded(dot(left, jp[i]))

    def backward_alone():
        return deep([zs[i] for i in range(cells)], [(ew, i) for i in range(cells)])

    alone = backward_alone()
    wait_f(0)
    left = stacked_vector(deep([fcame[0, k] for k in range(n)], between))
    gsend[0] = alone + folded(dot(left, hw[0]))
    send_g(0)
    send_answers()
    inside(0, left)
    wait_g(0)
    complete(0, deep([gcame[0, k] for k in range(n)], between))

    def halo_copy(side, other):
        return pltpu.make_async_remote_copy(
            src_ref=xs.at[0],
            dst_ref=halo.at[side],
            send_sem=halo_out.at[side],
            recv_sem=halo_in.at[side],
            device_id={"wide": other},
            device_id_type=MESH,
        )

    halo_copy(0, high_line).start()
    halo_copy(1, low_line).start()

    store_cells(xs[0].reshape(cells * NR, LANES), first_ref)

    loads[4].wait()
    weights = []
    for place in range(3):
        total = jnp.zeros((cells, NV), F32)
        for side in range(2):
            relative = lax.rem(face_ref[0, side] - line + 1 + lines, lines)
            total = total + jnp.where(
                relative == place, coef_ref[:, pl.ds(side * NV, NV)], 0.0
            )
        weights.append(jnp.concatenate([total, jnp.zeros((cells, LANES - NV), F32)], axis=1))

    def drain(step, _):
        @pl.when(me + step < n)
        def _():
            f_copy(0, step, me + step).wait_send()

        @pl.when(me - step >= 0)
        def _():
            g_copy(0, n - step, me - step).wait_send()

        @pl.when((me >= 1) & (me + step < n))
        def _():
            map_copy(0, step, me + step).wait_send()

        @pl.when((me <= n - 2) & (me - step >= 0))
        def _():
            map_copy(1, n - step, me - step).wait_send()

        return 0

    lax.fori_loop(1, n, drain, 0)
    take_answers()

    halo_copy(0, high_line).wait_recv()
    halo_copy(1, low_line).wait_recv()

    for i in range(cells):
        coupled = (
            weights[0][i : i + 1] * halo[0, i]
            + weights[1][i : i + 1] * xs[0, i]
            + weights[2][i : i + 1] * halo[1, i]
        )
        src[i] = src[i] - coupled

    leaving = start(1)
    gsend[1] = backward_alone() + by(leaving, (rho, 1))
    send_g(1)
    wait_f(1)
    left = stacked_vector(deep([fcame[1, k] for k in range(n)], between))
    inside(1, left)
    back = by(leaving, (rho, 0)) + folded(dot(left, rho[2]))
    halo_copy(0, high_line).wait_send()
    halo_copy(1, low_line).wait_send()

    def drain_last(step, _):
        @pl.when(me + step < n)
        def _():
            f_copy(1, step, me + step).wait_send()

        @pl.when(me - step >= 0)
        def _():
            g_copy(1, n - step, me - step).wait_send()
            answer_copy(n - step, me - step).wait_send()

        return 0

    lax.fori_loop(1, n, drain_last, 0)
    wait_g(1)
    complete(1, back + deep([gcame[1, k] for k in range(n)], between))
    store_cells(xs[1].reshape(cells * NR, LANES), second_ref)


def body(n, lines, rhs, pivot, upper, lower, neighbors, coupling):
    cells = rhs.shape[1]
    matrix = (LANES, 2 * LANES)
    tree = pltpu.VMEM((2 * cells - 1, *matrix), BF16)
    weight = pltpu.VMEM((cells, *matrix), BF16)
    vectors = pltpu.VMEM((cells, NR, LANES), F32)
    vmem = pl.BlockSpec(memory_space=pltpu.VMEM)
    hbm = pl.BlockSpec(memory_space=pltpu.HBM)
    dma = pltpu.SemaphoreType.DMA

    def in_hbm(x):
        return pltpu.with_memory_space_constraint(x, pltpu.HBM)

    first, second = pl.pallas_call(
        functools.partial(kernel, n, lines),
        out_shape=[pltpu.VMEM((cells, NV * NR), F32)] * 2,
        in_specs=[hbm] * 4 + [pl.BlockSpec(memory_space=pltpu.SMEM), hbm],
        out_specs=[vmem] * 2,
        scratch_shapes=[
            pltpu.VMEM((3, cells, NV * NV), BF16),
            pltpu.VMEM((cells, NV * NR), F32),
            pltpu.VMEM((cells, 2 * NV), F32),
            pltpu.VMEM((3, ROWS * cells, LANES), F32),
            pltpu.VMEM((LANES, LANES), F32),
            pltpu.VMEM((cells, LANES, LANES), BF16),
            tree,
            tree,
            weight,
            weight,
            weight,
            weight,
            pltpu.VMEM((1, *matrix), BF16),
            pltpu.VMEM((ROWS, LANES), F32),
            pltpu.VMEM((3, *matrix), BF16),
            pltpu.VMEM((2, PACKED, LANES), F32),
            pltpu.VMEM((n, PACKED, LANES), F32),
            pltpu.VMEM((n, PACKED, LANES), F32),
            pltpu.VMEM((n, PACKED, LANES), F32),
            pltpu.VMEM((n + 1, *matrix), BF16),
            vectors,
            vectors,
            pltpu.VMEM((2, cells, NR, LANES), F32),
            pltpu.VMEM((2, cells, NR, LANES), F32),
            pltpu.VMEM((2, NR, LANES), F32),
            pltpu.VMEM((2, NR, LANES), F32),
            pltpu.VMEM((2, n, NR, LANES), F32),
            pltpu.VMEM((2, n, NR, LANES), F32),
            dma((5,)),
            dma((n,)),
            dma((n,)),
            dma((n,)),
            dma((n,)),
            dma((2, n)),
            dma((2, n)),
            dma((2, n)),
            dma((2, n)),
            dma((2,)),
            dma((2,)),
        ],
        compiler_params=pltpu.CompilerParams(
            collective_id=0, has_side_effects=True, vmem_limit_bytes=40 * 1024 * 1024
        ),
    )(*(in_hbm(x) for x in (pivot[0], upper[0], lower[0], rhs[0], neighbors, coupling[0])))
    return first[None], second[None]


def solution(mesh):
    blocks = P("wide", "narrow", None)
    return jax.shard_map(
        functools.partial(body, mesh.shape["narrow"], mesh.shape["wide"]),
        mesh=mesh,
        in_specs=(blocks, blocks, blocks, blocks, P("wide", None), blocks),
        out_specs=(blocks, blocks),
        check_vma=False,
    )
```

```python
import functools

import jax
import jax.numpy as jnp
from jax import lax
from jax.experimental import pallas as pl
from jax.experimental.pallas import tpu as pltpu
from jax.sharding import PartitionSpec as P

NV = 95
NR = 8
ROWS = 96
PACKED = 72
LANES = 128
F32 = jnp.float32
BF16 = jnp.bfloat16
MESH = pl.DeviceIdType.MESH


def dot(left, right):
    return jnp.dot(left, right, preferred_element_type=F32)


def parts(value):
    high = value.astype(BF16)
    return high, (value - high.astype(F32)).astype(BF16)


def stacked_vector(value):
    high = value.astype(BF16).astype(F32)
    return jnp.concatenate([high, value - high], axis=0).astype(BF16)


def folded(product):
    rows = product.shape[0] // 2
    return product[:rows, :LANES] + (product[:rows, LANES:] + product[rows:, :LANES])


def put(ref, index, value):
    high, low = parts(value)
    ref[index, pl.ds(0, ROWS), pl.ds(0, LANES)] = high
    ref[index, pl.ds(0, ROWS), pl.ds(LANES, LANES)] = low


def left_of(place):
    ref, index = place
    return ref[index, pl.ds(0, ROWS), :]


def right_of(place):
    ref, index = place
    value = ref[index]
    return jnp.concatenate([value, value], axis=0)


def multiply(left, right):
    product = dot(left, right)
    return product[:, :LANES] + product[:, LANES:]


def packed(value):
    top, rest = value[:PACKED], value[PACKED:]
    lane = lax.broadcasted_iota(jnp.int32, rest.shape, 1)
    pieces = []
    for part in range(3):
        moved = pltpu.roll(rest, (ROWS - 32 * part) % LANES, 1)
        pieces.append(jnp.where(lane >= ROWS, moved, top[24 * part : 24 * part + 24]))
    return jnp.concatenate(pieces, axis=0)


def unpacked(value):
    lane = lax.broadcasted_iota(jnp.int32, (24, LANES), 1)
    rest = jnp.zeros((24, LANES), F32)
    pieces = []
    for part in range(3):
        own = value[24 * part : 24 * part + 24]
        moved = pltpu.roll(own, (LANES - ROWS + 32 * part) % LANES, 1)
        rest = jnp.where((lane >= 32 * part) & (lane < 32 * part + 32), moved, rest)
        pieces.append(jnp.where(lane < ROWS, own, 0.0))
    return jnp.concatenate(pieces + [rest], axis=0)


def granule_transpose(value):
    row = lax.broadcasted_iota(jnp.int32, value.shape, 0)
    group = lax.broadcasted_iota(jnp.int32, value.shape, 1) // NR
    height = value.shape[0]
    for bit in (1, 2, 4, 8):
        row_set = (row & bit) != 0
        group_set = (group & bit) != 0
        down = pltpu.roll(pltpu.roll(value, bit, 0), LANES - NR * bit, 1)
        up = pltpu.roll(pltpu.roll(value, height - bit, 0), NR * bit, 1)
        value = jnp.where(row_set == group_set, value, jnp.where(row_set, down, up))
    return value


def load_cells(flat_ref, pad_ref):
    cells = flat_ref.shape[0]
    width = NV * NR
    pad_ref[...] = jnp.zeros_like(pad_ref)
    for block in range(ROWS // 16):
        first = block * LANES
        wide = min(LANES, width - first)
        pad_ref[pl.ds(block * 16, cells), pl.ds(0, wide)] = flat_ref[:, pl.ds(first, wide)]
    turned = granule_transpose(pad_ref[pl.ds(0, ROWS), :])
    pad_ref[pl.ds(0, ROWS), :] = turned
    return jnp.transpose(pad_ref[...])


def store_cells(blocks, flat_ref):
    width = NV * NR
    cells = flat_ref.shape[0]
    turned = granule_transpose(jnp.transpose(blocks)[:ROWS])
    for block in range(ROWS // 16):
        first = block * LANES
        wide = min(LANES, width - first)
        flat_ref[:, pl.ds(first, wide)] = turned[block * 16 : block * 16 + cells, :wide]


def mixed_near_first(n):
    early = {4: 1.5, 8: 4.5, 12: 8.5}
    return sorted(range(1, n), key=lambda step: early.get(step, step))


def far_first(n):
    return sorted(range(1, n), key=lambda step: -sum(min(d, 4 - d) for d in (step % 4, step // 4 % 4)))


def low_bit(m):
    return m & -m


def node(level_size, cells, first):
    return 2 * cells - 2 * cells // level_size + first // level_size


def kernel(
    n,
    lines,
    pivot_hbm,
    upper_hbm,
    lower_hbm,
    rhs_hbm,
    face_ref,
    coef_hbm,
    first_ref,
    second_ref,
    flat,
    rhs_ref,
    coef_ref,
    slab,
    pad,
    pivot,
    tn,
    tb,
    ew,
    kw,
    jw,
    jp,
    hw,
    hsum,
    rho,
    maps,
    came,
    answers,
    answered,
    phi,
    src,
    zs,
    xs,
    halo,
    fsend,
    gsend,
    fcame,
    gcame,
    load_sem,
    map_out,
    map_in,
    answer_out,
    answer_in,
    f_out,
    f_in,
    g_out,
    g_in,
    halo_out,
    halo_in,
):
    cells = rhs_ref.shape[0]
    me = lax.axis_index("narrow")
    line = lax.axis_index("wide")
    low_line = lax.rem(line + lines - 1, lines)
    high_line = lax.rem(line + 1, lines)

    loads = [
        pltpu.make_async_copy(hbm, flat.at[number], load_sem.at[number])
        for number, hbm in enumerate((pivot_hbm, upper_hbm, lower_hbm))
    ]
    loads.append(pltpu.make_async_copy(rhs_hbm, rhs_ref, load_sem.at[3]))
    loads.append(pltpu.make_async_copy(coef_hbm, coef_ref, load_sem.at[4]))
    for load in loads:
        load.start()

    fcame[...] = jnp.zeros_like(fcame)
    gcame[...] = jnp.zeros_like(gcame)
    answered[...] = jnp.zeros_like(answered)

    barrier = pltpu.get_barrier_semaphore()

    def greet(step, _):
        pl.semaphore_signal(
            barrier, inc=1, device_id={"narrow": lax.rem(me + step, n)}, device_id_type=MESH
        )
        return 0

    lax.fori_loop(1, n, greet, 0)
    for other in (low_line, high_line):
        pl.semaphore_signal(barrier, inc=1, device_id={"wide": other}, device_id_type=MESH)

    slab[...] = jnp.zeros_like(slab)
    tail = jnp.zeros((LANES - ROWS, 2 * LANES), BF16)

    def clear_nodes(i, _):
        for ref in (tn, tb):
            ref[i, pl.ds(ROWS, LANES - ROWS), :] = tail
        return 0

    lax.fori_loop(0, 2 * cells - 1, clear_nodes, 0)

    def clear(i, _):
        for ref in (ew, kw, jw, jp):
            ref[i, pl.ds(ROWS, LANES - ROWS), :] = tail
        return 0

    lax.fori_loop(0, cells, clear, 0)
    hw[0, pl.ds(ROWS, LANES - ROWS), :] = tail
    for i in range(3):
        rho[i, pl.ds(ROWS, LANES - ROWS), :] = tail

    def clear_phi(i, _):
        phi[i] = jnp.zeros((LANES, 2 * LANES), BF16)
        return 0

    lax.fori_loop(0, n, clear_phi, 0)

    for number in range(3):
        loads[number].wait()
        for row in range(NV):
            slab[number, pl.ds(row * (cells + 1), cells), pl.ds(0, NV)] = flat[
                number, :, pl.ds(row * NV, NV)
            ].astype(F32)

    no_rows = jnp.zeros((LANES - ROWS, LANES), BF16)

    for i in range(cells):
        p, u, l = (
            slab[number, pl.ds(i, ROWS, stride=cells + 1), :] for number in range(3)
        )
        p16 = p.astype(BF16)
        pivot[i] = jnp.concatenate([p16, no_rows], axis=0)
        right = jnp.concatenate([(-u).astype(BF16), (-l).astype(BF16)], axis=1)
        right = jnp.concatenate([right, tail], axis=0)
        both = dot(p16, right)
        put(tn, i, both[:, :LANES])
        put(tb, i, both[:, LANES:])

    def join(place):
        forward = multiply(left_of((tn, 2 * place)), right_of((tn, 2 * place + 1)))
        backward = multiply(left_of((tb, 2 * place + 1)), right_of((tb, 2 * place)))
        return forward, backward

    last = cells - 2
    for place in range(last):
        forward, backward = join(place)
        put(tn, cells + place, forward)
        put(tb, cells + place, backward)
    forward, backward = join(last)
    maps[0] = packed(forward)
    maps[1] = packed(backward)

    pl.semaphore_wait(barrier, n - 1 + 2)

    def map_copy(which, slot, target):
        return pltpu.make_async_remote_copy(
            src_ref=maps.at[which],
            dst_ref=came.at[slot],
            send_sem=map_out.at[slot],
            recv_sem=map_in.at[slot],
            device_id={"narrow": target},
            device_id_type=MESH,
        )

    for step in mixed_near_first(n):

        @pl.when((me >= 1) & (me + step < n))
        def _():
            map_copy(0, step, me + step).start()

        @pl.when((me <= n - 2) & (me - step >= 0))
        def _():
            map_copy(1, n - step, me - step).start()

    whole = cells + last
    put(tn, whole, forward)
    put(tb, whole, backward)

    def offset_copy(source, target_ref, turn, slot, out, arrived, target):
        return pltpu.make_async_remote_copy(
            src_ref=source.at[turn],
            dst_ref=target_ref.at[turn, slot],
            send_sem=out.at[turn, slot],
            recv_sem=arrived.at[turn, slot],
            device_id={"narrow": target},
            device_id_type=MESH,
        )

    def f_copy(turn, slot, target):
        return offset_copy(fsend, fcame, turn, slot, f_out, f_in, target)

    def g_copy(turn, slot, target):
        return offset_copy(gsend, gcame, turn, slot, g_out, g_in, target)

    def send_f(turn):
        for step in far_first(n):

            @pl.when(me + step < n)
            def _():
                f_copy(turn, step, me + step).start()

    def send_g(turn):
        for step in far_first(n):

            @pl.when(me - step >= 0)
            def _():
                g_copy(turn, n - step, me - step).start()

    def wait_f(turn):
        for step in range(1, n):

            @pl.when(step <= me)
            def _():
                f_copy(turn, step, me).wait_recv()

    def wait_g(turn):
        for step in range(1, n):

            @pl.when(me + step < n)
            def _():
                g_copy(turn, n - step, me).wait_recv()

    def deep(vectors, weights):
        left = jnp.concatenate([stacked_vector(v) for v in vectors], axis=1)
        right = jnp.concatenate([ref[index] for ref, index in weights], axis=0)
        return folded(dot(left, right))

    def by(vector, place):
        ref, index = place
        return folded(dot(stacked_vector(vector), ref[index]))

    def forward_node(size, first):
        return tn, node(size, cells, first)

    def backward_node(size, first):
        return tb, node(size, cells, cells - first - size)

    def climb(source, at, whole):
        sums, source = {}, list(source)
        for p in range(0, cells, 2):
            source[p + 1] = source[p + 1] + by(source[p], at(1, p))
        for p in range(0, cells, 2):
            sums[2, p] = by(source[p + 1], at(1, p + 1))
        size = 2
        while size < cells // 2 or (whole and size < cells):
            for p in range(0, cells, 2 * size):
                sums[2 * size, p] = sums[size, p + size] + by(sums[size, p], at(size, p + size))
            size *= 2
        return source, sums

    def descend(source, sums, at):
        entering = {0: None}
        size = cells // 2
        while size >= 2:
            for p in range(0, cells, 2 * size):
                after = sums[size, p]
                if entering[p] is not None:
                    after = after + by(entering[p], at(size, p))
                entering[p + size] = after
            size //= 2
        values = list(source)
        for p in range(0, cells, 2):
            if entering[p] is not None:
                values[p] = values[p] + entering[p]
                values[p + 1] = values[p + 1] + by(entering[p], at(1, p))
        return values

    row = lax.broadcasted_iota(jnp.int32, (ROWS, LANES), 0)
    column = lax.broadcasted_iota(jnp.int32, (ROWS, LANES), 1)
    unit = jnp.where((row == column) & (row < NV), 1.0, 0.0).astype(F32)
    put(kw, 0, unit)
    put(jw, cells - 1, unit)
    ew[0] = tb[0]
    hsum[...] = jnp.zeros_like(hsum)
    came[0] = jnp.zeros_like(came[0])

    @pl.when(me >= 1)
    def _():
        put(phi, 1, unit)

    @pl.when(me <= n - 2)
    def _():
        put(phi, n - 1, unit)

    def start(turn):
        source, sums = climb([src[i] for i in range(cells)], forward_node, True)
        leaving = sums[cells, 0]
        fsend[turn] = leaving
        send_f(turn)
        for i, value in enumerate(descend(source, sums, forward_node)):
            zs[i] = value
        return leaving

    loads[3].wait()
    blocks = load_cells(rhs_ref, pad)
    for i in range(cells):
        src[i] = blocks[i * NR : (i + 1) * NR]
    start(0)

    from_before = jnp.maximum(me - 1, 0)
    from_after = jnp.maximum(n - 2 - me, 0)

    def with_pivot(i):
        exact = pivot[i]
        put(jp, i, dot(left_of((jw, i)), jnp.concatenate([exact, exact], axis=0)))

    def tables(step, _):
        before = step <= from_before
        after = step - from_before
        arrived = before | (after <= from_after)
        slot = jnp.where(before, step, jnp.where(arrived, n - after, 0))
        towards = jnp.where(before, step + 1, jnp.where(arrived, n - after - 1, n))

        @pl.when(arrived)
        def _():
            map_copy(0, slot, me).wait_recv()

        high, low = parts(unpacked(came[slot]))
        chained = multiply(jnp.concatenate([high, low], axis=1), right_of((phi, slot)))
        back = cells - 1 - step
        k = multiply(left_of((kw, step - 1)), right_of((tn, step - 1)))
        e = multiply(left_of((tb, step)), right_of((ew, step - 1)))
        j = multiply(left_of((jw, back + 1)), right_of((tb, back + 1)))
        h = multiply(left_of((kw, step - 1)), right_of((ew, step - 1)))
        with_pivot(back + 1)
        put(phi, towards, chained)
        put(kw, step, k)
        put(ew, step, e)
        put(jw, back, j)
        hsum[...] += h
        return 0

    lax.fori_loop(1, cells, tables, 0)
    with_pivot(0)
    put(hw, 0, hsum[...] + multiply(left_of((kw, cells - 1)), right_of((ew, cells - 1))))

    between = [(phi, k) for k in range(n)]

    def answer_copy(slot, target):
        return pltpu.make_async_remote_copy(
            src_ref=answers.at[slot],
            dst_ref=answered.at[slot],
            send_sem=answer_out.at[slot],
            recv_sem=answer_in.at[slot],
            device_id={"narrow": target},
            device_id_type=MESH,
        )

    def send_answers():
        high_low = jnp.concatenate([left_of((phi, k)) for k in range(1, n)], axis=0)
        products = multiply(high_low, right_of((hw, 0)))
        for k in range(1, n):
            answers[n - k] = packed(products[(k - 1) * ROWS : k * ROWS])

        def send(step, _):
            answer_copy(n - step, me - step).start()
            return 0

        lax.fori_loop(1, me + 1, send, 0)

    def take_answers():
        def wait(step, _):
            answer_copy(n - step, me).wait_recv()
            return 0

        lax.fori_loop(1, n - me, wait, 0)
        left = []
        for k in range(1, n):
            high, low = parts(unpacked(answered[k]))
            left += [high, low]
        put(
            rho,
            0,
            multiply(
                jnp.concatenate(left, axis=1),
                jnp.concatenate([right_of((phi, k)) for k in range(1, n)], axis=0),
            ),
        )
        put(rho, 1, multiply(left_of((rho, 0)), right_of((tb, whole))))
        put(rho, 2, multiply(left_of((tn, whole)), right_of((rho, 0))))

    def inside(turn, left):
        z = [zs[i] + folded(dot(left, kw[i])) for i in range(cells)]
        source, sums = climb(z[::-1], backward_node, False)
        for p, u in enumerate(descend(source, sums, backward_node)):
            i = cells - 1 - p
            product = dot(stacked_vector(u), pivot[i])
            xs[turn, i] = product[:NR] + product[NR:]

    def complete(turn, entering):
        left = stacked_vector(entering)
        for i in range(cells):
            xs[turn, i] = xs[turn, i] + folded(dot(left, jp[i]))

    def backward_alone():
        return deep([zs[i] for i in range(cells)], [(ew, i) for i in range(cells)])

    alone = backward_alone()
    wait_f(0)
    left = stacked_vector(deep([fcame[0, k] for k in range(n)], between))
    gsend[0] = alone + folded(dot(left, hw[0]))
    send_g(0)
    send_answers()
    inside(0, left)
    wait_g(0)
    complete(0, deep([gcame[0, k] for k in range(n)], between))

    def halo_copy(side, other):
        return pltpu.make_async_remote_copy(
            src_ref=xs.at[0],
            dst_ref=halo.at[side],
            send_sem=halo_out.at[side],
            recv_sem=halo_in.at[side],
            device_id={"wide": other},
            device_id_type=MESH,
        )

    halo_copy(0, high_line).start()
    halo_copy(1, low_line).start()

    store_cells(xs[0].reshape(cells * NR, LANES), first_ref)

    loads[4].wait()
    weights = []
    for place in range(3):
        total = jnp.zeros((cells, NV), F32)
        for side in range(2):
            relative = lax.rem(face_ref[0, side] - line + 1 + lines, lines)
            total = total + jnp.where(
                relative == place, coef_ref[:, pl.ds(side * NV, NV)], 0.0
            )
        weights.append(jnp.concatenate([total, jnp.zeros((cells, LANES - NV), F32)], axis=1))

    def drain(step, _):
        @pl.when(me + step < n)
        def _():
            f_copy(0, step, me + step).wait_send()

        @pl.when(me - step >= 0)
        def _():
            g_copy(0, n - step, me - step).wait_send()

        @pl.when((me >= 1) & (me + step < n))
        def _():
            map_copy(0, step, me + step).wait_send()

        @pl.when((me <= n - 2) & (me - step >= 0))
        def _():
            map_copy(1, n - step, me - step).wait_send()

        return 0

    lax.fori_loop(1, n, drain, 0)
    take_answers()

    halo_copy(0, high_line).wait_recv()
    halo_copy(1, low_line).wait_recv()

    for i in range(cells):
        coupled = (
            weights[0][i : i + 1] * halo[0, i]
            + weights[1][i : i + 1] * xs[0, i]
            + weights[2][i : i + 1] * halo[1, i]
        )
        src[i] = src[i] - coupled

    leaving = start(1)
    gsend[1] = backward_alone() + by(leaving, (rho, 1))
    send_g(1)
    wait_f(1)
    left = stacked_vector(deep([fcame[1, k] for k in range(n)], between))
    inside(1, left)
    back = by(leaving, (rho, 0)) + folded(dot(left, rho[2]))
    halo_copy(0, high_line).wait_send()
    halo_copy(1, low_line).wait_send()

    def drain_last(step, _):
        @pl.when(me + step < n)
        def _():
            f_copy(1, step, me + step).wait_send()

        @pl.when(me - step >= 0)
        def _():
            g_copy(1, n - step, me - step).wait_send()
            answer_copy(n - step, me - step).wait_send()

        return 0

    lax.fori_loop(1, n, drain_last, 0)
    wait_g(1)
    complete(1, back + deep([gcame[1, k] for k in range(n)], between))
    store_cells(xs[1].reshape(cells * NR, LANES), second_ref)


def body(n, lines, rhs, pivot, upper, lower, neighbors, coupling):
    cells = rhs.shape[1]
    matrix = (LANES, 2 * LANES)
    tree = pltpu.VMEM((2 * cells - 1, *matrix), BF16)
    weight = pltpu.VMEM((cells, *matrix), BF16)
    vectors = pltpu.VMEM((cells, NR, LANES), F32)
    vmem = pl.BlockSpec(memory_space=pltpu.VMEM)
    hbm = pl.BlockSpec(memory_space=pltpu.HBM)
    dma = pltpu.SemaphoreType.DMA

    def in_hbm(x):
        return pltpu.with_memory_space_constraint(x, pltpu.HBM)

    first, second = pl.pallas_call(
        functools.partial(kernel, n, lines),
        out_shape=[pltpu.VMEM((cells, NV * NR), F32)] * 2,
        in_specs=[hbm] * 4 + [pl.BlockSpec(memory_space=pltpu.SMEM), hbm],
        out_specs=[vmem] * 2,
        scratch_shapes=[
            pltpu.VMEM((3, cells, NV * NV), BF16),
            pltpu.VMEM((cells, NV * NR), F32),
            pltpu.VMEM((cells, 2 * NV), F32),
            pltpu.VMEM((3, ROWS * (cells + 1), LANES), F32),
            pltpu.VMEM((LANES, LANES), F32),
            pltpu.VMEM((cells, LANES, LANES), BF16),
            tree,
            tree,
            weight,
            weight,
            weight,
            weight,
            pltpu.VMEM((1, *matrix), BF16),
            pltpu.VMEM((ROWS, LANES), F32),
            pltpu.VMEM((3, *matrix), BF16),
            pltpu.VMEM((2, PACKED, LANES), F32),
            pltpu.VMEM((n, PACKED, LANES), F32),
            pltpu.VMEM((n, PACKED, LANES), F32),
            pltpu.VMEM((n, PACKED, LANES), F32),
            pltpu.VMEM((n + 1, *matrix), BF16),
            vectors,
            vectors,
            pltpu.VMEM((2, cells, NR, LANES), F32),
            pltpu.VMEM((2, cells, NR, LANES), F32),
            pltpu.VMEM((2, NR, LANES), F32),
            pltpu.VMEM((2, NR, LANES), F32),
            pltpu.VMEM((2, n, NR, LANES), F32),
            pltpu.VMEM((2, n, NR, LANES), F32),
            dma((5,)),
            dma((n,)),
            dma((n,)),
            dma((n,)),
            dma((n,)),
            dma((2, n)),
            dma((2, n)),
            dma((2, n)),
            dma((2, n)),
            dma((2,)),
            dma((2,)),
        ],
        compiler_params=pltpu.CompilerParams(
            collective_id=0, has_side_effects=True, vmem_limit_bytes=40 * 1024 * 1024
        ),
    )(*(in_hbm(x) for x in (pivot[0], upper[0], lower[0], rhs[0], neighbors, coupling[0])))
    return first[None], second[None]


def solution(mesh):
    blocks = P("wide", "narrow", None)
    return jax.shard_map(
        functools.partial(body, mesh.shape["narrow"], mesh.shape["wide"]),
        mesh=mesh,
        in_specs=(blocks, blocks, blocks, blocks, P("wide", None), blocks),
        out_specs=(blocks, blocks),
        check_vma=False,
    )
```

```python
import functools

import jax
import jax.numpy as jnp
from jax import lax
from jax.experimental import pallas as pl
from jax.experimental.pallas import tpu as pltpu
from jax.sharding import PartitionSpec as P

NV = 95
NR = 8
ROWS = 96
PACKED = 72
LANES = 128
F32 = jnp.float32
BF16 = jnp.bfloat16
MESH = pl.DeviceIdType.MESH


def dot(left, right):
    return jnp.dot(left, right, preferred_element_type=F32)


def parts(value):
    high = value.astype(BF16)
    return high, (value - high.astype(F32)).astype(BF16)


def stacked_vector(value):
    high = value.astype(BF16).astype(F32)
    return jnp.concatenate([high, value - high], axis=0).astype(BF16)


def folded(product):
    rows = product.shape[0] // 2
    return product[:rows, :LANES] + (product[:rows, LANES:] + product[rows:, :LANES])


def put(ref, index, value):
    high, low = parts(value)
    ref[index, pl.ds(0, ROWS), pl.ds(0, LANES)] = high
    ref[index, pl.ds(0, ROWS), pl.ds(LANES, LANES)] = low


def left_of(place):
    ref, index = place
    return ref[index, pl.ds(0, ROWS), :]


def right_of(place):
    ref, index = place
    value = ref[index]
    return jnp.concatenate([value, value], axis=0)


def multiply(left, right):
    product = dot(left, right)
    return product[:, :LANES] + product[:, LANES:]


def packed(value):
    top, rest = value[:PACKED], value[PACKED:]
    lane = lax.broadcasted_iota(jnp.int32, rest.shape, 1)
    pieces = []
    for part in range(3):
        moved = pltpu.roll(rest, (ROWS - 32 * part) % LANES, 1)
        pieces.append(jnp.where(lane >= ROWS, moved, top[24 * part : 24 * part + 24]))
    return jnp.concatenate(pieces, axis=0)


def unpacked(value):
    lane = lax.broadcasted_iota(jnp.int32, (24, LANES), 1)
    rest = jnp.zeros((24, LANES), F32)
    pieces = []
    for part in range(3):
        own = value[24 * part : 24 * part + 24]
        moved = pltpu.roll(own, (LANES - ROWS + 32 * part) % LANES, 1)
        rest = jnp.where((lane >= 32 * part) & (lane < 32 * part + 32), moved, rest)
        pieces.append(jnp.where(lane < ROWS, own, 0.0))
    return jnp.concatenate(pieces + [rest], axis=0)


def granule_transpose(value):
    row = lax.broadcasted_iota(jnp.int32, value.shape, 0)
    group = lax.broadcasted_iota(jnp.int32, value.shape, 1) // NR
    height = value.shape[0]
    for bit in (1, 2, 4, 8):
        row_set = (row & bit) != 0
        group_set = (group & bit) != 0
        down = pltpu.roll(pltpu.roll(value, bit, 0), LANES - NR * bit, 1)
        up = pltpu.roll(pltpu.roll(value, height - bit, 0), NR * bit, 1)
        value = jnp.where(row_set == group_set, value, jnp.where(row_set, down, up))
    return value


def load_cells(flat_ref, pad_ref):
    cells = flat_ref.shape[0]
    width = NV * NR
    pad_ref[...] = jnp.zeros_like(pad_ref)
    for block in range(ROWS // 16):
        first = block * LANES
        wide = min(LANES, width - first)
        pad_ref[pl.ds(block * 16, cells), pl.ds(0, wide)] = flat_ref[:, pl.ds(first, wide)]
    turned = granule_transpose(pad_ref[pl.ds(0, ROWS), :])
    pad_ref[pl.ds(0, ROWS), :] = turned
    return jnp.transpose(pad_ref[...])


def store_cells(blocks, flat_ref):
    width = NV * NR
    cells = flat_ref.shape[0]
    turned = granule_transpose(jnp.transpose(blocks)[:ROWS])
    for block in range(ROWS // 16):
        first = block * LANES
        wide = min(LANES, width - first)
        flat_ref[:, pl.ds(first, wide)] = turned[block * 16 : block * 16 + cells, :wide]


def mixed_near_first(n):
    early = {4: 1.5, 8: 4.5, 12: 8.5}
    return sorted(range(1, n), key=lambda step: early.get(step, step))


def far_first(n):
    return sorted(range(1, n), key=lambda step: -sum(min(d, 4 - d) for d in (step % 4, step // 4 % 4)))


def low_bit(m):
    return m & -m


def node(level_size, cells, first):
    return 2 * cells - 2 * cells // level_size + first // level_size


def kernel(
    n,
    lines,
    pivot_hbm,
    upper_hbm,
    lower_hbm,
    rhs_hbm,
    face_ref,
    coef_hbm,
    first_ref,
    second_ref,
    flat,
    rhs_ref,
    coef_ref,
    slab,
    pad,
    pivot,
    tn,
    tb,
    qw,
    ew,
    kw,
    jw,
    jp,
    hw,
    hsum,
    rho,
    maps,
    came,
    answers,
    answered,
    phi,
    src,
    zs,
    xs,
    halo,
    fsend,
    gsend,
    fcame,
    gcame,
    load_sem,
    map_out,
    map_in,
    answer_out,
    answer_in,
    f_out,
    f_in,
    g_out,
    g_in,
    halo_out,
    halo_in,
):
    cells = rhs_ref.shape[0]
    me = lax.axis_index("narrow")
    line = lax.axis_index("wide")
    low_line = lax.rem(line + lines - 1, lines)
    high_line = lax.rem(line + 1, lines)

    loads = [
        pltpu.make_async_copy(hbm, flat.at[number], load_sem.at[number])
        for number, hbm in enumerate((pivot_hbm, upper_hbm, lower_hbm))
    ]
    loads.append(pltpu.make_async_copy(rhs_hbm, rhs_ref, load_sem.at[3]))
    loads.append(pltpu.make_async_copy(coef_hbm, coef_ref, load_sem.at[4]))
    for load in loads:
        load.start()

    fcame[...] = jnp.zeros_like(fcame)
    gcame[...] = jnp.zeros_like(gcame)
    answered[...] = jnp.zeros_like(answered)

    barrier = pltpu.get_barrier_semaphore()

    def greet(step, _):
        pl.semaphore_signal(
            barrier, inc=1, device_id={"narrow": lax.rem(me + step, n)}, device_id_type=MESH
        )
        return 0

    lax.fori_loop(1, n, greet, 0)
    for other in (low_line, high_line):
        pl.semaphore_signal(barrier, inc=1, device_id={"wide": other}, device_id_type=MESH)

    slab[...] = jnp.zeros_like(slab)
    tail = jnp.zeros((LANES - ROWS, 2 * LANES), BF16)

    def clear_nodes(i, _):
        for ref in (tn, tb):
            ref[i, pl.ds(ROWS, LANES - ROWS), :] = tail
        return 0

    lax.fori_loop(0, 2 * cells - 1, clear_nodes, 0)

    def clear(i, _):
        for ref in (qw, ew, kw, jw, jp):
            ref[i, pl.ds(ROWS, LANES - ROWS), :] = tail
        return 0

    lax.fori_loop(0, cells, clear, 0)
    hw[0, pl.ds(ROWS, LANES - ROWS), :] = tail
    for i in range(3):
        rho[i, pl.ds(ROWS, LANES - ROWS), :] = tail

    def clear_phi(i, _):
        phi[i] = jnp.zeros((LANES, 2 * LANES), BF16)
        return 0

    lax.fori_loop(0, n, clear_phi, 0)

    for number in range(3):
        loads[number].wait()
        for row in range(NV):
            slab[number, pl.ds(row * (cells + 1), cells), pl.ds(0, NV)] = flat[
                number, :, pl.ds(row * NV, NV)
            ].astype(F32)

    no_rows = jnp.zeros((LANES - ROWS, LANES), BF16)

    for i in range(cells):
        p, u, l = (
            slab[number, pl.ds(i, ROWS, stride=cells + 1), :] for number in range(3)
        )
        p16 = p.astype(BF16)
        pivot[i] = jnp.concatenate([p16, no_rows], axis=0)
        right = jnp.concatenate([(-u).astype(BF16), (-l).astype(BF16)], axis=1)
        right = jnp.concatenate([right, tail], axis=0)
        both = dot(p16, right)
        put(tn, i, both[:, :LANES])
        put(tb, i, both[:, LANES:])

    last = cells - 2
    whole = cells + last
    for place in range(last):
        put(tn, cells + place, multiply(left_of((tn, 2 * place)), right_of((tn, 2 * place + 1))))
    forward = multiply(left_of((tn, 2 * last)), right_of((tn, 2 * last + 1)))
    maps[0] = packed(forward)

    pl.semaphore_wait(barrier, n - 1 + 2)

    def map_copy(which, slot, target):
        return pltpu.make_async_remote_copy(
            src_ref=maps.at[which],
            dst_ref=came.at[slot],
            send_sem=map_out.at[slot],
            recv_sem=map_in.at[slot],
            device_id={"narrow": target},
            device_id_type=MESH,
        )

    for step in mixed_near_first(n):

        @pl.when((me >= 1) & (me + step < n))
        def _():
            map_copy(0, step, me + step).start()

    for place in range(last):
        put(tb, cells + place, multiply(left_of((tb, 2 * place + 1)), right_of((tb, 2 * place))))
    backward = multiply(left_of((tb, 2 * last + 1)), right_of((tb, 2 * last)))
    maps[1] = packed(backward)
    for step in mixed_near_first(n):

        @pl.when((me <= n - 2) & (me - step >= 0))
        def _():
            map_copy(1, n - step, me - step).start()

    put(tn, whole, forward)
    put(tb, whole, backward)

    def offset_copy(source, target_ref, turn, slot, out, arrived, target):
        return pltpu.make_async_remote_copy(
            src_ref=source.at[turn],
            dst_ref=target_ref.at[turn, slot],
            send_sem=out.at[turn, slot],
            recv_sem=arrived.at[turn, slot],
            device_id={"narrow": target},
            device_id_type=MESH,
        )

    def f_copy(turn, slot, target):
        return offset_copy(fsend, fcame, turn, slot, f_out, f_in, target)

    def g_copy(turn, slot, target):
        return offset_copy(gsend, gcame, turn, slot, g_out, g_in, target)

    def send_f(turn):
        for step in far_first(n):

            @pl.when(me + step < n)
            def _():
                f_copy(turn, step, me + step).start()

    def send_g(turn):
        for step in far_first(n):

            @pl.when(me - step >= 0)
            def _():
                g_copy(turn, n - step, me - step).start()

    def wait_f(turn):
        for step in range(1, n):

            @pl.when(step <= me)
            def _():
                f_copy(turn, step, me).wait_recv()

    def wait_g(turn):
        for step in range(1, n):

            @pl.when(me + step < n)
            def _():
                g_copy(turn, n - step, me).wait_recv()

    def deep(vectors, weights):
        left = jnp.concatenate([stacked_vector(v) for v in vectors], axis=1)
        right = jnp.concatenate([ref[index] for ref, index in weights], axis=0)
        return folded(dot(left, right))

    def by(vector, place):
        ref, index = place
        return folded(dot(stacked_vector(vector), ref[index]))

    def forward_node(size, first):
        return tn, node(size, cells, first)

    def backward_node(size, first):
        return tb, node(size, cells, cells - first - size)

    def climb(source, at, whole):
        sums, source = {}, list(source)
        for p in range(0, cells, 2):
            source[p + 1] = source[p + 1] + by(source[p], at(1, p))
        for p in range(0, cells, 2):
            sums[2, p] = by(source[p + 1], at(1, p + 1))
        size = 2
        while size < cells // 2 or (whole and size < cells):
            for p in range(0, cells, 2 * size):
                sums[2 * size, p] = sums[size, p + size] + by(sums[size, p], at(size, p + size))
            size *= 2
        return source, sums

    def descend(source, sums, at):
        entering = {0: None}
        size = cells // 2
        while size >= 2:
            for p in range(0, cells, 2 * size):
                after = sums[size, p]
                if entering[p] is not None:
                    after = after + by(entering[p], at(size, p))
                entering[p + size] = after
            size //= 2
        values = list(source)
        for p in range(0, cells, 2):
            if entering[p] is not None:
                values[p] = values[p] + entering[p]
                values[p + 1] = values[p + 1] + by(entering[p], at(1, p))
        return values

    row = lax.broadcasted_iota(jnp.int32, (ROWS, LANES), 0)
    column = lax.broadcasted_iota(jnp.int32, (ROWS, LANES), 1)
    unit = jnp.where((row == column) & (row < NV), 1.0, 0.0).astype(F32)
    put(kw, 0, unit)
    put(jw, cells - 1, unit)
    ew[0] = tb[0]
    hsum[...] = jnp.zeros_like(hsum)
    came[0] = jnp.zeros_like(came[0])

    @pl.when(me >= 1)
    def _():
        put(phi, 1, unit)

    @pl.when(me <= n - 2)
    def _():
        put(phi, n - 1, unit)

    def keep_alone(source, sums):
        for i, value in enumerate(descend(source, sums, forward_node)):
            zs[i] = value

    loads[3].wait()
    blocks = load_cells(rhs_ref, pad)
    for i in range(cells):
        src[i] = blocks[i * NR : (i + 1) * NR]
    source, sums = climb([src[i] for i in range(cells)], forward_node, True)
    fsend[0] = sums[cells, 0]
    send_f(0)
    keep_alone(source, sums)

    from_before = jnp.maximum(me - 1, 0)
    from_after = jnp.maximum(n - 2 - me, 0)

    def with_pivot(i):
        exact = pivot[i]
        put(jp, i, dot(left_of((jw, i)), jnp.concatenate([exact, exact], axis=0)))

    def extended(slot):
        high, low = parts(unpacked(came[slot]))
        return multiply(jnp.concatenate([high, low], axis=1), right_of((phi, slot)))

    def tables(step, _):
        arrived = step <= from_before
        slot = jnp.where(arrived, step, 0)
        towards = jnp.where(arrived, step + 1, n)

        @pl.when(arrived)
        def _():
            map_copy(0, slot, me).wait_recv()

        chained = extended(slot)
        back = cells - 1 - step
        k = multiply(left_of((kw, step - 1)), right_of((tn, step - 1)))
        e = multiply(left_of((tb, step)), right_of((ew, step - 1)))
        j = multiply(left_of((jw, back + 1)), right_of((tb, back + 1)))
        h = multiply(left_of((kw, step - 1)), right_of((ew, step - 1)))
        with_pivot(back + 1)
        put(phi, towards, chained)
        put(kw, step, k)
        put(ew, step, e)
        put(jw, back, j)
        hsum[...] += h
        return 0

    lax.fori_loop(1, cells, tables, 0)
    with_pivot(0)
    put(hw, 0, hsum[...] + multiply(left_of((kw, cells - 1)), right_of((ew, cells - 1))))

    between = [(phi, k) for k in range(n)]

    def answer_copy(slot, target):
        return pltpu.make_async_remote_copy(
            src_ref=answers.at[slot],
            dst_ref=answered.at[slot],
            send_sem=answer_out.at[slot],
            recv_sem=answer_in.at[slot],
            device_id={"narrow": target},
            device_id_type=MESH,
        )

    def send_answers():
        high_low = jnp.concatenate([left_of((phi, k)) for k in range(1, n)], axis=0)
        products = multiply(high_low, right_of((hw, 0)))
        for k in range(1, n):
            answers[n - k] = packed(products[(k - 1) * ROWS : k * ROWS])

        def send(step, _):
            answer_copy(n - step, me - step).start()
            return 0

        lax.fori_loop(1, me + 1, send, 0)

    def take_answers():
        def wait(step, _):
            answer_copy(n - step, me).wait_recv()
            return 0

        lax.fori_loop(1, n - me, wait, 0)
        left = []
        for k in range(1, n):
            high, low = parts(unpacked(answered[k]))
            left += [high, low]
        put(
            rho,
            0,
            multiply(
                jnp.concatenate(left, axis=1),
                jnp.concatenate([right_of((phi, k)) for k in range(1, n)], axis=0),
            ),
        )
        put(rho, 1, multiply(left_of((rho, 0)), right_of((tb, whole))))
        put(rho, 2, multiply(left_of((tn, whole)), right_of((rho, 0))))

    def inside(turn, left):
        z = [zs[i] + folded(dot(left, kw[i])) for i in range(cells)]
        source, sums = climb(z[::-1], backward_node, False)
        for p, u in enumerate(descend(source, sums, backward_node)):
            i = cells - 1 - p
            product = dot(stacked_vector(u), pivot[i])
            xs[turn, i] = product[:NR] + product[NR:]

    def complete(turn, entering):
        left = stacked_vector(entering)
        for i in range(cells):
            xs[turn, i] = xs[turn, i] + folded(dot(left, jp[i]))

    def backward_alone():
        return deep([zs[i] for i in range(cells)], [(ew, i) for i in range(cells)])

    alone = backward_alone()
    wait_f(0)
    left = stacked_vector(deep([fcame[0, k] for k in range(n)], between))
    gsend[0] = alone + folded(dot(left, hw[0]))
    send_g(0)
    send_answers()
    inside(0, left)

    def chain_back(step, _):
        slot = n - step
        map_copy(1, slot, me).wait_recv()
        put(phi, slot - 1, extended(slot))
        return 0

    lax.fori_loop(1, from_after + 1, chain_back, 0)
    wait_g(0)
    complete(0, deep([gcame[0, k] for k in range(n)], between))

    def halo_copy(side, other):
        return pltpu.make_async_remote_copy(
            src_ref=xs.at[0],
            dst_ref=halo.at[side],
            send_sem=halo_out.at[side],
            recv_sem=halo_in.at[side],
            device_id={"wide": other},
            device_id_type=MESH,
        )

    halo_copy(0, high_line).start()
    halo_copy(1, low_line).start()

    store_cells(xs[0].reshape(cells * NR, LANES), first_ref)

    loads[4].wait()
    weights = []
    for place in range(3):
        total = jnp.zeros((cells, NV), F32)
        for side in range(2):
            relative = lax.rem(face_ref[0, side] - line + 1 + lines, lines)
            total = total + jnp.where(
                relative == place, coef_ref[:, pl.ds(side * NV, NV)], 0.0
            )
        weights.append(jnp.concatenate([total, jnp.zeros((cells, LANES - NV), F32)], axis=1))

    def drain(step, _):
        @pl.when(me + step < n)
        def _():
            f_copy(0, step, me + step).wait_send()

        @pl.when(me - step >= 0)
        def _():
            g_copy(0, n - step, me - step).wait_send()

        @pl.when((me >= 1) & (me + step < n))
        def _():
            map_copy(0, step, me + step).wait_send()

        @pl.when((me <= n - 2) & (me - step >= 0))
        def _():
            map_copy(1, n - step, me - step).wait_send()

        return 0

    lax.fori_loop(1, n, drain, 0)
    take_answers()

    def last_n(m):
        return (tn, node(m, cells, cells - m)) if low_bit(m) == m else (qw, m)

    for m in range(1, cells):
        size = low_bit(m)
        if size != m:
            first = node(size, cells, cells - m)
            put(qw, m, multiply(left_of((tn, first)), right_of(last_n(m - size))))

    halo_copy(0, high_line).wait_recv()
    halo_copy(1, low_line).wait_recv()

    for i in range(cells):
        coupled = (
            weights[0][i : i + 1] * halo[0, i]
            + weights[1][i : i + 1] * xs[0, i]
            + weights[2][i : i + 1] * halo[1, i]
        )
        src[i] = src[i] - coupled

    leaving = deep([src[i] for i in range(cells)], [last_n(cells - i) for i in range(cells)])
    fsend[1] = leaving
    send_f(1)
    keep_alone(*climb([src[i] for i in range(cells)], forward_node, False))
    gsend[1] = backward_alone() + by(leaving, (rho, 1))
    send_g(1)
    wait_f(1)
    left = stacked_vector(deep([fcame[1, k] for k in range(n)], between))
    inside(1, left)
    back = by(leaving, (rho, 0)) + folded(dot(left, rho[2]))
    halo_copy(0, high_line).wait_send()
    halo_copy(1, low_line).wait_send()

    def drain_last(step, _):
        @pl.when(me + step < n)
        def _():
            f_copy(1, step, me + step).wait_send()

        @pl.when(me - step >= 0)
        def _():
            g_copy(1, n - step, me - step).wait_send()
            answer_copy(n - step, me - step).wait_send()

        return 0

    lax.fori_loop(1, n, drain_last, 0)
    wait_g(1)
    complete(1, back + deep([gcame[1, k] for k in range(n)], between))
    store_cells(xs[1].reshape(cells * NR, LANES), second_ref)


def body(n, lines, rhs, pivot, upper, lower, neighbors, coupling):
    cells = rhs.shape[1]
    matrix = (LANES, 2 * LANES)
    tree = pltpu.VMEM((2 * cells - 1, *matrix), BF16)
    weight = pltpu.VMEM((cells, *matrix), BF16)
    vectors = pltpu.VMEM((cells, NR, LANES), F32)
    vmem = pl.BlockSpec(memory_space=pltpu.VMEM)
    hbm = pl.BlockSpec(memory_space=pltpu.HBM)
    dma = pltpu.SemaphoreType.DMA

    def in_hbm(x):
        return pltpu.with_memory_space_constraint(x, pltpu.HBM)

    first, second = pl.pallas_call(
        functools.partial(kernel, n, lines),
        out_shape=[pltpu.VMEM((cells, NV * NR), F32)] * 2,
        in_specs=[hbm] * 4 + [pl.BlockSpec(memory_space=pltpu.SMEM), hbm],
        out_specs=[vmem] * 2,
        scratch_shapes=[
            pltpu.VMEM((3, cells, NV * NV), BF16),
            pltpu.VMEM((cells, NV * NR), F32),
            pltpu.VMEM((cells, 2 * NV), F32),
            pltpu.VMEM((3, ROWS * (cells + 1), LANES), F32),
            pltpu.VMEM((LANES, LANES), F32),
            pltpu.VMEM((cells, LANES, LANES), BF16),
            tree,
            tree,
            weight,
            weight,
            weight,
            weight,
            weight,
            pltpu.VMEM((1, *matrix), BF16),
            pltpu.VMEM((ROWS, LANES), F32),
            pltpu.VMEM((3, *matrix), BF16),
            pltpu.VMEM((2, PACKED, LANES), F32),
            pltpu.VMEM((n, PACKED, LANES), F32),
            pltpu.VMEM((n, PACKED, LANES), F32),
            pltpu.VMEM((n, PACKED, LANES), F32),
            pltpu.VMEM((n + 1, *matrix), BF16),
            vectors,
            vectors,
            pltpu.VMEM((2, cells, NR, LANES), F32),
            pltpu.VMEM((2, cells, NR, LANES), F32),
            pltpu.VMEM((2, NR, LANES), F32),
            pltpu.VMEM((2, NR, LANES), F32),
            pltpu.VMEM((2, n, NR, LANES), F32),
            pltpu.VMEM((2, n, NR, LANES), F32),
            dma((5,)),
            dma((n,)),
            dma((n,)),
            dma((n,)),
            dma((n,)),
            dma((2, n)),
            dma((2, n)),
            dma((2, n)),
            dma((2, n)),
            dma((2,)),
            dma((2,)),
        ],
        compiler_params=pltpu.CompilerParams(
            collective_id=0, has_side_effects=True, vmem_limit_bytes=40 * 1024 * 1024
        ),
    )(*(in_hbm(x) for x in (pivot[0], upper[0], lower[0], rhs[0], neighbors, coupling[0])))
    return first[None], second[None]


def solution(mesh):
    blocks = P("wide", "narrow", None)
    return jax.shard_map(
        functools.partial(body, mesh.shape["narrow"], mesh.shape["wide"]),
        mesh=mesh,
        in_specs=(blocks, blocks, blocks, blocks, P("wide", None), blocks),
        out_specs=(blocks, blocks),
        check_vma=False,
    )
```

```python
import functools

import jax
import jax.numpy as jnp
from jax import lax
from jax.experimental import pallas as pl
from jax.experimental.pallas import tpu as pltpu
from jax.sharding import PartitionSpec as P

NV = 95
NR = 8
ROWS = 96
PACKED = 72
LANES = 128
F32 = jnp.float32
BF16 = jnp.bfloat16
MESH = pl.DeviceIdType.MESH


def dot(left, right):
    return jnp.dot(left, right, preferred_element_type=F32)


def parts(value):
    high = value.astype(BF16)
    return high, (value - high.astype(F32)).astype(BF16)


def stacked_vector(value):
    high = value.astype(BF16).astype(F32)
    return jnp.concatenate([high, value - high], axis=0).astype(BF16)


def folded(product):
    rows = product.shape[0] // 2
    return product[:rows, :LANES] + (product[:rows, LANES:] + product[rows:, :LANES])


def put(ref, index, value):
    high, low = parts(value)
    ref[index, pl.ds(0, ROWS), pl.ds(0, LANES)] = high
    ref[index, pl.ds(0, ROWS), pl.ds(LANES, LANES)] = low


def left_of(place):
    ref, index = place
    return ref[index, pl.ds(0, ROWS), :]


def right_of(place):
    ref, index = place
    value = ref[index]
    return jnp.concatenate([value, value], axis=0)


def multiply(left, right):
    product = dot(left, right)
    return product[:, :LANES] + product[:, LANES:]


def packed(value):
    top, rest = value[:PACKED], value[PACKED:]
    lane = lax.broadcasted_iota(jnp.int32, rest.shape, 1)
    pieces = []
    for part in range(3):
        moved = pltpu.roll(rest, (ROWS - 32 * part) % LANES, 1)
        pieces.append(jnp.where(lane >= ROWS, moved, top[24 * part : 24 * part + 24]))
    return jnp.concatenate(pieces, axis=0)


def unpacked(value):
    lane = lax.broadcasted_iota(jnp.int32, (24, LANES), 1)
    rest = jnp.zeros((24, LANES), F32)
    pieces = []
    for part in range(3):
        own = value[24 * part : 24 * part + 24]
        moved = pltpu.roll(own, (LANES - ROWS + 32 * part) % LANES, 1)
        rest = jnp.where((lane >= 32 * part) & (lane < 32 * part + 32), moved, rest)
        pieces.append(jnp.where(lane < ROWS, own, 0.0))
    return jnp.concatenate(pieces + [rest], axis=0)


def granule_transpose(value):
    row = lax.broadcasted_iota(jnp.int32, value.shape, 0)
    group = lax.broadcasted_iota(jnp.int32, value.shape, 1) // NR
    height = value.shape[0]
    for bit in (1, 2, 4, 8):
        row_set = (row & bit) != 0
        group_set = (group & bit) != 0
        down = pltpu.roll(pltpu.roll(value, bit, 0), LANES - NR * bit, 1)
        up = pltpu.roll(pltpu.roll(value, height - bit, 0), NR * bit, 1)
        value = jnp.where(row_set == group_set, value, jnp.where(row_set, down, up))
    return value


def load_cells(flat_ref, pad_ref):
    cells = flat_ref.shape[0]
    width = NV * NR
    pad_ref[...] = jnp.zeros_like(pad_ref)
    for block in range(ROWS // 16):
        first = block * LANES
        wide = min(LANES, width - first)
        pad_ref[pl.ds(block * 16, cells), pl.ds(0, wide)] = flat_ref[:, pl.ds(first, wide)]
    turned = granule_transpose(pad_ref[pl.ds(0, ROWS), :])
    pad_ref[pl.ds(0, ROWS), :] = turned
    return jnp.transpose(pad_ref[...])


def store_cells(blocks, flat_ref):
    width = NV * NR
    cells = flat_ref.shape[0]
    turned = granule_transpose(jnp.transpose(blocks)[:ROWS])
    for block in range(ROWS // 16):
        first = block * LANES
        wide = min(LANES, width - first)
        flat_ref[:, pl.ds(first, wide)] = turned[block * 16 : block * 16 + cells, :wide]


def mixed_near_first(n):
    early = {4: 1.5, 8: 4.5, 12: 8.5}
    return sorted(range(1, n), key=lambda step: early.get(step, step))


def far_first(n):
    return sorted(range(1, n), key=lambda step: -sum(min(d, 4 - d) for d in (step % 4, step // 4 % 4)))


def low_bit(m):
    return m & -m


def node(level_size, cells, first):
    return 2 * cells - 2 * cells // level_size + first // level_size


def kernel(
    n,
    lines,
    pivot_hbm,
    upper_hbm,
    lower_hbm,
    rhs_hbm,
    face_ref,
    coef_hbm,
    first_ref,
    second_ref,
    flat,
    rhs_ref,
    coef_ref,
    slab,
    pad,
    pivot,
    tn,
    tb,
    qw,
    ew,
    kw,
    jw,
    jp,
    ku,
    kx,
    hw,
    hsum,
    rho,
    maps,
    came,
    answers,
    answered,
    phi,
    src,
    zs,
    xs,
    halo,
    fsend,
    gsend,
    fcame,
    gcame,
    load_sem,
    map_out,
    map_in,
    answer_out,
    answer_in,
    f_out,
    f_in,
    g_out,
    g_in,
    halo_out,
    halo_in,
):
    cells = rhs_ref.shape[0]
    me = lax.axis_index("narrow")
    line = lax.axis_index("wide")
    low_line = lax.rem(line + lines - 1, lines)
    high_line = lax.rem(line + 1, lines)

    loads = [
        pltpu.make_async_copy(hbm, flat.at[number], load_sem.at[number])
        for number, hbm in enumerate((pivot_hbm, upper_hbm, lower_hbm))
    ]
    loads.append(pltpu.make_async_copy(rhs_hbm, rhs_ref, load_sem.at[3]))
    loads.append(pltpu.make_async_copy(coef_hbm, coef_ref, load_sem.at[4]))
    for load in loads:
        load.start()

    fcame[...] = jnp.zeros_like(fcame)
    gcame[...] = jnp.zeros_like(gcame)
    answered[...] = jnp.zeros_like(answered)

    barrier = pltpu.get_barrier_semaphore()

    def greet(step, _):
        pl.semaphore_signal(
            barrier, inc=1, device_id={"narrow": lax.rem(me + step, n)}, device_id_type=MESH
        )
        return 0

    lax.fori_loop(1, n, greet, 0)
    for other in (low_line, high_line):
        pl.semaphore_signal(barrier, inc=1, device_id={"wide": other}, device_id_type=MESH)

    slab[...] = jnp.zeros_like(slab)
    tail = jnp.zeros((LANES - ROWS, 2 * LANES), BF16)

    def clear_nodes(i, _):
        for ref in (tn, tb):
            ref[i, pl.ds(ROWS, LANES - ROWS), :] = tail
        return 0

    lax.fori_loop(0, 2 * cells - 1, clear_nodes, 0)

    def clear(i, _):
        for ref in (qw, ew, kw, jw, jp, ku, kx):
            ref[i, pl.ds(ROWS, LANES - ROWS), :] = tail
        return 0

    lax.fori_loop(0, cells, clear, 0)
    hw[0, pl.ds(ROWS, LANES - ROWS), :] = tail
    for i in range(3):
        rho[i, pl.ds(ROWS, LANES - ROWS), :] = tail

    def clear_phi(i, _):
        phi[i] = jnp.zeros((LANES, 2 * LANES), BF16)
        return 0

    lax.fori_loop(0, n, clear_phi, 0)

    for number in range(3):
        loads[number].wait()
        for row in range(NV):
            slab[number, pl.ds(row * (cells + 1), cells), pl.ds(0, NV)] = flat[
                number, :, pl.ds(row * NV, NV)
            ].astype(F32)

    no_rows = jnp.zeros((LANES - ROWS, LANES), BF16)

    for i in range(cells):
        p, u, l = (
            slab[number, pl.ds(i, ROWS, stride=cells + 1), :] for number in range(3)
        )
        p16 = p.astype(BF16)
        pivot[i] = jnp.concatenate([p16, no_rows], axis=0)
        right = jnp.concatenate([(-u).astype(BF16), (-l).astype(BF16)], axis=1)
        right = jnp.concatenate([right, tail], axis=0)
        both = dot(p16, right)
        put(tn, i, both[:, :LANES])
        put(tb, i, both[:, LANES:])

    last = cells - 2
    whole = cells + last
    for place in range(last):
        put(tn, cells + place, multiply(left_of((tn, 2 * place)), right_of((tn, 2 * place + 1))))
    forward = multiply(left_of((tn, 2 * last)), right_of((tn, 2 * last + 1)))
    maps[0] = packed(forward)

    pl.semaphore_wait(barrier, n - 1 + 2)

    def map_copy(which, slot, target):
        return pltpu.make_async_remote_copy(
            src_ref=maps.at[which],
            dst_ref=came.at[slot],
            send_sem=map_out.at[slot],
            recv_sem=map_in.at[slot],
            device_id={"narrow": target},
            device_id_type=MESH,
        )

    for step in mixed_near_first(n):

        @pl.when((me >= 1) & (me + step < n))
        def _():
            map_copy(0, step, me + step).start()

    for place in range(last):
        put(tb, cells + place, multiply(left_of((tb, 2 * place + 1)), right_of((tb, 2 * place))))
    backward = multiply(left_of((tb, 2 * last + 1)), right_of((tb, 2 * last)))
    maps[1] = packed(backward)
    for step in mixed_near_first(n):

        @pl.when((me <= n - 2) & (me - step >= 0))
        def _():
            map_copy(1, n - step, me - step).start()

    put(tn, whole, forward)
    put(tb, whole, backward)

    def offset_copy(source, target_ref, turn, slot, out, arrived, target):
        return pltpu.make_async_remote_copy(
            src_ref=source.at[turn],
            dst_ref=target_ref.at[turn, slot],
            send_sem=out.at[turn, slot],
            recv_sem=arrived.at[turn, slot],
            device_id={"narrow": target},
            device_id_type=MESH,
        )

    def f_copy(turn, slot, target):
        return offset_copy(fsend, fcame, turn, slot, f_out, f_in, target)

    def g_copy(turn, slot, target):
        return offset_copy(gsend, gcame, turn, slot, g_out, g_in, target)

    def send_f(turn):
        for step in far_first(n):

            @pl.when(me + step < n)
            def _():
                f_copy(turn, step, me + step).start()

    def send_g(turn):
        for step in far_first(n):

            @pl.when(me - step >= 0)
            def _():
                g_copy(turn, n - step, me - step).start()

    def wait_f(turn):
        for step in range(1, n):

            @pl.when(step <= me)
            def _():
                f_copy(turn, step, me).wait_recv()

    def wait_g(turn):
        for step in range(1, n):

            @pl.when(me + step < n)
            def _():
                g_copy(turn, n - step, me).wait_recv()

    def deep(vectors, weights):
        left = jnp.concatenate([stacked_vector(v) for v in vectors], axis=1)
        right = jnp.concatenate([ref[index] for ref, index in weights], axis=0)
        return folded(dot(left, right))

    def by(vector, place):
        ref, index = place
        return folded(dot(stacked_vector(vector), ref[index]))

    def forward_node(size, first):
        return tn, node(size, cells, first)

    def backward_node(size, first):
        return tb, node(size, cells, cells - first - size)

    def climb(source, at, whole):
        sums, source = {}, list(source)
        for p in range(0, cells, 2):
            source[p + 1] = source[p + 1] + by(source[p], at(1, p))
        for p in range(0, cells, 2):
            sums[2, p] = by(source[p + 1], at(1, p + 1))
        size = 2
        while size < cells // 2 or (whole and size < cells):
            for p in range(0, cells, 2 * size):
                sums[2 * size, p] = sums[size, p + size] + by(sums[size, p], at(size, p + size))
            size *= 2
        return source, sums

    def descend(source, sums, at):
        entering = {0: None}
        size = cells // 2
        while size >= 2:
            for p in range(0, cells, 2 * size):
                after = sums[size, p]
                if entering[p] is not None:
                    after = after + by(entering[p], at(size, p))
                entering[p + size] = after
            size //= 2
        values = list(source)
        for p in range(0, cells, 2):
            if entering[p] is not None:
                values[p] = values[p] + entering[p]
                values[p + 1] = values[p + 1] + by(entering[p], at(1, p))
        return values

    row = lax.broadcasted_iota(jnp.int32, (ROWS, LANES), 0)
    column = lax.broadcasted_iota(jnp.int32, (ROWS, LANES), 1)
    unit = jnp.where((row == column) & (row < NV), 1.0, 0.0).astype(F32)
    put(kw, 0, unit)
    put(jw, cells - 1, unit)
    ew[0] = tb[0]
    hsum[...] = jnp.zeros_like(hsum)
    came[0] = jnp.zeros_like(came[0])

    @pl.when(me >= 1)
    def _():
        put(phi, 1, unit)

    @pl.when(me <= n - 2)
    def _():
        put(phi, n - 1, unit)

    def keep_alone(source, sums):
        for i, value in enumerate(descend(source, sums, forward_node)):
            zs[i] = value

    loads[3].wait()
    blocks = load_cells(rhs_ref, pad)
    for i in range(cells):
        src[i] = blocks[i * NR : (i + 1) * NR]
    source, sums = climb([src[i] for i in range(cells)], forward_node, True)
    fsend[0] = sums[cells, 0]
    send_f(0)
    keep_alone(source, sums)

    from_before = jnp.maximum(me - 1, 0)
    from_after = jnp.maximum(n - 2 - me, 0)

    def times_pivot(table, i):
        exact = pivot[i]
        return dot(left_of((table, i)), jnp.concatenate([exact, exact], axis=0))

    def extended(slot):
        high, low = parts(unpacked(came[slot]))
        return multiply(jnp.concatenate([high, low], axis=1), right_of((phi, slot)))

    def tables(step, _):
        arrived = step <= from_before
        slot = jnp.where(arrived, step, 0)
        towards = jnp.where(arrived, step + 1, n)

        @pl.when(arrived)
        def _():
            map_copy(0, slot, me).wait_recv()

        chained = extended(slot)
        back = cells - 1 - step
        k = multiply(left_of((kw, step - 1)), right_of((tn, step - 1)))
        e = multiply(left_of((tb, step)), right_of((ew, step - 1)))
        j = multiply(left_of((jw, back + 1)), right_of((tb, back + 1)))
        h = multiply(left_of((kw, step - 1)), right_of((ew, step - 1)))
        put(jp, back + 1, times_pivot(jw, back + 1))
        put(phi, towards, chained)
        put(kw, step, k)
        put(ew, step, e)
        put(jw, back, j)
        hsum[...] += h
        return 0

    lax.fori_loop(1, cells, tables, 0)
    put(jp, 0, times_pivot(jw, 0))
    put(hw, 0, hsum[...] + multiply(left_of((kw, cells - 1)), right_of((ew, cells - 1))))

    between = [(phi, k) for k in range(n)]

    def answer_copy(slot, target):
        return pltpu.make_async_remote_copy(
            src_ref=answers.at[slot],
            dst_ref=answered.at[slot],
            send_sem=answer_out.at[slot],
            recv_sem=answer_in.at[slot],
            device_id={"narrow": target},
            device_id_type=MESH,
        )

    def send_answers():
        high_low = jnp.concatenate([left_of((phi, k)) for k in range(1, n)], axis=0)
        products = multiply(high_low, right_of((hw, 0)))
        for k in range(1, n):
            answers[n - k] = packed(products[(k - 1) * ROWS : k * ROWS])

        def send(step, _):
            answer_copy(n - step, me - step).start()
            return 0

        lax.fori_loop(1, me + 1, send, 0)

    def take_answers():
        def wait(step, _):
            answer_copy(n - step, me).wait_recv()
            return 0

        lax.fori_loop(1, n - me, wait, 0)
        left = []
        for k in range(1, n):
            high, low = parts(unpacked(answered[k]))
            left += [high, low]
        put(
            rho,
            0,
            multiply(
                jnp.concatenate(left, axis=1),
                jnp.concatenate([right_of((phi, k)) for k in range(1, n)], axis=0),
            ),
        )
        put(rho, 1, multiply(left_of((rho, 0)), right_of((tb, whole))))
        put(rho, 2, multiply(left_of((tn, whole)), right_of((rho, 0))))

    def inside(turn, z):
        source, sums = climb(z[::-1], backward_node, False)
        for p, u in enumerate(descend(source, sums, backward_node)):
            i = cells - 1 - p
            product = dot(stacked_vector(u), pivot[i])
            xs[turn, i] = product[:NR] + product[NR:]

    def complete(turn, entering, table):
        left = stacked_vector(entering)
        for i in range(cells):
            xs[turn, i] = xs[turn, i] + folded(dot(left, table[i]))

    def backward_alone():
        return deep([zs[i] for i in range(cells)], [(ew, i) for i in range(cells)])

    alone = backward_alone()
    wait_f(0)
    left = stacked_vector(deep([fcame[0, k] for k in range(n)], between))
    gsend[0] = alone + folded(dot(left, hw[0]))
    send_g(0)
    inside(0, [z + folded(dot(left, kw[i])) for i, z in enumerate(zs[i] for i in range(cells))])

    def chain_back(step, _):
        slot = n - step
        map_copy(1, slot, me).wait_recv()
        put(phi, slot - 1, extended(slot))
        return 0

    lax.fori_loop(1, from_after + 1, chain_back, 0)
    send_answers()
    wait_g(0)
    complete(0, deep([gcame[0, k] for k in range(n)], between), jp)

    def halo_copy(side, other):
        return pltpu.make_async_remote_copy(
            src_ref=xs.at[0],
            dst_ref=halo.at[side],
            send_sem=halo_out.at[side],
            recv_sem=halo_in.at[side],
            device_id={"wide": other},
            device_id_type=MESH,
        )

    halo_copy(0, high_line).start()
    halo_copy(1, low_line).start()

    store_cells(xs[0].reshape(cells * NR, LANES), first_ref)

    loads[4].wait()
    weights = []
    for place in range(3):
        total = jnp.zeros((cells, NV), F32)
        for side in range(2):
            relative = lax.rem(face_ref[0, side] - line + 1 + lines, lines)
            total = total + jnp.where(
                relative == place, coef_ref[:, pl.ds(side * NV, NV)], 0.0
            )
        weights.append(jnp.concatenate([total, jnp.zeros((cells, LANES - NV), F32)], axis=1))

    def drain(step, _):
        @pl.when(me + step < n)
        def _():
            f_copy(0, step, me + step).wait_send()

        @pl.when(me - step >= 0)
        def _():
            g_copy(0, n - step, me - step).wait_send()

        @pl.when((me >= 1) & (me + step < n))
        def _():
            map_copy(0, step, me + step).wait_send()

        @pl.when((me <= n - 2) & (me - step >= 0))
        def _():
            map_copy(1, n - step, me - step).wait_send()

        return 0

    lax.fori_loop(1, n, drain, 0)

    def last_n(m):
        return (tn, node(m, cells, cells - m)) if low_bit(m) == m else (qw, m)

    for m in range(1, cells):
        size = low_bit(m)
        if size != m:
            first = node(size, cells, cells - m)
            put(qw, m, multiply(left_of((tn, first)), right_of(last_n(m - size))))

    ku[cells - 1] = kw[cells - 1]

    def respond(step, _):
        back = cells - 1 - step
        own = left_of((kw, back))
        own = own[:, :LANES].astype(F32) + own[:, LANES:].astype(F32)
        put(ku, back, own + multiply(left_of((ku, back + 1)), right_of((tb, back + 1))))
        put(kx, back + 1, times_pivot(ku, back + 1))
        return 0

    lax.fori_loop(1, cells, respond, 0)
    put(kx, 0, times_pivot(ku, 0))
    take_answers()

    halo_copy(0, high_line).wait_recv()
    halo_copy(1, low_line).wait_recv()

    for i in range(cells):
        coupled = (
            weights[0][i : i + 1] * halo[0, i]
            + weights[1][i : i + 1] * xs[0, i]
            + weights[2][i : i + 1] * halo[1, i]
        )
        src[i] = src[i] - coupled

    leaving = deep([src[i] for i in range(cells)], [last_n(cells - i) for i in range(cells)])
    fsend[1] = leaving
    send_f(1)
    keep_alone(*climb([src[i] for i in range(cells)], forward_node, False))
    gsend[1] = backward_alone() + by(leaving, (rho, 1))
    send_g(1)
    inside(1, [zs[i] for i in range(cells)])
    wait_f(1)
    entering = deep([fcame[1, k] for k in range(n)], between)
    complete(1, entering, kx)
    back = by(leaving, (rho, 0)) + by(entering, (rho, 2))
    halo_copy(0, high_line).wait_send()
    halo_copy(1, low_line).wait_send()

    def drain_last(step, _):
        @pl.when(me + step < n)
        def _():
            f_copy(1, step, me + step).wait_send()

        @pl.when(me - step >= 0)
        def _():
            g_copy(1, n - step, me - step).wait_send()
            answer_copy(n - step, me - step).wait_send()

        return 0

    lax.fori_loop(1, n, drain_last, 0)
    wait_g(1)
    complete(1, back + deep([gcame[1, k] for k in range(n)], between), jp)
    store_cells(xs[1].reshape(cells * NR, LANES), second_ref)


def body(n, lines, rhs, pivot, upper, lower, neighbors, coupling):
    cells = rhs.shape[1]
    matrix = (LANES, 2 * LANES)
    tree = pltpu.VMEM((2 * cells - 1, *matrix), BF16)
    weight = pltpu.VMEM((cells, *matrix), BF16)
    vectors = pltpu.VMEM((cells, NR, LANES), F32)
    vmem = pl.BlockSpec(memory_space=pltpu.VMEM)
    hbm = pl.BlockSpec(memory_space=pltpu.HBM)
    dma = pltpu.SemaphoreType.DMA

    def in_hbm(x):
        return pltpu.with_memory_space_constraint(x, pltpu.HBM)

    first, second = pl.pallas_call(
        functools.partial(kernel, n, lines),
        out_shape=[pltpu.VMEM((cells, NV * NR), F32)] * 2,
        in_specs=[hbm] * 4 + [pl.BlockSpec(memory_space=pltpu.SMEM), hbm],
        out_specs=[vmem] * 2,
        scratch_shapes=[
            pltpu.VMEM((3, cells, NV * NV), BF16),
            pltpu.VMEM((cells, NV * NR), F32),
            pltpu.VMEM((cells, 2 * NV), F32),
            pltpu.VMEM((3, ROWS * (cells + 1), LANES), F32),
            pltpu.VMEM((LANES, LANES), F32),
            pltpu.VMEM((cells, LANES, LANES), BF16),
            tree,
            tree,
            weight,
            weight,
            weight,
            weight,
            weight,
            weight,
            weight,
            pltpu.VMEM((1, *matrix), BF16),
            pltpu.VMEM((ROWS, LANES), F32),
            pltpu.VMEM((3, *matrix), BF16),
            pltpu.VMEM((2, PACKED, LANES), F32),
            pltpu.VMEM((n, PACKED, LANES), F32),
            pltpu.VMEM((n, PACKED, LANES), F32),
            pltpu.VMEM((n, PACKED, LANES), F32),
            pltpu.VMEM((n + 1, *matrix), BF16),
            vectors,
            vectors,
            pltpu.VMEM((2, cells, NR, LANES), F32),
            pltpu.VMEM((2, cells, NR, LANES), F32),
            pltpu.VMEM((2, NR, LANES), F32),
            pltpu.VMEM((2, NR, LANES), F32),
            pltpu.VMEM((2, n, NR, LANES), F32),
            pltpu.VMEM((2, n, NR, LANES), F32),
            dma((5,)),
            dma((n,)),
            dma((n,)),
            dma((n,)),
            dma((n,)),
            dma((2, n)),
            dma((2, n)),
            dma((2, n)),
            dma((2, n)),
            dma((2,)),
            dma((2,)),
        ],
        compiler_params=pltpu.CompilerParams(
            collective_id=0, has_side_effects=True, vmem_limit_bytes=40 * 1024 * 1024
        ),
    )(*(in_hbm(x) for x in (pivot[0], upper[0], lower[0], rhs[0], neighbors, coupling[0])))
    return first[None], second[None]


def solution(mesh):
    blocks = P("wide", "narrow", None)
    return jax.shard_map(
        functools.partial(body, mesh.shape["narrow"], mesh.shape["wide"]),
        mesh=mesh,
        in_specs=(blocks, blocks, blocks, blocks, P("wide", None), blocks),
        out_specs=(blocks, blocks),
        check_vma=False,
    )
```

```python
import functools

import jax
import jax.numpy as jnp
from jax import lax
from jax.experimental import pallas as pl
from jax.experimental.pallas import tpu as pltpu
from jax.sharding import PartitionSpec as P

NV = 95
NR = 8
ROWS = 96
PACKED = 72
LANES = 128
F32 = jnp.float32
BF16 = jnp.bfloat16
MESH = pl.DeviceIdType.MESH


def dot(left, right):
    return jnp.dot(left, right, preferred_element_type=F32)


def parts(value):
    high = value.astype(BF16)
    return high, (value - high.astype(F32)).astype(BF16)


def stacked_vector(value):
    high = value.astype(BF16).astype(F32)
    return jnp.concatenate([high, value - high], axis=0).astype(BF16)


def folded(product):
    rows = product.shape[0] // 2
    return product[:rows, :LANES] + (product[:rows, LANES:] + product[rows:, :LANES])


def put(ref, index, value):
    high, low = parts(value)
    ref[index, pl.ds(0, ROWS), pl.ds(0, LANES)] = high
    ref[index, pl.ds(0, ROWS), pl.ds(LANES, LANES)] = low


def left_of(place):
    ref, index = place
    return ref[index, pl.ds(0, ROWS), :]


def right_of(place):
    ref, index = place
    value = ref[index]
    return jnp.concatenate([value, value], axis=0)


def multiply(left, right):
    product = dot(left, right)
    return product[:, :LANES] + product[:, LANES:]


def packed(value):
    top, rest = value[:PACKED], value[PACKED:]
    lane = lax.broadcasted_iota(jnp.int32, rest.shape, 1)
    pieces = []
    for part in range(3):
        moved = pltpu.roll(rest, (ROWS - 32 * part) % LANES, 1)
        pieces.append(jnp.where(lane >= ROWS, moved, top[24 * part : 24 * part + 24]))
    return jnp.concatenate(pieces, axis=0)


def unpacked(value):
    lane = lax.broadcasted_iota(jnp.int32, (24, LANES), 1)
    rest = jnp.zeros((24, LANES), F32)
    pieces = []
    for part in range(3):
        own = value[24 * part : 24 * part + 24]
        moved = pltpu.roll(own, (LANES - ROWS + 32 * part) % LANES, 1)
        rest = jnp.where((lane >= 32 * part) & (lane < 32 * part + 32), moved, rest)
        pieces.append(jnp.where(lane < ROWS, own, 0.0))
    return jnp.concatenate(pieces + [rest], axis=0)


def granule_transpose(value):
    row = lax.broadcasted_iota(jnp.int32, value.shape, 0)
    group = lax.broadcasted_iota(jnp.int32, value.shape, 1) // NR
    height = value.shape[0]
    for bit in (1, 2, 4, 8):
        row_set = (row & bit) != 0
        group_set = (group & bit) != 0
        down = pltpu.roll(pltpu.roll(value, bit, 0), LANES - NR * bit, 1)
        up = pltpu.roll(pltpu.roll(value, height - bit, 0), NR * bit, 1)
        value = jnp.where(row_set == group_set, value, jnp.where(row_set, down, up))
    return value


def load_cells(flat_ref, pad_ref):
    cells = flat_ref.shape[0]
    width = NV * NR
    pad_ref[...] = jnp.zeros_like(pad_ref)
    for block in range(ROWS // 16):
        first = block * LANES
        wide = min(LANES, width - first)
        pad_ref[pl.ds(block * 16, cells), pl.ds(0, wide)] = flat_ref[:, pl.ds(first, wide)]
    turned = granule_transpose(pad_ref[pl.ds(0, ROWS), :])
    pad_ref[pl.ds(0, ROWS), :] = turned
    return jnp.transpose(pad_ref[...])


def store_cells(blocks, flat_ref):
    width = NV * NR
    cells = flat_ref.shape[0]
    turned = granule_transpose(jnp.transpose(blocks)[:ROWS])
    for block in range(ROWS // 16):
        first = block * LANES
        wide = min(LANES, width - first)
        flat_ref[:, pl.ds(first, wide)] = turned[block * 16 : block * 16 + cells, :wide]


def mixed_near_first(n):
    early = {4: 1.5, 8: 4.5, 12: 8.5}
    return sorted(range(1, n), key=lambda step: early.get(step, step))


def far_first(n):
    return sorted(range(1, n), key=lambda step: -sum(min(d, 4 - d) for d in (step % 4, step // 4 % 4)))


def low_bit(m):
    return m & -m


def node(level_size, cells, first):
    return 2 * cells - 2 * cells // level_size + first // level_size


def kernel(
    n,
    lines,
    pivot_hbm,
    upper_hbm,
    lower_hbm,
    rhs_hbm,
    face_ref,
    coef_hbm,
    first_ref,
    second_ref,
    flat,
    rhs_ref,
    coef_ref,
    slab,
    pad,
    pivot,
    tn,
    tb,
    qw,
    ew,
    kw,
    jw,
    jp,
    ku,
    kx,
    hw,
    hsum,
    rho,
    maps,
    came,
    answers,
    answered,
    phi,
    src,
    zs,
    xs,
    halo,
    fsend,
    gsend,
    fcame,
    gcame,
    load_sem,
    map_out,
    map_in,
    answer_out,
    answer_in,
    f_out,
    f_in,
    g_out,
    g_in,
    halo_out,
    halo_in,
):
    cells = rhs_ref.shape[0]
    me = lax.axis_index("narrow")
    line = lax.axis_index("wide")
    low_line = lax.rem(line + lines - 1, lines)
    high_line = lax.rem(line + 1, lines)

    loads = [
        pltpu.make_async_copy(hbm, flat.at[number], load_sem.at[number])
        for number, hbm in enumerate((pivot_hbm, upper_hbm, lower_hbm))
    ]
    loads.append(pltpu.make_async_copy(rhs_hbm, rhs_ref, load_sem.at[3]))
    loads.append(pltpu.make_async_copy(coef_hbm, coef_ref, load_sem.at[4]))
    for load in loads:
        load.start()

    fcame[...] = jnp.zeros_like(fcame)
    gcame[...] = jnp.zeros_like(gcame)
    answered[...] = jnp.zeros_like(answered)

    barrier = pltpu.get_barrier_semaphore()

    def greet(step, _):
        pl.semaphore_signal(
            barrier, inc=1, device_id={"narrow": lax.rem(me + step, n)}, device_id_type=MESH
        )
        return 0

    lax.fori_loop(1, n, greet, 0)
    for other in (low_line, high_line):
        pl.semaphore_signal(barrier, inc=1, device_id={"wide": other}, device_id_type=MESH)

    slab[...] = jnp.zeros_like(slab)
    tail = jnp.zeros((LANES - ROWS, 2 * LANES), BF16)

    def clear_nodes(i, _):
        for ref in (tn, tb):
            ref[i, pl.ds(ROWS, LANES - ROWS), :] = tail
        return 0

    lax.fori_loop(0, 2 * cells - 1, clear_nodes, 0)

    def clear(i, _):
        for ref in (qw, ew, kw, jw, jp, ku, kx):
            ref[i, pl.ds(ROWS, LANES - ROWS), :] = tail
        return 0

    lax.fori_loop(0, cells, clear, 0)
    hw[0, pl.ds(ROWS, LANES - ROWS), :] = tail
    for i in range(3):
        rho[i, pl.ds(ROWS, LANES - ROWS), :] = tail

    def clear_phi(i, _):
        phi[i] = jnp.zeros((LANES, 2 * LANES), BF16)
        return 0

    lax.fori_loop(0, n, clear_phi, 0)

    for number in range(3):
        loads[number].wait()
        for row in range(NV):
            slab[number, pl.ds(row * (cells + 1), cells), pl.ds(0, NV)] = flat[
                number, :, pl.ds(row * NV, NV)
            ].astype(F32)

    no_rows = jnp.zeros((LANES - ROWS, LANES), BF16)

    for i in range(cells):
        p, u, l = (
            slab[number, pl.ds(i, ROWS, stride=cells + 1), :] for number in range(3)
        )
        p16 = p.astype(BF16)
        pivot[i] = jnp.concatenate([p16, no_rows], axis=0)
        right = jnp.concatenate([(-u).astype(BF16), (-l).astype(BF16)], axis=1)
        right = jnp.concatenate([right, tail], axis=0)
        both = dot(p16, right)
        put(tn, i, both[:, :LANES])
        put(tb, i, both[:, LANES:])

    last = cells - 2
    whole = cells + last
    for place in range(last):
        put(tn, cells + place, multiply(left_of((tn, 2 * place)), right_of((tn, 2 * place + 1))))
    forward = multiply(left_of((tn, 2 * last)), right_of((tn, 2 * last + 1)))
    maps[0] = packed(forward)

    pl.semaphore_wait(barrier, n - 1 + 2)

    def map_copy(which, slot, target):
        return pltpu.make_async_remote_copy(
            src_ref=maps.at[which],
            dst_ref=came.at[slot],
            send_sem=map_out.at[slot],
            recv_sem=map_in.at[slot],
            device_id={"narrow": target},
            device_id_type=MESH,
        )

    for step in mixed_near_first(n):

        @pl.when((me >= 1) & (me + step < n))
        def _():
            map_copy(0, step, me + step).start()

    for place in range(last):
        put(tb, cells + place, multiply(left_of((tb, 2 * place + 1)), right_of((tb, 2 * place))))
    backward = multiply(left_of((tb, 2 * last + 1)), right_of((tb, 2 * last)))
    maps[1] = packed(backward)
    for step in mixed_near_first(n):

        @pl.when((me <= n - 2) & (me - step >= 0))
        def _():
            map_copy(1, n - step, me - step).start()

    put(tn, whole, forward)
    put(tb, whole, backward)

    def offset_copy(source, target_ref, turn, slot, out, arrived, target):
        return pltpu.make_async_remote_copy(
            src_ref=source.at[turn],
            dst_ref=target_ref.at[turn, slot],
            send_sem=out.at[turn, slot],
            recv_sem=arrived.at[turn, slot],
            device_id={"narrow": target},
            device_id_type=MESH,
        )

    def f_copy(turn, slot, target):
        return offset_copy(fsend, fcame, turn, slot, f_out, f_in, target)

    def g_copy(turn, slot, target):
        return offset_copy(gsend, gcame, turn, slot, g_out, g_in, target)

    def send_f(turn):
        for step in far_first(n):

            @pl.when(me + step < n)
            def _():
                f_copy(turn, step, me + step).start()

    def send_g(turn):
        for step in far_first(n):

            @pl.when(me - step >= 0)
            def _():
                g_copy(turn, n - step, me - step).start()

    def wait_f(turn):
        for step in range(1, n):

            @pl.when(step <= me)
            def _():
                f_copy(turn, step, me).wait_recv()

    def wait_g(turn):
        for step in range(1, n):

            @pl.when(me + step < n)
            def _():
                g_copy(turn, n - step, me).wait_recv()

    def deep(vectors, weights):
        left = jnp.concatenate([stacked_vector(v) for v in vectors], axis=1)
        right = jnp.concatenate([ref[index] for ref, index in weights], axis=0)
        return folded(dot(left, right))

    def by(vector, place):
        ref, index = place
        return folded(dot(stacked_vector(vector), ref[index]))

    def forward_node(size, first):
        return tn, node(size, cells, first)

    def backward_node(size, first):
        return tb, node(size, cells, cells - first - size)

    def climb(source, at, whole):
        sums, source = {}, list(source)
        for p in range(0, cells, 2):
            source[p + 1] = source[p + 1] + by(source[p], at(1, p))
        for p in range(0, cells, 2):
            sums[2, p] = by(source[p + 1], at(1, p + 1))
        size = 2
        while size < cells // 2 or (whole and size < cells):
            for p in range(0, cells, 2 * size):
                sums[2 * size, p] = sums[size, p + size] + by(sums[size, p], at(size, p + size))
            size *= 2
        return source, sums

    def descend(source, sums, at):
        entering = {0: None}
        size = cells // 2
        while size >= 2:
            for p in range(0, cells, 2 * size):
                after = sums[size, p]
                if entering[p] is not None:
                    after = after + by(entering[p], at(size, p))
                entering[p + size] = after
            size //= 2
        values = list(source)
        for p in range(0, cells, 2):
            if entering[p] is not None:
                values[p] = values[p] + entering[p]
                values[p + 1] = values[p + 1] + by(entering[p], at(1, p))
        return values

    row = lax.broadcasted_iota(jnp.int32, (ROWS, LANES), 0)
    column = lax.broadcasted_iota(jnp.int32, (ROWS, LANES), 1)
    unit = jnp.where((row == column) & (row < NV), 1.0, 0.0).astype(F32)
    put(kw, 0, unit)
    put(jw, cells - 1, unit)
    ew[0] = tb[0]
    hsum[...] = jnp.zeros_like(hsum)
    came[0] = jnp.zeros_like(came[0])

    @pl.when(me >= 1)
    def _():
        put(phi, 1, unit)

    @pl.when(me <= n - 2)
    def _():
        put(phi, n - 1, unit)

    def keep_alone(source, sums):
        for i, value in enumerate(descend(source, sums, forward_node)):
            zs[i] = value

    loads[3].wait()
    blocks = load_cells(rhs_ref, pad)
    for i in range(cells):
        src[i] = blocks[i * NR : (i + 1) * NR]
    source, sums = climb([src[i] for i in range(cells)], forward_node, True)
    fsend[0] = sums[cells, 0]
    send_f(0)
    keep_alone(source, sums)

    from_before = jnp.maximum(me - 1, 0)
    from_after = jnp.maximum(n - 2 - me, 0)

    def times_pivot(table, i):
        exact = pivot[i]
        return dot(left_of((table, i)), jnp.concatenate([exact, exact], axis=0))

    def extended(slot):
        high, low = parts(unpacked(came[slot]))
        return multiply(jnp.concatenate([high, low], axis=1), right_of((phi, slot)))

    def tables(step, _):
        arrived = step <= from_before
        slot = jnp.where(arrived, step, 0)
        towards = jnp.where(arrived, step + 1, n)

        @pl.when(arrived)
        def _():
            map_copy(0, slot, me).wait_recv()

        chained = extended(slot)
        back = cells - 1 - step
        k = multiply(left_of((kw, step - 1)), right_of((tn, step - 1)))
        e = multiply(left_of((tb, step)), right_of((ew, step - 1)))
        j = multiply(left_of((jw, back + 1)), right_of((tb, back + 1)))
        h = multiply(left_of((kw, step - 1)), right_of((ew, step - 1)))
        put(jp, back + 1, times_pivot(jw, back + 1))
        put(phi, towards, chained)
        put(kw, step, k)
        put(ew, step, e)
        put(jw, back, j)
        hsum[...] += h
        return 0

    lax.fori_loop(1, cells, tables, 0)
    put(jp, 0, times_pivot(jw, 0))
    put(hw, 0, hsum[...] + multiply(left_of((kw, cells - 1)), right_of((ew, cells - 1))))

    between = [(phi, k) for k in range(n)]

    def answer_copy(slot, target):
        return pltpu.make_async_remote_copy(
            src_ref=answers.at[slot],
            dst_ref=answered.at[slot],
            send_sem=answer_out.at[slot],
            recv_sem=answer_in.at[slot],
            device_id={"narrow": target},
            device_id_type=MESH,
        )

    def send_answers():
        high_low = jnp.concatenate([left_of((phi, k)) for k in range(1, n)], axis=0)
        products = multiply(high_low, right_of((hw, 0)))
        for k in range(1, n):
            answers[n - k] = packed(products[(k - 1) * ROWS : k * ROWS])

        def send(step, _):
            answer_copy(n - step, me - step).start()
            return 0

        lax.fori_loop(1, me + 1, send, 0)

    def take_answers():
        def wait(step, _):
            answer_copy(n - step, me).wait_recv()
            return 0

        lax.fori_loop(1, n - me, wait, 0)
        left = []
        for k in range(1, n):
            high, low = parts(unpacked(answered[k]))
            left += [high, low]
        put(
            rho,
            0,
            multiply(
                jnp.concatenate(left, axis=1),
                jnp.concatenate([right_of((phi, k)) for k in range(1, n)], axis=0),
            ),
        )
        put(rho, 1, multiply(left_of((rho, 0)), right_of((tb, whole))))
        put(rho, 2, multiply(left_of((tn, whole)), right_of((rho, 0))))

    def inside(turn, z):
        source, sums = climb(z[::-1], backward_node, False)
        for p, u in enumerate(descend(source, sums, backward_node)):
            i = cells - 1 - p
            product = dot(stacked_vector(u), pivot[i])
            xs[turn, i] = product[:NR] + product[NR:]

    def complete(turn, entering, table):
        left = stacked_vector(entering)
        for i in range(cells):
            xs[turn, i] = xs[turn, i] + folded(dot(left, table[i]))

    def backward_alone():
        return deep([zs[i] for i in range(cells)], [(ew, i) for i in range(cells)])

    alone = backward_alone()
    wait_f(0)
    left = stacked_vector(deep([fcame[0, k] for k in range(n)], between))
    gsend[0] = alone + folded(dot(left, hw[0]))
    send_g(0)
    send_answers()
    inside(0, [z + folded(dot(left, kw[i])) for i, z in enumerate(zs[i] for i in range(cells))])

    def chain_back(step, _):
        slot = n - step
        map_copy(1, slot, me).wait_recv()
        put(phi, slot - 1, extended(slot))
        return 0

    lax.fori_loop(1, from_after + 1, chain_back, 0)
    wait_g(0)
    complete(0, deep([gcame[0, k] for k in range(n)], between), jp)

    def halo_copy(side, other):
        return pltpu.make_async_remote_copy(
            src_ref=xs.at[0],
            dst_ref=halo.at[side],
            send_sem=halo_out.at[side],
            recv_sem=halo_in.at[side],
            device_id={"wide": other},
            device_id_type=MESH,
        )

    halo_copy(0, high_line).start()
    halo_copy(1, low_line).start()

    store_cells(xs[0].reshape(cells * NR, LANES), first_ref)

    loads[4].wait()
    weights = []
    for place in range(3):
        total = jnp.zeros((cells, NV), F32)
        for side in range(2):
            relative = lax.rem(face_ref[0, side] - line + 1 + lines, lines)
            total = total + jnp.where(
                relative == place, coef_ref[:, pl.ds(side * NV, NV)], 0.0
            )
        weights.append(jnp.concatenate([total, jnp.zeros((cells, LANES - NV), F32)], axis=1))

    def drain(step, _):
        @pl.when(me + step < n)
        def _():
            f_copy(0, step, me + step).wait_send()

        @pl.when(me - step >= 0)
        def _():
            g_copy(0, n - step, me - step).wait_send()

        @pl.when((me >= 1) & (me + step < n))
        def _():
            map_copy(0, step, me + step).wait_send()

        @pl.when((me <= n - 2) & (me - step >= 0))
        def _():
            map_copy(1, n - step, me - step).wait_send()

        return 0

    lax.fori_loop(1, n, drain, 0)

    def last_n(m):
        return (tn, node(m, cells, cells - m)) if low_bit(m) == m else (qw, m)

    for m in range(1, cells):
        size = low_bit(m)
        if size != m:
            first = node(size, cells, cells - m)
            put(qw, m, multiply(left_of((tn, first)), right_of(last_n(m - size))))

    ku[cells - 1] = kw[cells - 1]

    def respond(step, _):
        back = cells - 1 - step
        own = left_of((kw, back))
        own = own[:, :LANES].astype(F32) + own[:, LANES:].astype(F32)
        put(ku, back, own + multiply(left_of((ku, back + 1)), right_of((tb, back + 1))))
        put(kx, back + 1, times_pivot(ku, back + 1))
        return 0

    lax.fori_loop(1, cells, respond, 0)
    put(kx, 0, times_pivot(ku, 0))
    take_answers()

    halo_copy(0, high_line).wait_recv()
    halo_copy(1, low_line).wait_recv()

    for i in range(cells):
        coupled = (
            weights[0][i : i + 1] * halo[0, i]
            + weights[1][i : i + 1] * xs[0, i]
            + weights[2][i : i + 1] * halo[1, i]
        )
        src[i] = src[i] - coupled

    leaving = deep([src[i] for i in range(cells)], [last_n(cells - i) for i in range(cells)])
    fsend[1] = leaving
    send_f(1)
    keep_alone(*climb([src[i] for i in range(cells)], forward_node, False))
    gsend[1] = backward_alone() + by(leaving, (rho, 1))
    send_g(1)
    inside(1, [zs[i] for i in range(cells)])
    wait_f(1)
    entering = deep([fcame[1, k] for k in range(n)], between)
    complete(1, entering, kx)
    back = by(leaving, (rho, 0)) + by(entering, (rho, 2))
    halo_copy(0, high_line).wait_send()
    halo_copy(1, low_line).wait_send()

    def drain_last(step, _):
        @pl.when(me + step < n)
        def _():
            f_copy(1, step, me + step).wait_send()

        @pl.when(me - step >= 0)
        def _():
            g_copy(1, n - step, me - step).wait_send()
            answer_copy(n - step, me - step).wait_send()

        return 0

    lax.fori_loop(1, n, drain_last, 0)
    wait_g(1)
    complete(1, back + deep([gcame[1, k] for k in range(n)], between), jp)
    store_cells(xs[1].reshape(cells * NR, LANES), second_ref)


def body(n, lines, rhs, pivot, upper, lower, neighbors, coupling):
    cells = rhs.shape[1]
    matrix = (LANES, 2 * LANES)
    tree = pltpu.VMEM((2 * cells - 1, *matrix), BF16)
    weight = pltpu.VMEM((cells, *matrix), BF16)
    vectors = pltpu.VMEM((cells, NR, LANES), F32)
    vmem = pl.BlockSpec(memory_space=pltpu.VMEM)
    hbm = pl.BlockSpec(memory_space=pltpu.HBM)
    dma = pltpu.SemaphoreType.DMA

    def in_hbm(x):
        return pltpu.with_memory_space_constraint(x, pltpu.HBM)

    first, second = pl.pallas_call(
        functools.partial(kernel, n, lines),
        out_shape=[pltpu.VMEM((cells, NV * NR), F32)] * 2,
        in_specs=[hbm] * 4 + [pl.BlockSpec(memory_space=pltpu.SMEM), hbm],
        out_specs=[vmem] * 2,
        scratch_shapes=[
            pltpu.VMEM((3, cells, NV * NV), BF16),
            pltpu.VMEM((cells, NV * NR), F32),
            pltpu.VMEM((cells, 2 * NV), F32),
            pltpu.VMEM((3, ROWS * (cells + 1), LANES), F32),
            pltpu.VMEM((LANES, LANES), F32),
            pltpu.VMEM((cells, LANES, LANES), BF16),
            tree,
            tree,
            weight,
            weight,
            weight,
            weight,
            weight,
            weight,
            weight,
            pltpu.VMEM((1, *matrix), BF16),
            pltpu.VMEM((ROWS, LANES), F32),
            pltpu.VMEM((3, *matrix), BF16),
            pltpu.VMEM((2, PACKED, LANES), F32),
            pltpu.VMEM((n, PACKED, LANES), F32),
            pltpu.VMEM((n, PACKED, LANES), F32),
            pltpu.VMEM((n, PACKED, LANES), F32),
            pltpu.VMEM((n + 1, *matrix), BF16),
            vectors,
            vectors,
            pltpu.VMEM((2, cells, NR, LANES), F32),
            pltpu.VMEM((2, cells, NR, LANES), F32),
            pltpu.VMEM((2, NR, LANES), F32),
            pltpu.VMEM((2, NR, LANES), F32),
            pltpu.VMEM((2, n, NR, LANES), F32),
            pltpu.VMEM((2, n, NR, LANES), F32),
            dma((5,)),
            dma((n,)),
            dma((n,)),
            dma((n,)),
            dma((n,)),
            dma((2, n)),
            dma((2, n)),
            dma((2, n)),
            dma((2, n)),
            dma((2,)),
            dma((2,)),
        ],
        compiler_params=pltpu.CompilerParams(
            collective_id=0, has_side_effects=True, vmem_limit_bytes=40 * 1024 * 1024
        ),
    )(*(in_hbm(x) for x in (pivot[0], upper[0], lower[0], rhs[0], neighbors, coupling[0])))
    return first[None], second[None]


def solution(mesh):
    blocks = P("wide", "narrow", None)
    return jax.shard_map(
        functools.partial(body, mesh.shape["narrow"], mesh.shape["wide"]),
        mesh=mesh,
        in_specs=(blocks, blocks, blocks, blocks, P("wide", None), blocks),
        out_specs=(blocks, blocks),
        check_vma=False,
    )
```

```python
import functools

import jax
import jax.numpy as jnp
from jax import lax
from jax.experimental import pallas as pl
from jax.experimental.pallas import tpu as pltpu
from jax.sharding import PartitionSpec as P

NV = 95
NR = 8
ROWS = 96
PACKED = 72
LANES = 128
F32 = jnp.float32
BF16 = jnp.bfloat16
MESH = pl.DeviceIdType.MESH


def dot(left, right):
    return jnp.dot(left, right, preferred_element_type=F32)


def parts(value):
    high = value.astype(BF16)
    return high, (value - high.astype(F32)).astype(BF16)


def stacked_vector(value):
    high = value.astype(BF16).astype(F32)
    return jnp.concatenate([high, value - high], axis=0).astype(BF16)


def folded(product):
    rows = product.shape[0] // 2
    return product[:rows, :LANES] + (product[:rows, LANES:] + product[rows:, :LANES])


def put(ref, index, value):
    high, low = parts(value)
    ref[index, pl.ds(0, ROWS), pl.ds(0, LANES)] = high
    ref[index, pl.ds(0, ROWS), pl.ds(LANES, LANES)] = low


def left_of(place):
    ref, index = place
    return ref[index, pl.ds(0, ROWS), :]


def right_of(place):
    ref, index = place
    value = ref[index]
    return jnp.concatenate([value, value], axis=0)


def multiply(left, right):
    product = dot(left, right)
    return product[:, :LANES] + product[:, LANES:]


def packed(value):
    top, rest = value[:PACKED], value[PACKED:]
    lane = lax.broadcasted_iota(jnp.int32, rest.shape, 1)
    pieces = []
    for part in range(3):
        moved = pltpu.roll(rest, (ROWS - 32 * part) % LANES, 1)
        pieces.append(jnp.where(lane >= ROWS, moved, top[24 * part : 24 * part + 24]))
    return jnp.concatenate(pieces, axis=0)


def unpacked(value):
    lane = lax.broadcasted_iota(jnp.int32, (24, LANES), 1)
    rest = jnp.zeros((24, LANES), F32)
    pieces = []
    for part in range(3):
        own = value[24 * part : 24 * part + 24]
        moved = pltpu.roll(own, (LANES - ROWS + 32 * part) % LANES, 1)
        rest = jnp.where((lane >= 32 * part) & (lane < 32 * part + 32), moved, rest)
        pieces.append(jnp.where(lane < ROWS, own, 0.0))
    return jnp.concatenate(pieces + [rest], axis=0)


def granule_transpose(value):
    row = lax.broadcasted_iota(jnp.int32, value.shape, 0)
    group = lax.broadcasted_iota(jnp.int32, value.shape, 1) // NR
    height = value.shape[0]
    for bit in (1, 2, 4, 8):
        row_set = (row & bit) != 0
        group_set = (group & bit) != 0
        down = pltpu.roll(pltpu.roll(value, bit, 0), LANES - NR * bit, 1)
        up = pltpu.roll(pltpu.roll(value, height - bit, 0), NR * bit, 1)
        value = jnp.where(row_set == group_set, value, jnp.where(row_set, down, up))
    return value


def load_cells(flat_ref, pad_ref):
    cells = flat_ref.shape[0]
    width = NV * NR
    pad_ref[...] = jnp.zeros_like(pad_ref)
    for block in range(ROWS // 16):
        first = block * LANES
        wide = min(LANES, width - first)
        pad_ref[pl.ds(block * 16, cells), pl.ds(0, wide)] = flat_ref[:, pl.ds(first, wide)]
    turned = granule_transpose(pad_ref[pl.ds(0, ROWS), :])
    pad_ref[pl.ds(0, ROWS), :] = turned
    return jnp.transpose(pad_ref[...])


def store_cells(blocks, flat_ref):
    width = NV * NR
    cells = flat_ref.shape[0]
    turned = granule_transpose(jnp.transpose(blocks)[:ROWS])
    for block in range(ROWS // 16):
        first = block * LANES
        wide = min(LANES, width - first)
        flat_ref[:, pl.ds(first, wide)] = turned[block * 16 : block * 16 + cells, :wide]


def mixed_near_first(n):
    early = {4: 1.5, 8: 4.5, 12: 8.5}
    return sorted(range(1, n), key=lambda step: early.get(step, step))


def far_first(n):
    return sorted(range(1, n), key=lambda step: -sum(min(d, 4 - d) for d in (step % 4, step // 4 % 4)))


def low_bit(m):
    return m & -m


def node(level_size, cells, first):
    return 2 * cells - 2 * cells // level_size + first // level_size


def kernel(
    n,
    lines,
    pivot_hbm,
    upper_hbm,
    lower_hbm,
    rhs_hbm,
    face_ref,
    coef_hbm,
    first_ref,
    second_ref,
    flat,
    rhs_ref,
    coef_ref,
    slab,
    pad,
    pivot,
    tn,
    tb,
    qw,
    ew,
    kw,
    jw,
    jp,
    hw,
    hsum,
    rho,
    maps,
    came,
    answers,
    answered,
    phi,
    src,
    zs,
    xs,
    halo,
    fsend,
    gsend,
    fcame,
    gcame,
    load_sem,
    map_out,
    map_in,
    answer_out,
    answer_in,
    f_out,
    f_in,
    g_out,
    g_in,
    halo_out,
    halo_in,
):
    cells = rhs_ref.shape[0]
    me = lax.axis_index("narrow")
    line = lax.axis_index("wide")
    low_line = lax.rem(line + lines - 1, lines)
    high_line = lax.rem(line + 1, lines)

    loads = [
        pltpu.make_async_copy(hbm, flat.at[number], load_sem.at[number])
        for number, hbm in enumerate((pivot_hbm, upper_hbm, lower_hbm))
    ]
    loads.append(pltpu.make_async_copy(rhs_hbm, rhs_ref, load_sem.at[3]))
    loads.append(pltpu.make_async_copy(coef_hbm, coef_ref, load_sem.at[4]))
    for load in loads:
        load.start()

    fcame[...] = jnp.zeros_like(fcame)
    gcame[...] = jnp.zeros_like(gcame)
    answered[...] = jnp.zeros_like(answered)

    barrier = pltpu.get_barrier_semaphore()

    def greet(step, _):
        pl.semaphore_signal(
            barrier, inc=1, device_id={"narrow": lax.rem(me + step, n)}, device_id_type=MESH
        )
        return 0

    lax.fori_loop(1, n, greet, 0)
    for other in (low_line, high_line):
        pl.semaphore_signal(barrier, inc=1, device_id={"wide": other}, device_id_type=MESH)

    slab[...] = jnp.zeros_like(slab)
    tail = jnp.zeros((LANES - ROWS, 2 * LANES), BF16)

    def clear_nodes(i, _):
        for ref in (tn, tb):
            ref[i, pl.ds(ROWS, LANES - ROWS), :] = tail
        return 0

    lax.fori_loop(0, 2 * cells - 1, clear_nodes, 0)

    def clear(i, _):
        for ref in (qw, ew, kw, jw, jp):
            ref[i, pl.ds(ROWS, LANES - ROWS), :] = tail
        return 0

    lax.fori_loop(0, cells, clear, 0)
    hw[0, pl.ds(ROWS, LANES - ROWS), :] = tail
    for i in range(3):
        rho[i, pl.ds(ROWS, LANES - ROWS), :] = tail

    def clear_phi(i, _):
        phi[i] = jnp.zeros((LANES, 2 * LANES), BF16)
        return 0

    lax.fori_loop(0, n, clear_phi, 0)

    for number in range(3):
        loads[number].wait()
        for row in range(NV):
            slab[number, pl.ds(row * (cells + 1), cells), pl.ds(0, NV)] = flat[
                number, :, pl.ds(row * NV, NV)
            ].astype(F32)

    no_rows = jnp.zeros((LANES - ROWS, LANES), BF16)

    for i in range(cells):
        p, u, l = (
            slab[number, pl.ds(i, ROWS, stride=cells + 1), :] for number in range(3)
        )
        p16 = p.astype(BF16)
        pivot[i] = jnp.concatenate([p16, no_rows], axis=0)
        right = jnp.concatenate([(-u).astype(BF16), (-l).astype(BF16)], axis=1)
        right = jnp.concatenate([right, tail], axis=0)
        both = dot(p16, right)
        put(tn, i, both[:, :LANES])
        put(tb, i, both[:, LANES:])

    last = cells - 2
    whole = cells + last
    for place in range(last):
        put(tn, cells + place, multiply(left_of((tn, 2 * place)), right_of((tn, 2 * place + 1))))
    forward = multiply(left_of((tn, 2 * last)), right_of((tn, 2 * last + 1)))
    maps[0] = packed(forward)

    pl.semaphore_wait(barrier, n - 1 + 2)

    def map_copy(which, slot, target):
        return pltpu.make_async_remote_copy(
            src_ref=maps.at[which],
            dst_ref=came.at[slot],
            send_sem=map_out.at[slot],
            recv_sem=map_in.at[slot],
            device_id={"narrow": target},
            device_id_type=MESH,
        )

    for step in mixed_near_first(n):

        @pl.when((me >= 1) & (me + step < n))
        def _():
            map_copy(0, step, me + step).start()

    for place in range(last):
        put(tb, cells + place, multiply(left_of((tb, 2 * place + 1)), right_of((tb, 2 * place))))
    backward = multiply(left_of((tb, 2 * last + 1)), right_of((tb, 2 * last)))
    maps[1] = packed(backward)
    for step in mixed_near_first(n):

        @pl.when((me <= n - 2) & (me - step >= 0))
        def _():
            map_copy(1, n - step, me - step).start()

    put(tn, whole, forward)
    put(tb, whole, backward)

    def offset_copy(source, target_ref, turn, slot, out, arrived, target):
        return pltpu.make_async_remote_copy(
            src_ref=source.at[turn],
            dst_ref=target_ref.at[turn, slot],
            send_sem=out.at[turn, slot],
            recv_sem=arrived.at[turn, slot],
            device_id={"narrow": target},
            device_id_type=MESH,
        )

    def f_copy(turn, slot, target):
        return offset_copy(fsend, fcame, turn, slot, f_out, f_in, target)

    def g_copy(turn, slot, target):
        return offset_copy(gsend, gcame, turn, slot, g_out, g_in, target)

    def send_f(turn):
        for step in far_first(n):

            @pl.when(me + step < n)
            def _():
                f_copy(turn, step, me + step).start()

    def send_g(turn):
        for step in far_first(n):

            @pl.when(me - step >= 0)
            def _():
                g_copy(turn, n - step, me - step).start()

    def wait_f(turn):
        for step in range(1, n):

            @pl.when(step <= me)
            def _():
                f_copy(turn, step, me).wait_recv()

    def wait_g(turn):
        for step in range(1, n):

            @pl.when(me + step < n)
            def _():
                g_copy(turn, n - step, me).wait_recv()

    def deep(vectors, weights):
        left = jnp.concatenate([stacked_vector(v) for v in vectors], axis=1)
        right = jnp.concatenate([ref[index] for ref, index in weights], axis=0)
        return folded(dot(left, right))

    def by(vector, place):
        ref, index = place
        return folded(dot(stacked_vector(vector), ref[index]))

    def forward_node(size, first):
        return tn, node(size, cells, first)

    def backward_node(size, first):
        return tb, node(size, cells, cells - first - size)

    def climb(source, at, whole):
        sums, source = {}, list(source)
        for p in range(0, cells, 2):
            source[p + 1] = source[p + 1] + by(source[p], at(1, p))
        for p in range(0, cells, 2):
            sums[2, p] = by(source[p + 1], at(1, p + 1))
        size = 2
        while size < cells // 2 or (whole and size < cells):
            for p in range(0, cells, 2 * size):
                sums[2 * size, p] = sums[size, p + size] + by(sums[size, p], at(size, p + size))
            size *= 2
        return source, sums

    def descend(source, sums, at):
        entering = {0: None}
        size = cells // 2
        while size >= 2:
            for p in range(0, cells, 2 * size):
                after = sums[size, p]
                if entering[p] is not None:
                    after = after + by(entering[p], at(size, p))
                entering[p + size] = after
            size //= 2
        values = list(source)
        for p in range(0, cells, 2):
            if entering[p] is not None:
                values[p] = values[p] + entering[p]
                values[p + 1] = values[p + 1] + by(entering[p], at(1, p))
        return values

    row = lax.broadcasted_iota(jnp.int32, (ROWS, LANES), 0)
    column = lax.broadcasted_iota(jnp.int32, (ROWS, LANES), 1)
    unit = jnp.where((row == column) & (row < NV), 1.0, 0.0).astype(F32)
    put(kw, 0, unit)
    put(jw, cells - 1, unit)
    ew[0] = tb[0]
    hsum[...] = jnp.zeros_like(hsum)
    came[0] = jnp.zeros_like(came[0])

    @pl.when(me >= 1)
    def _():
        put(phi, 1, unit)

    @pl.when(me <= n - 2)
    def _():
        put(phi, n - 1, unit)

    def keep_alone(source, sums):
        for i, value in enumerate(descend(source, sums, forward_node)):
            zs[i] = value

    loads[3].wait()
    blocks = load_cells(rhs_ref, pad)
    for i in range(cells):
        src[i] = blocks[i * NR : (i + 1) * NR]
    source, sums = climb([src[i] for i in range(cells)], forward_node, True)
    fsend[0] = sums[cells, 0]
    send_f(0)
    keep_alone(source, sums)

    from_before = jnp.maximum(me - 1, 0)
    from_after = jnp.maximum(n - 2 - me, 0)

    def with_pivot(i):
        exact = pivot[i]
        put(jp, i, dot(left_of((jw, i)), jnp.concatenate([exact, exact], axis=0)))

    def extended(slot):
        high, low = parts(unpacked(came[slot]))
        return multiply(jnp.concatenate([high, low], axis=1), right_of((phi, slot)))

    def tables(step, _):
        arrived = step <= from_before
        slot = jnp.where(arrived, step, 0)
        towards = jnp.where(arrived, step + 1, n)

        @pl.when(arrived)
        def _():
            map_copy(0, slot, me).wait_recv()

        chained = extended(slot)
        back = cells - 1 - step
        k = multiply(left_of((kw, step - 1)), right_of((tn, step - 1)))
        e = multiply(left_of((tb, step)), right_of((ew, step - 1)))
        j = multiply(left_of((jw, back + 1)), right_of((tb, back + 1)))
        h = multiply(left_of((kw, step - 1)), right_of((ew, step - 1)))
        with_pivot(back + 1)
        put(phi, towards, chained)
        put(kw, step, k)
        put(ew, step, e)
        put(jw, back, j)
        hsum[...] += h
        return 0

    lax.fori_loop(1, cells, tables, 0)
    with_pivot(0)
    put(hw, 0, hsum[...] + multiply(left_of((kw, cells - 1)), right_of((ew, cells - 1))))

    between = [(phi, k) for k in range(n)]

    def answer_copy(slot, target):
        return pltpu.make_async_remote_copy(
            src_ref=answers.at[slot],
            dst_ref=answered.at[slot],
            send_sem=answer_out.at[slot],
            recv_sem=answer_in.at[slot],
            device_id={"narrow": target},
            device_id_type=MESH,
        )

    def send_answers():
        high_low = jnp.concatenate([left_of((phi, k)) for k in range(1, n)], axis=0)
        products = multiply(high_low, right_of((hw, 0)))
        for k in range(1, n):
            answers[n - k] = packed(products[(k - 1) * ROWS : k * ROWS])

        def send(step, _):
            answer_copy(n - step, me - step).start()
            return 0

        lax.fori_loop(1, me + 1, send, 0)

    def take_answers():
        def wait(step, _):
            answer_copy(n - step, me).wait_recv()
            return 0

        lax.fori_loop(1, n - me, wait, 0)
        left = []
        for k in range(1, n):
            high, low = parts(unpacked(answered[k]))
            left += [high, low]
        put(
            rho,
            0,
            multiply(
                jnp.concatenate(left, axis=1),
                jnp.concatenate([right_of((phi, k)) for k in range(1, n)], axis=0),
            ),
        )
        put(rho, 1, multiply(left_of((rho, 0)), right_of((tb, whole))))
        put(rho, 2, multiply(left_of((tn, whole)), right_of((rho, 0))))

    def inside(turn, left):
        z = [zs[i] + folded(dot(left, kw[i])) for i in range(cells)]
        source, sums = climb(z[::-1], backward_node, False)
        for p, u in enumerate(descend(source, sums, backward_node)):
            i = cells - 1 - p
            product = dot(stacked_vector(u), pivot[i])
            xs[turn, i] = product[:NR] + product[NR:]

    def complete(turn, entering):
        left = stacked_vector(entering)
        for i in range(cells):
            xs[turn, i] = xs[turn, i] + folded(dot(left, jp[i]))

    def backward_alone():
        return deep([zs[i] for i in range(cells)], [(ew, i) for i in range(cells)])

    alone = backward_alone()
    wait_f(0)
    left = stacked_vector(deep([fcame[0, k] for k in range(n)], between))
    gsend[0] = alone + folded(dot(left, hw[0]))
    send_g(0)
    send_answers()
    inside(0, left)

    def chain_back(step, _):
        slot = n - step
        map_copy(1, slot, me).wait_recv()
        put(phi, slot - 1, extended(slot))
        return 0

    lax.fori_loop(1, from_after + 1, chain_back, 0)
    wait_g(0)
    complete(0, deep([gcame[0, k] for k in range(n)], between))

    def halo_copy(side, other):
        return pltpu.make_async_remote_copy(
            src_ref=xs.at[0],
            dst_ref=halo.at[side],
            send_sem=halo_out.at[side],
            recv_sem=halo_in.at[side],
            device_id={"wide": other},
            device_id_type=MESH,
        )

    halo_copy(0, high_line).start()
    halo_copy(1, low_line).start()

    loads[4].wait()
    weights = []
    for place in range(3):
        total = jnp.zeros((cells, NV), F32)
        for side in range(2):
            relative = lax.rem(face_ref[0, side] - line + 1 + lines, lines)
            total = total + jnp.where(
                relative == place, coef_ref[:, pl.ds(side * NV, NV)], 0.0
            )
        weights.append(jnp.concatenate([total, jnp.zeros((cells, LANES - NV), F32)], axis=1))

    def last_n(m):
        return (tn, node(m, cells, cells - m)) if low_bit(m) == m else (qw, m)

    for m in range(1, cells):
        size = low_bit(m)
        if size != m:
            first = node(size, cells, cells - m)
            put(qw, m, multiply(left_of((tn, first)), right_of(last_n(m - size))))

    @pl.when(me >= n // 2)
    def _():
        take_answers()

    halo_copy(0, high_line).wait_recv()
    halo_copy(1, low_line).wait_recv()

    for i in range(cells):
        coupled = (
            weights[0][i : i + 1] * halo[0, i]
            + weights[1][i : i + 1] * xs[0, i]
            + weights[2][i : i + 1] * halo[1, i]
        )
        src[i] = src[i] - coupled

    leaving = deep([src[i] for i in range(cells)], [last_n(cells - i) for i in range(cells)])
    fsend[1] = leaving
    send_f(1)

    @pl.when(me < n // 2)
    def _():
        take_answers()

    keep_alone(*climb([src[i] for i in range(cells)], forward_node, False))
    gsend[1] = backward_alone() + by(leaving, (rho, 1))
    send_g(1)
    store_cells(xs[0].reshape(cells * NR, LANES), first_ref)
    wait_f(1)
    left = stacked_vector(deep([fcame[1, k] for k in range(n)], between))
    inside(1, left)
    back = by(leaving, (rho, 0)) + folded(dot(left, rho[2]))
    halo_copy(0, high_line).wait_send()
    halo_copy(1, low_line).wait_send()

    def drain(step, _):
        @pl.when(me + step < n)
        def _():
            f_copy(0, step, me + step).wait_send()
            f_copy(1, step, me + step).wait_send()

        @pl.when((me >= 1) & (me + step < n))
        def _():
            map_copy(0, step, me + step).wait_send()

        @pl.when((me <= n - 2) & (me - step >= 0))
        def _():
            map_copy(1, n - step, me - step).wait_send()

        @pl.when(me - step >= 0)
        def _():
            g_copy(0, n - step, me - step).wait_send()
            g_copy(1, n - step, me - step).wait_send()
            answer_copy(n - step, me - step).wait_send()

        return 0

    lax.fori_loop(1, n, drain, 0)
    wait_g(1)
    complete(1, back + deep([gcame[1, k] for k in range(n)], between))
    store_cells(xs[1].reshape(cells * NR, LANES), second_ref)


def body(n, lines, rhs, pivot, upper, lower, neighbors, coupling):
    cells = rhs.shape[1]
    matrix = (LANES, 2 * LANES)
    tree = pltpu.VMEM((2 * cells - 1, *matrix), BF16)
    weight = pltpu.VMEM((cells, *matrix), BF16)
    vectors = pltpu.VMEM((cells, NR, LANES), F32)
    vmem = pl.BlockSpec(memory_space=pltpu.VMEM)
    hbm = pl.BlockSpec(memory_space=pltpu.HBM)
    dma = pltpu.SemaphoreType.DMA

    def in_hbm(x):
        return pltpu.with_memory_space_constraint(x, pltpu.HBM)

    first, second = pl.pallas_call(
        functools.partial(kernel, n, lines),
        out_shape=[pltpu.VMEM((cells, NV * NR), F32)] * 2,
        in_specs=[hbm] * 4 + [pl.BlockSpec(memory_space=pltpu.SMEM), hbm],
        out_specs=[vmem] * 2,
        scratch_shapes=[
            pltpu.VMEM((3, cells, NV * NV), BF16),
            pltpu.VMEM((cells, NV * NR), F32),
            pltpu.VMEM((cells, 2 * NV), F32),
            pltpu.VMEM((3, ROWS * (cells + 1), LANES), F32),
            pltpu.VMEM((LANES, LANES), F32),
            pltpu.VMEM((cells, LANES, LANES), BF16),
            tree,
            tree,
            weight,
            weight,
            weight,
            weight,
            weight,
            pltpu.VMEM((1, *matrix), BF16),
            pltpu.VMEM((ROWS, LANES), F32),
            pltpu.VMEM((3, *matrix), BF16),
            pltpu.VMEM((2, PACKED, LANES), F32),
            pltpu.VMEM((n, PACKED, LANES), F32),
            pltpu.VMEM((n, PACKED, LANES), F32),
            pltpu.VMEM((n, PACKED, LANES), F32),
            pltpu.VMEM((n + 1, *matrix), BF16),
            vectors,
            vectors,
            pltpu.VMEM((2, cells, NR, LANES), F32),
            pltpu.VMEM((2, cells, NR, LANES), F32),
            pltpu.VMEM((2, NR, LANES), F32),
            pltpu.VMEM((2, NR, LANES), F32),
            pltpu.VMEM((2, n, NR, LANES), F32),
            pltpu.VMEM((2, n, NR, LANES), F32),
            dma((5,)),
            dma((n,)),
            dma((n,)),
            dma((n,)),
            dma((n,)),
            dma((2, n)),
            dma((2, n)),
            dma((2, n)),
            dma((2, n)),
            dma((2,)),
            dma((2,)),
        ],
        compiler_params=pltpu.CompilerParams(
            collective_id=0, has_side_effects=True, vmem_limit_bytes=40 * 1024 * 1024
        ),
    )(*(in_hbm(x) for x in (pivot[0], upper[0], lower[0], rhs[0], neighbors, coupling[0])))
    return first[None], second[None]


def solution(mesh):
    blocks = P("wide", "narrow", None)
    return jax.shard_map(
        functools.partial(body, mesh.shape["narrow"], mesh.shape["wide"]),
        mesh=mesh,
        in_specs=(blocks, blocks, blocks, blocks, P("wide", None), blocks),
        out_specs=(blocks, blocks),
        check_vma=False,
    )
```

```python
import functools

import jax
import jax.numpy as jnp
from jax import lax
from jax.experimental import pallas as pl
from jax.experimental.pallas import tpu as pltpu
from jax.sharding import PartitionSpec as P

NV = 95
NR = 8
ROWS = 96
PACKED = 72
LANES = 128
F32 = jnp.float32
BF16 = jnp.bfloat16
MESH = pl.DeviceIdType.MESH


def dot(left, right):
    return jnp.dot(left, right, preferred_element_type=F32)


def parts(value):
    high = value.astype(BF16)
    return high, (value - high.astype(F32)).astype(BF16)


def stacked_vector(value):
    high = value.astype(BF16).astype(F32)
    return jnp.concatenate([high, value - high], axis=0).astype(BF16)


def folded(product):
    rows = product.shape[0] // 2
    return product[:rows, :LANES] + (product[:rows, LANES:] + product[rows:, :LANES])


def put(ref, index, value):
    high, low = parts(value)
    ref[index, pl.ds(0, ROWS), pl.ds(0, LANES)] = high
    ref[index, pl.ds(0, ROWS), pl.ds(LANES, LANES)] = low


def left_of(place):
    ref, index = place
    return ref[index, pl.ds(0, ROWS), :]


def right_of(place):
    ref, index = place
    value = ref[index]
    return jnp.concatenate([value, value], axis=0)


def multiply(left, right):
    product = dot(left, right)
    return product[:, :LANES] + product[:, LANES:]


def packed(value):
    top, rest = value[:PACKED], value[PACKED:]
    lane = lax.broadcasted_iota(jnp.int32, rest.shape, 1)
    pieces = []
    for part in range(3):
        moved = pltpu.roll(rest, (ROWS - 32 * part) % LANES, 1)
        pieces.append(jnp.where(lane >= ROWS, moved, top[24 * part : 24 * part + 24]))
    return jnp.concatenate(pieces, axis=0)


def unpacked(value):
    lane = lax.broadcasted_iota(jnp.int32, (24, LANES), 1)
    rest = jnp.zeros((24, LANES), F32)
    pieces = []
    for part in range(3):
        own = value[24 * part : 24 * part + 24]
        moved = pltpu.roll(own, (LANES - ROWS + 32 * part) % LANES, 1)
        rest = jnp.where((lane >= 32 * part) & (lane < 32 * part + 32), moved, rest)
        pieces.append(jnp.where(lane < ROWS, own, 0.0))
    return jnp.concatenate(pieces + [rest], axis=0)


def granule_transpose(value):
    row = lax.broadcasted_iota(jnp.int32, value.shape, 0)
    group = lax.broadcasted_iota(jnp.int32, value.shape, 1) // NR
    height = value.shape[0]
    for bit in (1, 2, 4, 8):
        row_set = (row & bit) != 0
        group_set = (group & bit) != 0
        down = pltpu.roll(pltpu.roll(value, bit, 0), LANES - NR * bit, 1)
        up = pltpu.roll(pltpu.roll(value, height - bit, 0), NR * bit, 1)
        value = jnp.where(row_set == group_set, value, jnp.where(row_set, down, up))
    return value


def load_cells(flat_ref, pad_ref):
    cells = flat_ref.shape[0]
    width = NV * NR
    pad_ref[...] = jnp.zeros_like(pad_ref)
    for block in range(ROWS // 16):
        first = block * LANES
        wide = min(LANES, width - first)
        pad_ref[pl.ds(block * 16, cells), pl.ds(0, wide)] = flat_ref[:, pl.ds(first, wide)]
    turned = granule_transpose(pad_ref[pl.ds(0, ROWS), :])
    pad_ref[pl.ds(0, ROWS), :] = turned
    return jnp.transpose(pad_ref[...])


def store_cells(blocks, flat_ref):
    width = NV * NR
    cells = flat_ref.shape[0]
    turned = granule_transpose(jnp.transpose(blocks)[:ROWS])
    for block in range(ROWS // 16):
        first = block * LANES
        wide = min(LANES, width - first)
        flat_ref[:, pl.ds(first, wide)] = turned[block * 16 : block * 16 + cells, :wide]


def mixed_near_first(n):
    early = {4: 1.5, 8: 4.5, 12: 8.5}
    return sorted(range(1, n), key=lambda step: early.get(step, step))


def far_first(n):
    return sorted(range(1, n), key=lambda step: -sum(min(d, 4 - d) for d in (step % 4, step // 4 % 4)))


def low_bit(m):
    return m & -m


def node(level_size, cells, first):
    return 2 * cells - 2 * cells // level_size + first // level_size


def kernel(
    n,
    lines,
    pivot_hbm,
    upper_hbm,
    lower_hbm,
    rhs_hbm,
    face_ref,
    coef_hbm,
    first_ref,
    second_ref,
    flat,
    rhs_ref,
    coef_ref,
    slab,
    pad,
    pivot,
    tn,
    tb,
    qw,
    ew,
    kw,
    jw,
    jp,
    hw,
    hsum,
    rho,
    maps,
    came,
    answers,
    answered,
    phi,
    src,
    zs,
    xs,
    halo,
    fsend,
    gsend,
    fcame,
    gcame,
    load_sem,
    map_out,
    map_in,
    answer_out,
    answer_in,
    f_out,
    f_in,
    g_out,
    g_in,
    halo_out,
    halo_in,
):
    cells = rhs_ref.shape[0]
    me = lax.axis_index("narrow")
    line = lax.axis_index("wide")
    low_line = lax.rem(line + lines - 1, lines)
    high_line = lax.rem(line + 1, lines)

    loads = [
        pltpu.make_async_copy(hbm, flat.at[number], load_sem.at[number])
        for number, hbm in enumerate((pivot_hbm, upper_hbm, lower_hbm))
    ]
    loads.append(pltpu.make_async_copy(rhs_hbm, rhs_ref, load_sem.at[3]))
    loads.append(pltpu.make_async_copy(coef_hbm, coef_ref, load_sem.at[4]))
    for load in loads:
        load.start()

    fcame[...] = jnp.zeros_like(fcame)
    gcame[...] = jnp.zeros_like(gcame)
    answered[...] = jnp.zeros_like(answered)

    barrier = pltpu.get_barrier_semaphore()

    def greet(step, _):
        pl.semaphore_signal(
            barrier, inc=1, device_id={"narrow": lax.rem(me + step, n)}, device_id_type=MESH
        )
        return 0

    lax.fori_loop(1, n, greet, 0)
    for other in (low_line, high_line):
        pl.semaphore_signal(barrier, inc=1, device_id={"wide": other}, device_id_type=MESH)

    slab[...] = jnp.zeros_like(slab)
    tail = jnp.zeros((LANES - ROWS, 2 * LANES), BF16)

    def clear_nodes(i, _):
        for ref in (tn, tb):
            ref[i, pl.ds(ROWS, LANES - ROWS), :] = tail
        return 0

    lax.fori_loop(0, 2 * cells - 1, clear_nodes, 0)

    def clear(i, _):
        for ref in (qw, ew, kw, jw, jp):
            ref[i, pl.ds(ROWS, LANES - ROWS), :] = tail
        return 0

    lax.fori_loop(0, cells, clear, 0)
    hw[0, pl.ds(ROWS, LANES - ROWS), :] = tail
    for i in range(3):
        rho[i, pl.ds(ROWS, LANES - ROWS), :] = tail

    def clear_phi(i, _):
        phi[i] = jnp.zeros((LANES, 2 * LANES), BF16)
        return 0

    lax.fori_loop(0, n, clear_phi, 0)

    for number in range(3):
        loads[number].wait()
        for row in range(NV):
            slab[number, pl.ds(row * (cells + 1), cells), pl.ds(0, NV)] = flat[
                number, :, pl.ds(row * NV, NV)
            ].astype(F32)

    no_rows = jnp.zeros((LANES - ROWS, LANES), BF16)

    for i in range(cells):
        p, u, l = (
            slab[number, pl.ds(i, ROWS, stride=cells + 1), :] for number in range(3)
        )
        p16 = p.astype(BF16)
        pivot[i] = jnp.concatenate([p16, no_rows], axis=0)
        right = jnp.concatenate([(-u).astype(BF16), (-l).astype(BF16)], axis=1)
        right = jnp.concatenate([right, tail], axis=0)
        both = dot(p16, right)
        put(tn, i, both[:, :LANES])
        put(tb, i, both[:, LANES:])

    last = cells - 2
    whole = cells + last
    for place in range(last):
        put(tn, cells + place, multiply(left_of((tn, 2 * place)), right_of((tn, 2 * place + 1))))
    forward = multiply(left_of((tn, 2 * last)), right_of((tn, 2 * last + 1)))
    maps[0] = packed(forward)

    pl.semaphore_wait(barrier, n - 1 + 2)

    def map_copy(which, slot, target):
        return pltpu.make_async_remote_copy(
            src_ref=maps.at[which],
            dst_ref=came.at[slot],
            send_sem=map_out.at[slot],
            recv_sem=map_in.at[slot],
            device_id={"narrow": target},
            device_id_type=MESH,
        )

    for step in mixed_near_first(n):

        @pl.when((me >= 1) & (me + step < n))
        def _():
            map_copy(0, step, me + step).start()

    for place in range(last):
        put(tb, cells + place, multiply(left_of((tb, 2 * place + 1)), right_of((tb, 2 * place))))
    backward = multiply(left_of((tb, 2 * last + 1)), right_of((tb, 2 * last)))
    maps[1] = packed(backward)
    for step in mixed_near_first(n):

        @pl.when((me <= n - 2) & (me - step >= 0))
        def _():
            map_copy(1, n - step, me - step).start()

    put(tn, whole, forward)
    put(tb, whole, backward)

    def offset_copy(source, target_ref, turn, slot, out, arrived, target):
        return pltpu.make_async_remote_copy(
            src_ref=source.at[turn],
            dst_ref=target_ref.at[turn, slot],
            send_sem=out.at[turn, slot],
            recv_sem=arrived.at[turn, slot],
            device_id={"narrow": target},
            device_id_type=MESH,
        )

    def f_copy(turn, slot, target):
        return offset_copy(fsend, fcame, turn, slot, f_out, f_in, target)

    def g_copy(turn, slot, target):
        return offset_copy(gsend, gcame, turn, slot, g_out, g_in, target)

    def send_f(turn):
        for step in far_first(n):

            @pl.when(me + step < n)
            def _():
                f_copy(turn, step, me + step).start()

    def send_g(turn):
        for step in far_first(n):

            @pl.when(me - step >= 0)
            def _():
                g_copy(turn, n - step, me - step).start()

    def wait_f(turn):
        for step in range(1, n):

            @pl.when(step <= me)
            def _():
                f_copy(turn, step, me).wait_recv()

    def wait_g(turn):
        for step in range(1, n):

            @pl.when(me + step < n)
            def _():
                g_copy(turn, n - step, me).wait_recv()

    def deep(vectors, weights):
        left = jnp.concatenate([stacked_vector(v) for v in vectors], axis=1)
        right = jnp.concatenate([ref[index] for ref, index in weights], axis=0)
        return folded(dot(left, right))

    def by(vector, place):
        ref, index = place
        return folded(dot(stacked_vector(vector), ref[index]))

    def forward_node(size, first):
        return tn, node(size, cells, first)

    def backward_node(size, first):
        return tb, node(size, cells, cells - first - size)

    def climb(source, at, whole):
        sums, source = {}, list(source)
        for p in range(0, cells, 2):
            source[p + 1] = source[p + 1] + by(source[p], at(1, p))
        for p in range(0, cells, 2):
            sums[2, p] = by(source[p + 1], at(1, p + 1))
        size = 2
        while size < cells // 2 or (whole and size < cells):
            for p in range(0, cells, 2 * size):
                sums[2 * size, p] = sums[size, p + size] + by(sums[size, p], at(size, p + size))
            size *= 2
        return source, sums

    def descend(source, sums, at):
        entering = {0: None}
        size = cells // 2
        while size >= 2:
            for p in range(0, cells, 2 * size):
                after = sums[size, p]
                if entering[p] is not None:
                    after = after + by(entering[p], at(size, p))
                entering[p + size] = after
            size //= 2
        values = list(source)
        for p in range(0, cells, 2):
            if entering[p] is not None:
                values[p] = values[p] + entering[p]
                values[p + 1] = values[p + 1] + by(entering[p], at(1, p))
        return values

    row = lax.broadcasted_iota(jnp.int32, (ROWS, LANES), 0)
    column = lax.broadcasted_iota(jnp.int32, (ROWS, LANES), 1)
    unit = jnp.where((row == column) & (row < NV), 1.0, 0.0).astype(F32)
    put(kw, 0, unit)
    put(jw, cells - 1, unit)
    ew[0] = tb[0]
    hsum[...] = jnp.zeros_like(hsum)
    came[0] = jnp.zeros_like(came[0])

    @pl.when(me >= 1)
    def _():
        put(phi, 1, unit)

    @pl.when(me <= n - 2)
    def _():
        put(phi, n - 1, unit)

    def keep_alone(source, sums):
        for i, value in enumerate(descend(source, sums, forward_node)):
            zs[i] = value

    loads[3].wait()
    blocks = load_cells(rhs_ref, pad)
    for i in range(cells):
        src[i] = blocks[i * NR : (i + 1) * NR]
    source, sums = climb([src[i] for i in range(cells)], forward_node, True)
    fsend[0] = sums[cells, 0]
    send_f(0)
    keep_alone(source, sums)

    from_before = jnp.maximum(me - 1, 0)
    from_after = jnp.maximum(n - 2 - me, 0)

    def with_pivot(i):
        exact = pivot[i]
        put(jp, i, dot(left_of((jw, i)), jnp.concatenate([exact, exact], axis=0)))

    def extended(slot):
        high, low = parts(unpacked(came[slot]))
        return multiply(jnp.concatenate([high, low], axis=1), right_of((phi, slot)))

    def tables(step, _):
        arrived = step <= from_before
        slot = jnp.where(arrived, step, 0)
        towards = jnp.where(arrived, step + 1, n)

        @pl.when(arrived)
        def _():
            map_copy(0, slot, me).wait_recv()

        chained = extended(slot)
        back = cells - 1 - step
        k = multiply(left_of((kw, step - 1)), right_of((tn, step - 1)))
        e = multiply(left_of((tb, step)), right_of((ew, step - 1)))
        j = multiply(left_of((jw, back + 1)), right_of((tb, back + 1)))
        h = multiply(left_of((kw, step - 1)), right_of((ew, step - 1)))
        with_pivot(back + 1)
        put(phi, towards, chained)
        put(kw, step, k)
        put(ew, step, e)
        put(jw, back, j)
        hsum[...] += h
        return 0

    lax.fori_loop(1, cells, tables, 0)
    with_pivot(0)
    put(hw, 0, hsum[...] + multiply(left_of((kw, cells - 1)), right_of((ew, cells - 1))))

    between = [(phi, k) for k in range(n)]

    def answer_copy(slot, target):
        return pltpu.make_async_remote_copy(
            src_ref=answers.at[slot],
            dst_ref=answered.at[slot],
            send_sem=answer_out.at[slot],
            recv_sem=answer_in.at[slot],
            device_id={"narrow": target},
            device_id_type=MESH,
        )

    def send_answers():
        high_low = jnp.concatenate([left_of((phi, k)) for k in range(1, n)], axis=0)
        products = multiply(high_low, right_of((hw, 0)))
        for k in range(1, n):
            answers[n - k] = packed(products[(k - 1) * ROWS : k * ROWS])

        def send(step, _):
            answer_copy(n - step, me - step).start()
            return 0

        lax.fori_loop(1, me + 1, send, 0)

    def take_answers():
        def wait(step, _):
            answer_copy(n - step, me).wait_recv()
            return 0

        lax.fori_loop(1, n - me, wait, 0)
        left = []
        for k in range(1, n):
            high, low = parts(unpacked(answered[k]))
            left += [high, low]
        put(
            rho,
            0,
            multiply(
                jnp.concatenate(left, axis=1),
                jnp.concatenate([right_of((phi, k)) for k in range(1, n)], axis=0),
            ),
        )
        put(rho, 1, multiply(left_of((rho, 0)), right_of((tb, whole))))
        put(rho, 2, multiply(left_of((tn, whole)), right_of((rho, 0))))

    def inside(turn, left):
        z = [zs[i] + folded(dot(left, kw[i])) for i in range(cells)]
        source, sums = climb(z[::-1], backward_node, False)
        for p, u in enumerate(descend(source, sums, backward_node)):
            i = cells - 1 - p
            product = dot(stacked_vector(u), pivot[i])
            xs[turn, i] = product[:NR] + product[NR:]

    def complete(turn, entering):
        left = stacked_vector(entering)
        for i in range(cells):
            xs[turn, i] = xs[turn, i] + folded(dot(left, jp[i]))

    def backward_alone():
        return deep([zs[i] for i in range(cells)], [(ew, i) for i in range(cells)])

    alone = backward_alone()
    wait_f(0)
    left = stacked_vector(deep([fcame[0, k] for k in range(n)], between))
    gsend[0] = alone + folded(dot(left, hw[0]))
    send_g(0)
    send_answers()
    inside(0, left)

    def chain_back(step, _):
        slot = n - step
        map_copy(1, slot, me).wait_recv()
        put(phi, slot - 1, extended(slot))
        return 0

    lax.fori_loop(1, from_after + 1, chain_back, 0)
    wait_g(0)
    complete(0, deep([gcame[0, k] for k in range(n)], between))

    def halo_copy(side, other):
        return pltpu.make_async_remote_copy(
            src_ref=xs.at[0],
            dst_ref=halo.at[side],
            send_sem=halo_out.at[side],
            recv_sem=halo_in.at[side],
            device_id={"wide": other},
            device_id_type=MESH,
        )

    halo_copy(0, high_line).start()
    halo_copy(1, low_line).start()

    loads[4].wait()
    weights = []
    for place in range(3):
        total = jnp.zeros((cells, NV), F32)
        for side in range(2):
            relative = lax.rem(face_ref[0, side] - line + 1 + lines, lines)
            total = total + jnp.where(
                relative == place, coef_ref[:, pl.ds(side * NV, NV)], 0.0
            )
        weights.append(jnp.concatenate([total, jnp.zeros((cells, LANES - NV), F32)], axis=1))

    def last_n(m):
        return (tn, node(m, cells, cells - m)) if low_bit(m) == m else (qw, m)

    for m in range(1, cells):
        size = low_bit(m)
        if size != m:
            first = node(size, cells, cells - m)
            put(qw, m, multiply(left_of((tn, first)), right_of(last_n(m - size))))

    take_answers()

    halo_copy(0, high_line).wait_recv()
    halo_copy(1, low_line).wait_recv()

    for i in range(cells):
        coupled = (
            weights[0][i : i + 1] * halo[0, i]
            + weights[1][i : i + 1] * xs[0, i]
            + weights[2][i : i + 1] * halo[1, i]
        )
        src[i] = src[i] - coupled

    leaving = deep([src[i] for i in range(cells)], [last_n(cells - i) for i in range(cells)])
    fsend[1] = leaving
    send_f(1)

    keep_alone(*climb([src[i] for i in range(cells)], forward_node, False))
    gsend[1] = backward_alone() + by(leaving, (rho, 1))
    send_g(1)
    store_cells(xs[0].reshape(cells * NR, LANES), first_ref)
    wait_f(1)
    left = stacked_vector(deep([fcame[1, k] for k in range(n)], between))
    inside(1, left)
    back = by(leaving, (rho, 0)) + folded(dot(left, rho[2]))
    halo_copy(0, high_line).wait_send()
    halo_copy(1, low_line).wait_send()

    def drain(step, _):
        @pl.when(me + step < n)
        def _():
            f_copy(0, step, me + step).wait_send()
            f_copy(1, step, me + step).wait_send()

        @pl.when((me >= 1) & (me + step < n))
        def _():
            map_copy(0, step, me + step).wait_send()

        @pl.when((me <= n - 2) & (me - step >= 0))
        def _():
            map_copy(1, n - step, me - step).wait_send()

        @pl.when(me - step >= 0)
        def _():
            g_copy(0, n - step, me - step).wait_send()
            g_copy(1, n - step, me - step).wait_send()
            answer_copy(n - step, me - step).wait_send()

        return 0

    lax.fori_loop(1, n, drain, 0)
    wait_g(1)
    complete(1, back + deep([gcame[1, k] for k in range(n)], between))
    store_cells(xs[1].reshape(cells * NR, LANES), second_ref)


def body(n, lines, rhs, pivot, upper, lower, neighbors, coupling):
    cells = rhs.shape[1]
    matrix = (LANES, 2 * LANES)
    tree = pltpu.VMEM((2 * cells - 1, *matrix), BF16)
    weight = pltpu.VMEM((cells, *matrix), BF16)
    vectors = pltpu.VMEM((cells, NR, LANES), F32)
    vmem = pl.BlockSpec(memory_space=pltpu.VMEM)
    hbm = pl.BlockSpec(memory_space=pltpu.HBM)
    dma = pltpu.SemaphoreType.DMA

    def in_hbm(x):
        return pltpu.with_memory_space_constraint(x, pltpu.HBM)

    first, second = pl.pallas_call(
        functools.partial(kernel, n, lines),
        out_shape=[pltpu.VMEM((cells, NV * NR), F32)] * 2,
        in_specs=[hbm] * 4 + [pl.BlockSpec(memory_space=pltpu.SMEM), hbm],
        out_specs=[vmem] * 2,
        scratch_shapes=[
            pltpu.VMEM((3, cells, NV * NV), BF16),
            pltpu.VMEM((cells, NV * NR), F32),
            pltpu.VMEM((cells, 2 * NV), F32),
            pltpu.VMEM((3, ROWS * (cells + 1), LANES), F32),
            pltpu.VMEM((LANES, LANES), F32),
            pltpu.VMEM((cells, LANES, LANES), BF16),
            tree,
            tree,
            weight,
            weight,
            weight,
            weight,
            weight,
            pltpu.VMEM((1, *matrix), BF16),
            pltpu.VMEM((ROWS, LANES), F32),
            pltpu.VMEM((3, *matrix), BF16),
            pltpu.VMEM((2, PACKED, LANES), F32),
            pltpu.VMEM((n, PACKED, LANES), F32),
            pltpu.VMEM((n, PACKED, LANES), F32),
            pltpu.VMEM((n, PACKED, LANES), F32),
            pltpu.VMEM((n + 1, *matrix), BF16),
            vectors,
            vectors,
            pltpu.VMEM((2, cells, NR, LANES), F32),
            pltpu.VMEM((2, cells, NR, LANES), F32),
            pltpu.VMEM((2, NR, LANES), F32),
            pltpu.VMEM((2, NR, LANES), F32),
            pltpu.VMEM((2, n, NR, LANES), F32),
            pltpu.VMEM((2, n, NR, LANES), F32),
            dma((5,)),
            dma((n,)),
            dma((n,)),
            dma((n,)),
            dma((n,)),
            dma((2, n)),
            dma((2, n)),
            dma((2, n)),
            dma((2, n)),
            dma((2,)),
            dma((2,)),
        ],
        compiler_params=pltpu.CompilerParams(
            collective_id=0, has_side_effects=True, vmem_limit_bytes=40 * 1024 * 1024
        ),
    )(*(in_hbm(x) for x in (pivot[0], upper[0], lower[0], rhs[0], neighbors, coupling[0])))
    return first[None], second[None]


def solution(mesh):
    blocks = P("wide", "narrow", None)
    return jax.shard_map(
        functools.partial(body, mesh.shape["narrow"], mesh.shape["wide"]),
        mesh=mesh,
        in_specs=(blocks, blocks, blocks, blocks, P("wide", None), blocks),
        out_specs=(blocks, blocks),
        check_vma=False,
    )
```
